32 devices in a mesh: seq: 8 (over z, x), chan: 4 (over y, core).
Axes of the slice: x: 2, y: 2, z: 4, core: 2. Of those that a mesh axis runs over, the one named last changes fastest.
Arguments:
- residual_in: bfloat16 [8, 1024, 2048], P(None, 'seq', 'chan'), may hold values from -6 to 6
- norm_gain: bfloat16 [2048], replicated, may hold values from 0.5 to 1.5
- in_weight: bfloat16 [2048, 2, 4096], P(None, None, 'chan'), may hold values from -0.125 to 0.125
- conv_weight: bfloat16 [4, 4096], P(None, 'chan'), may hold values from -3 to 3
- conv_bias: bfloat16 [4096], P('chan'), may hold values from -3 to 3
- proj_weight: bfloat16 [160, 4096], P(None, 'chan')
- step_weight: bfloat16 [128, 4096], P(None, 'chan'), may hold values from -0.25 to 0.25
- step_bias: bfloat16 [4096], P('chan')
- decay_log: float32 [16, 4096], P(None, 'chan'), may hold values from 0 to 2.77
- skip_gain: float32 [4096], P('chan'), may hold values from 0.5 to 1.5
- out_weight: bfloat16 [2048, 4096], P(None, 'chan'), may hold values from -0.09375 to 0.09375
- out_grad: bfloat16 [8, 1024, 2048], P(None, 'seq', 'chan'), may hold values from -6 to 6
Outputs:
- block_out: bfloat16 [8, 1024, 2048], P(None, 'seq', 'chan')
- in_grad: bfloat16 [8, 1024, 2048], P(None, 'seq', 'chan')
- gain_grad: float32 [2048], P('chan')
- in_weight_grad: float32 [2048, 2, 4096], P('seq', None, 'chan')
- conv_weight_grad: float32 [4, 4096], P(None, 'chan')
- conv_bias_grad: float32 [4096], P('chan')
- proj_weight_grad: float32 [160, 4096], P('seq', 'chan')
- step_weight_grad: float32 [128, 4096], P('seq', 'chan')
- step_bias_grad: float32 [4096], P('chan')
- decay_log_grad: float32 [16, 4096], P(None, 'chan')
- skip_gain_grad: float32 [4096], P('chan')
- out_weight_grad: float32 [2048, 4096], P('seq', 'chan')
The draws below stay inside these ranges and needn't reach their ends.
All inputs are finite; a program needn't handle non-finite values.
Results may differ from the reference program's by a relative error of at most 0.011.
Values may be sent and summed in bfloat16 or wider, within the bound.
No kernel may reach another device: no remote copies, remote signals or barrier semaphores. Data moves between devices by JAX's collectives and lax.ppermute only.
A program may use at most 320 MiB of HBM per device.

```python
import math
import jax
import jax.numpy as jnp
from jax import lax

D = 2048
INNER = 4096
STATE = 16
RANK = 128
CONV = 4
TOK_DEV = 128
SEQS = 8
LENGTH = 1024


def draw_proj_weight(key, part):
    key = jax.random.fold_in(key, 11)
    normal_draw = jnp.clip(jax.random.normal(key, (RANK + 2 * STATE, INNER), jnp.float32), -6.0, 6.0)
    row_index = jnp.arange(RANK + 2 * STATE)[:, None]
    row_scale = jnp.where(row_index < RANK, 1.0, 6.0) / math.sqrt(INNER)
    return (normal_draw * row_scale).astype(jnp.bfloat16)


def draw_step_bias(key, part):
    key = jax.random.fold_in(key, 23)
    low_end = math.log(0.25 / LENGTH)
    high_end = math.log(16.0 / LENGTH)
    level = jax.random.uniform(key, (INNER,), jnp.float32, low_end, high_end)
    return jnp.log(jnp.expm1(jnp.exp(level))).astype(jnp.bfloat16)


def block_scale(key, shape, split, least, high):
    def one(axis_at, shards_of):
        draws = jax.random.uniform(jax.random.fold_in(jax.random.fold_in(key, 6), axis_at), (shards_of,), jnp.float32, least / len(split), high / len(split))
        return jnp.repeat(jnp.exp(draws), shape[axis_at] // shards_of).reshape((-1,) + (1,) * (len(shape) - axis_at - 1))

    factor_of = one(*split[0])
    for cut in split[1:]:
        factor_of = factor_of * one(*cut)
    return factor_of


def centred(stream_key, shape, deviation, reach, split=(), held_as=jnp.bfloat16):
    loudness = block_scale(stream_key, shape, split, -0.22, 0.18) if split else 1.0
    array = jax.random.normal(stream_key, shape, jnp.float32) * deviation * loudness
    return jnp.minimum(jnp.maximum(array, -reach), reach).astype(held_as)


def setup_inputs(seed: int = 0) -> dict:
    splits = jax.random.split(jax.random.key(seed), 13)
    return {
        "residual_in": centred(splits[0], (SEQS, LENGTH, D), 1.0, 6.0, ((1, 8), (2, 4))),
        "norm_gain": jnp.clip(1.0 + 0.1 * jax.random.normal(splits[1], (D,), jnp.float32), 0.5, 1.5).astype(jnp.bfloat16),
        "in_weight": centred(splits[2], (D, 2, INNER), D ** -0.5, 0.125, ((2, 4),)),
        "conv_weight": centred(splits[3], (CONV, INNER), CONV ** -0.5, 3.0, ((1, 4),)),
        "conv_bias": centred(splits[4], (INNER,), 0.5, 3.0, ((0, 4),)),
        "proj_weight": draw_proj_weight(jax.random.fold_in(splits[12], 71), 0),
        "step_weight": centred(splits[6], (RANK, INNER), (4 * RANK) ** -0.5, 0.25, ((1, 4),)),
        "step_bias": draw_step_bias(jax.random.fold_in(splits[12], 71), 0),
        "decay_log": jnp.clip(2.77 * jax.random.uniform(splits[8], (STATE, INNER), jnp.float32) ** block_scale(splits[8], (STATE, INNER), ((1, 4),), -0.2, 0.2), 0.0, 2.77),
        "skip_gain": jnp.clip(0.5 + 1.0 * jax.random.uniform(splits[9], (INNER,), jnp.float32) ** block_scale(splits[9], (INNER,), ((0, 4),), -0.2, 0.2), 0.5, 1.5),
        "out_weight": centred(splits[10], (D, INNER), INNER ** -0.5, 0.09375, ((1, 4),)),
        "out_grad": centred(splits[11], (SEQS, LENGTH, D), 1.0, 6.0, ((1, 8), (2, 4))),
    }


EPSILON = 1e-05
HIGHEST = lax.Precision.HIGHEST

@jax.custom_vjp
def low(v):
    return lax.optimization_barrier(v.astype(jnp.bfloat16)).astype(jnp.float32)

@jax.custom_vjp
def low_back(v):
    return v

def low_keep(v):
    return (low(v), None)

def low_pass(kept, grad):
    return (grad,)

def back_keep(v):
    return (v, None)

def back_low(kept, grad):
    return (low(grad),)
low.defvjp(low_keep, low_pass)
low_back.defvjp(back_keep, back_low)

def token_scan(step_size, mixed_in, b_rows, c_rows, decay_rate):
    blocks = step_size.shape[0] // TOK_DEV

    def blocked(value):
        return value.reshape(blocks, TOK_DEV, value.shape[1])

    @jax.checkpoint
    def block_step(state, block):

        def token_step(carried, token):
            step_tok, mixed_tok, b_tok, c_tok = token
            carried = jnp.exp(step_tok[None, :] * decay_rate) * carried + b_tok[:, None] * (step_tok * mixed_tok)[None, :]
            return (carried, lax.optimization_barrier(jnp.sum(c_tok[:, None] * carried, axis=0)))
        return lax.scan(token_step, state, block)
    start_state = jnp.zeros(decay_rate.shape, jnp.float32)
    _, outputs = lax.scan(block_step, start_state, (blocked(step_size), blocked(mixed_in), blocked(b_rows), blocked(c_rows)))
    return outputs.reshape(step_size.shape)

def mamba_block(residual, norm_gain, in_weight, conv_weight, conv_bias, proj_weight, step_weight, step_bias, decay_log, skip_gain, out_weight):
    inv_rms = lax.rsqrt(lax.optimization_barrier(jnp.mean(residual * residual, axis=-1, keepdims=True)) + EPSILON)
    normed = low(residual * inv_rms * norm_gain)
    projected_in = jnp.dot(normed, in_weight.reshape(D, 2 * INNER), precision=HIGHEST)
    conv_in = low_back(low(projected_in[:, :INNER]))
    gate_pre = low_back(projected_in[:, INNER:])
    padded = jnp.concatenate([jnp.zeros((CONV - 1, INNER), jnp.float32), conv_in], axis=0)
    seq_length = residual.shape[0]
    conv_out = conv_bias + sum((conv_weight[offset] * padded[offset:offset + seq_length] for offset in range(CONV)))
    mixed_in = low(jax.nn.silu(conv_out))
    projected = low_back(jnp.dot(mixed_in, proj_weight.T, precision=HIGHEST))
    step_low = low(projected[:, :RANK])
    b_rows = projected[:, RANK:RANK + STATE]
    c_rows = projected[:, RANK + STATE:]
    step_size = jax.nn.softplus(low_back(jnp.dot(step_low, step_weight, precision=HIGHEST) + step_bias))
    decay_rate = -jnp.exp(decay_log)
    scan_out = token_scan(step_size, mixed_in, b_rows, c_rows, decay_rate) + skip_gain * mixed_in
    gated_out = low(scan_out * jax.nn.silu(gate_pre))
    return residual + jnp.dot(gated_out, out_weight.T, precision=HIGHEST)

def reference(residual_in, norm_gain, in_weight, conv_weight, conv_bias, proj_weight, step_weight, step_bias, decay_log, skip_gain, out_weight, out_grad):
    weights = tuple((weight.astype(jnp.float32) for weight in (norm_gain, in_weight, conv_weight, conv_bias, proj_weight, step_weight, step_bias, decay_log, skip_gain, out_weight)))
    zero_grads = tuple((jnp.zeros_like(weight) for weight in weights))

    def one_sequence(running, seq_pair):
        seq_in, seq_grad = seq_pair
        seq_out, pull_back = jax.vjp(mamba_block, seq_in, *weights)
        part_grads = pull_back(seq_grad)
        running = tuple((so_far + part for so_far, part in zip(running, part_grads[1:])))
        return (running, (seq_out, part_grads[0]))
    totals, (outputs, in_grads) = lax.scan(one_sequence, zero_grads, (residual_in.astype(jnp.float32), out_grad.astype(jnp.float32)))
    return (outputs.astype(jnp.bfloat16), in_grads.astype(jnp.bfloat16), totals[0], totals[1], totals[2], totals[3], totals[4], totals[5], totals[6], totals[7], totals[8], totals[9])
```

```python
import functools, math
import jax, jax.numpy as jnp
from jax import lax
from jax.sharding import PartitionSpec as P
from jax.experimental import pallas as pl
from jax.experimental.pallas import tpu as pltpu

LANES = 128
LOG2E = 1.4426950408889634
VM = 56 * 1024 * 1024


def spread(bc_ref, spread_ref, chunk, seqs, count):
    for tok in range(chunk):
        tile = bc_ref[pl.ds(tok * seqs, seqs), :]
        for col in range(count):
            spread_ref[tok, col] = jnp.broadcast_to(tile[:, col : col + 1], (seqs, LANES))


def pre_kernel(chunk, step_ref, mixed_ref, yg_ref, bc_ref, rate_ref, h_ref, q_ref, p_ref, spread_ref):
    states, seqs, width = rate_ref.shape

    @pl.when(pl.program_id(0) == 0)
    def _():
        h_ref[...] = jnp.zeros_like(h_ref)
        q_ref[...] = jnp.zeros_like(q_ref)
        p_ref[...] = jnp.ones_like(p_ref)

    spread(bc_ref, spread_ref, chunk, seqs, 2 * states)
    part = 8

    def tile_step(j, _):
        lanes = pl.ds(pl.multiple_of(j * LANES, LANES), LANES)
        for low in range(0, states, part):
            idx = range(low, low + part)
            h = [h_ref[n, :, lanes] for n in idx]
            q = [q_ref[n, :, lanes] for n in idx]
            p = [p_ref[n, :, lanes] for n in idx]
            for tok in range(chunk):
                rows = pl.ds(tok * seqs, seqs)
                if tok % 2 == 0:
                    pair = mixed_ref[pl.ds(tok * seqs, 2 * seqs), lanes].astype(jnp.float32)
                s = step_ref[rows, lanes]
                y = yg_ref[rows, lanes]
                x = s * pair[(tok % 2) * seqs : (tok % 2 + 1) * seqs]
                for i, n in enumerate(idx):
                    d = jnp.exp2(s * rate_ref[n, :, lanes])
                    h[i] = d * h[i] + spread_ref[tok, n] * x
                    p[i] = d * p[i]
                    q[i] = q[i] + p[i] * (spread_ref[tok, states + n] * y)
            for i, n in enumerate(idx):
                h_ref[n, :, lanes] = h[i]
                q_ref[n, :, lanes] = q[i]
                p_ref[n, :, lanes] = p[i]
        return 0

    lax.fori_loop(0, width // LANES, tile_step, 0)


def prepass(step, mixed, yg, bc, rate, chunk):
    rows, width = step.shape
    states, seqs, _ = rate.shape
    grid = rows // (chunk * seqs)
    row_spec = pl.BlockSpec((chunk * seqs, width), lambda i: (i, 0))
    whole = pl.BlockSpec((states, seqs, width), lambda i: (0, 0, 0))
    return pl.pallas_call(
        functools.partial(pre_kernel, chunk),
        grid=(grid,),
        in_specs=[row_spec, row_spec, row_spec, pl.BlockSpec((chunk * seqs, LANES), lambda i: (i, 0)), whole],
        out_specs=[whole, whole],
        out_shape=[jax.ShapeDtypeStruct(rate.shape, jnp.float32)] * 2,
        scratch_shapes=[pltpu.VMEM(rate.shape, jnp.float32), pltpu.VMEM((chunk, 2 * states, seqs, LANES), jnp.float32)],
        compiler_params=pltpu.CompilerParams(vmem_limit_bytes=VM),
        name="local_ends",
    )(step, mixed, yg, bc, rate)


def fwd_kernel(chunk, step_ref, mixed_ref, gate_ref, gg_ref, bc_ref, rate_ref, hin_ref, skip_ref,
               hist_ref, start_ref, gated_ref, ggrad_ref, state_ref, spread_ref):
    states, seqs, width = rate_ref.shape

    @pl.when(pl.program_id(0) == 0)
    def _():
        state_ref[...] = hin_ref[...]

    start_ref[0] = state_ref[...]
    spread(bc_ref, spread_ref, chunk, seqs, 2 * states)

    def tile_step(j, _):
        lanes = pl.ds(pl.multiple_of(j * LANES, LANES), LANES)
        h = [state_ref[n, :, lanes] for n in range(states)]
        skip = skip_ref[:, lanes]
        for tok in range(0, chunk, 2):
            pair_rows = pl.ds(tok * seqs, 2 * seqs)
            pair = mixed_ref[pair_rows, lanes].astype(jnp.float32)
            gated, ggrad = [], []
            for k in range(2):
                rows = pl.ds((tok + k) * seqs, seqs)
                s = step_ref[rows, lanes]
                m = pair[k * seqs : (k + 1) * seqs]
                x = s * m
                y = skip * m
                for n in range(states):
                    d = jnp.exp2(s * rate_ref[n, :, lanes])
                    h[n] = d * h[n] + spread_ref[tok + k, n] * x
                    y = y + spread_ref[tok + k, states + n] * h[n]
                for n in range(0, states, 2):
                    at = pl.ds(((tok + k) * states + n) * seqs, 2 * seqs)
                    hist_ref[at, lanes] = jnp.concatenate([h[n], h[n + 1]], axis=0).astype(jnp.bfloat16)
                v = gate_ref[rows, lanes]
                sig = 1.0 / (1.0 + jnp.exp2(v * (-LOG2E)))
                gated.append(y * (v * sig))
                ggrad.append(gg_ref[rows, lanes] * y * (sig * (1.0 + v * (1.0 - sig))))
            gated_ref[pair_rows, lanes] = jnp.concatenate(gated, axis=0).astype(jnp.bfloat16)
            ggrad_ref[pair_rows, lanes] = jnp.concatenate(ggrad, axis=0).astype(jnp.bfloat16)
        for n in range(states):
            state_ref[n, :, lanes] = h[n]
        return 0

    lax.fori_loop(0, width // LANES, tile_step, 0)


def forward(step, mixed, gate, gg, bc, rate, hin, skip, chunk):
    rows, width = step.shape
    states, seqs, _ = rate.shape
    grid = rows // (chunk * seqs)
    row_spec = pl.BlockSpec((chunk * seqs, width), lambda i: (i, 0))
    whole = pl.BlockSpec((states, seqs, width), lambda i: (0, 0, 0))
    return pl.pallas_call(
        functools.partial(fwd_kernel, chunk),
        grid=(grid,),
        in_specs=[row_spec, row_spec, row_spec, row_spec, pl.BlockSpec((chunk * seqs, LANES), lambda i: (i, 0)), whole, whole,
                  pl.BlockSpec((seqs, width), lambda i: (0, 0))],
        out_specs=[pl.BlockSpec((chunk * states * seqs, width), lambda i: (i, 0)),
                   pl.BlockSpec((1, states, seqs, width), lambda i: (i, 0, 0, 0)), row_spec, row_spec],
        out_shape=[jax.ShapeDtypeStruct((rows * states, width), jnp.bfloat16),
                   jax.ShapeDtypeStruct((grid, states, seqs, width), jnp.float32),
                   jax.ShapeDtypeStruct((rows, width), jnp.bfloat16),
                   jax.ShapeDtypeStruct((rows, width), jnp.bfloat16)],
        scratch_shapes=[pltpu.VMEM(rate.shape, jnp.float32), pltpu.VMEM((chunk, 2 * states, seqs, LANES), jnp.float32)],
        compiler_params=pltpu.CompilerParams(vmem_limit_bytes=VM),
        name="scan_forward",
    )(step, mixed, gate, gg, bc, rate, hin, skip)


def bwd_kernel(chunk, step_ref, sig_ref, mixed_ref, yg_ref, bc_ref, rate_ref, rate_e_ref, gin_ref, skip_ref, hist_ref, start_ref,
               pre_ref, part_ref, bcg_ref, decay_ref, bias_ref, skipg_ref, state_ref, spread_ref, g_ref, x_ref):
    states, seqs, width = rate_ref.shape

    @pl.when(pl.program_id(0) == 0)
    def _():
        state_ref[...] = gin_ref[...]
        decay_ref[...] = jnp.zeros_like(decay_ref)
        bias_ref[...] = jnp.zeros_like(bias_ref)
        skipg_ref[...] = jnp.zeros_like(skipg_ref)

    spread(bc_ref, spread_ref, chunk, seqs, 2 * states)

    def tile_step(j, _):
        lanes = pl.ds(pl.multiple_of(j * LANES, LANES), LANES)
        q = [state_ref[n, :, lanes] for n in range(states)]
        acc = [decay_ref[n, :, lanes] for n in range(states)]
        skip = skip_ref[:, lanes]
        bias = bias_ref[:, lanes]
        skipg = skipg_ref[:, lanes]
        for tok in range(chunk - 2, -1, -2):
            pair_rows = pl.ds(tok * seqs, 2 * seqs)
            pair = mixed_ref[pair_rows, lanes].astype(jnp.float32)
            pre, xs = [None, None], [None, None]
            for k in (1, 0):
                now = tok + k
                rows = pl.ds(now * seqs, seqs)
                s = step_ref[rows, lanes]
                y = yg_ref[rows, lanes]
                m = pair[k * seqs : (k + 1) * seqs]
                along = jnp.zeros_like(s)
                size = jnp.zeros_like(s)
                for n in range(0, states, 2):
                    if now > 0:
                        at = pl.ds(((now - 1) * states + n) * seqs, 2 * seqs)
                        both = hist_ref[at, lanes].astype(jnp.float32)
                        before = [both[:seqs], both[seqs:]]
                    else:
                        before = [start_ref[0, n, :, lanes], start_ref[0, n + 1, :, lanes]]
                    gs = []
                    for i in range(2):
                        r = rate_ref[n + i, :, lanes]
                        g = spread_ref[now, states + n + i] * y + q[n + i]
                        along = along + g * spread_ref[now, n + i]
                        q[n + i] = jnp.exp2(s * r) * g
                        w = q[n + i] * before[i]
                        acc[n + i] = acc[n + i] + w * s
                        size = size + w * r
                        gs.append(g)
                    at = pl.ds((now * states + n) * seqs, 2 * seqs)
                    g_ref[at, lanes] = jnp.concatenate(gs, axis=0).astype(jnp.bfloat16)
                part_ref[rows, lanes] = s * along + skip * y
                skipg = skipg + y * m
                xs[k] = s * m
                pre[k] = (size * (1.0 / LOG2E) + m * along) * sig_ref[rows, lanes]
            rounded = jnp.concatenate(pre, axis=0).astype(jnp.bfloat16)
            pre_ref[pair_rows, lanes] = rounded
            wide = rounded.astype(jnp.float32)
            bias = bias + wide[:seqs] + wide[seqs:]
            x_ref[pair_rows, lanes] = jnp.concatenate(xs, axis=0).astype(jnp.bfloat16)
        for n in range(states):
            state_ref[n, :, lanes] = q[n]
            decay_ref[n, :, lanes] = acc[n]
        bias_ref[:, lanes] = bias
        skipg_ref[:, lanes] = skipg
        return 0

    lax.fori_loop(0, width // LANES, tile_step, 0)
    span = 2 * states * seqs
    row = lax.broadcasted_iota(jnp.int32, (2 * seqs, span), 0)
    col = lax.broadcasted_iota(jnp.int32, (2 * seqs, span), 1)
    match = (row // seqs == col // (states * seqs)) & (row % seqs == col % seqs)
    contract = (((1,), (1,)), ((), ()))
    b_rows, c_rows = [], []
    for tok in range(0, chunk, 2):
        pair_rows = pl.ds(tok * seqs, 2 * seqs)
        at = pl.ds(tok * states * seqs, span)
        bg = lax.dot_general(x_ref[pair_rows, :], g_ref[at, :], contract, preferred_element_type=jnp.float32)
        cg = lax.dot_general(yg_ref[pair_rows, :].astype(jnp.bfloat16), hist_ref[at, :], contract, preferred_element_type=jnp.float32)
        b_rows.append(jnp.where(match, bg, 0.0))
        c_rows.append(jnp.where(match, cg, 0.0))
    src = lax.broadcasted_iota(jnp.int32, (2 * states, span), 1) // seqs % states
    dst = lax.broadcasted_iota(jnp.int32, (2 * states, span), 0)
    fold_b = (src == dst).astype(jnp.bfloat16)
    fold_c = (src + states == dst).astype(jnp.bfloat16)
    bcg_ref[...] = lax.dot_general(
        fold_b, jnp.concatenate(b_rows, axis=0).astype(jnp.bfloat16), contract, preferred_element_type=jnp.float32
    ) + lax.dot_general(
        fold_c, jnp.concatenate(c_rows, axis=0).astype(jnp.bfloat16), contract, preferred_element_type=jnp.float32
    )


def backward(step, sig, mixed, yg, bc, rate, gin, skip, hist, start, chunk):
    rows, width = step.shape
    states, seqs, _ = rate.shape
    grid = rows // (chunk * seqs)
    back = lambda i: (grid - 1 - i, 0)
    row_spec = pl.BlockSpec((chunk * seqs, width), back)
    bc_spec = pl.BlockSpec((chunk * seqs, LANES), back)
    whole = pl.BlockSpec((states, seqs, width), lambda i: (0, 0, 0))
    one = pl.BlockSpec((seqs, width), lambda i: (0, 0))
    f32 = jnp.float32
    return pl.pallas_call(
        functools.partial(bwd_kernel, chunk),
        grid=(grid,),
        in_specs=[row_spec, row_spec, row_spec, row_spec, bc_spec, whole, whole, whole, one,
                  pl.BlockSpec((chunk * states * seqs, width), back),
                  pl.BlockSpec((1, states, seqs, width), lambda i: (grid - 1 - i, 0, 0, 0))],
        out_specs=[row_spec, row_spec, pl.BlockSpec((2 * states, chunk * seqs), lambda i: (0, grid - 1 - i)), whole, one, one],
        out_shape=[jax.ShapeDtypeStruct((rows, width), jnp.bfloat16), jax.ShapeDtypeStruct((rows, width), f32),
                   jax.ShapeDtypeStruct((2 * states, rows), f32), jax.ShapeDtypeStruct(rate.shape, f32),
                   jax.ShapeDtypeStruct((seqs, width), f32), jax.ShapeDtypeStruct((seqs, width), f32)],
        scratch_shapes=[pltpu.VMEM(rate.shape, f32), pltpu.VMEM((chunk, 2 * states, seqs, LANES), f32),
                        pltpu.VMEM((chunk * states * seqs, width), jnp.bfloat16), pltpu.VMEM((chunk * seqs, width), jnp.bfloat16)],
        compiler_params=pltpu.CompilerParams(vmem_limit_bytes=VM),
        name="scan_backward",
    )(step, sig, mixed, yg, bc, rate, rate, gin, skip, hist, start)


EPSILON = 1e-05
CONTRACT_LAST = (((1,), (1,)), ((), ()))
CONTRACT_FIRST = (((0,), (0,)), ((), ()))


def dot(a, b, dims=(((1,), (0,)), ((), ())), out=jnp.float32):
    return lax.dot_general(a, b, dims, preferred_element_type=out)


def swapped(value, axis, bit):
    count = lax.axis_size(axis)
    return lax.ppermute(value, axis, [(i, i ^ (1 << bit)) for i in range(count)])


def moved(value, axis, distance):
    count = lax.axis_size(axis)
    return lax.ppermute(value, axis, [(i, i + distance) for i in range(count) if 0 <= i + distance < count])


def bits_of(axis):
    return lax.axis_size(axis).bit_length() - 1


def own_bit(axis, bit):
    return (lax.axis_index(axis) >> bit) & 1


def gathered(value, axis):
    count = lax.axis_size(axis)
    parts = {0: value}
    for bit in reversed(range(bits_of(axis))):
        parts |= {mask | (1 << bit): swapped(part, axis, bit) for mask, part in parts.items()}
    for bit in range(bits_of(axis)):
        high = own_bit(axis, bit) == 1
        low_of = lambda m: m & ~(1 << bit)
        parts = {m: jnp.where(high, parts[m ^ (1 << bit)], parts[m]) for m in range(count)}
    return jnp.concatenate([parts[m] for m in range(count)], axis=-1)


def summed(value, axis, narrow_from):
    for bit in range(bits_of(axis)):
        sent = value.astype(jnp.bfloat16) if bit >= narrow_from else value
        value = value + swapped(sent, axis, bit).astype(jnp.float32)
    return value


def pick(value, dim, index):
    return lax.dynamic_index_in_dim(value, index, dim, keepdims=False)


def scattered(blocks, axis):
    bits = bits_of(axis)
    value = blocks.reshape((2,) * bits + blocks.shape[1:])
    for bit in range(bits):
        dim = bits - 1 - bit
        mine = own_bit(axis, bit)
        received = swapped(pick(value, dim, 1 - mine), axis, bit)
        value = pick(value, dim, mine).astype(jnp.float32) + received.astype(jnp.float32)
        if bit < bits - 1:
            value = value.astype(jnp.bfloat16)
    return value


def entering(local, total, rate, axis, direction):
    states = rate.shape[0]
    enter, enter_sum = jnp.zeros_like(local), jnp.zeros_like(total)
    through, through_sum = local, total
    distance = 1
    while distance < lax.axis_size(axis):
        upper = through_sum.astype(jnp.bfloat16)
        lower = (through_sum - upper.astype(jnp.float32)).astype(jnp.bfloat16)
        packet = jnp.concatenate([through.astype(jnp.bfloat16), upper[None], lower[None]], axis=0)
        got = moved(packet, axis, distance * direction).astype(jnp.float32)
        state, step_sum = got[:states], got[states] + got[states + 1]
        enter, enter_sum = enter + jnp.exp2(rate * enter_sum) * state, enter_sum + step_sum
        through, through_sum = through + jnp.exp2(rate * through_sum) * state, through_sum + step_sum
        distance *= 2
    return enter


def silu_slope(pre_value):
    sigmoid_value = jax.nn.sigmoid(pre_value)
    return sigmoid_value * (1.0 + pre_value * (1.0 - sigmoid_value))


def shards(
    residual_in,
    norm_gain,
    in_weight,
    conv_weight,
    conv_bias,
    proj_weight,
    step_weight,
    step_bias,
    decay_log,
    skip_gain,
    out_weight,
    out_grad,
):
    f32, bf16 = jnp.float32, jnp.bfloat16
    seqs, toks, share = residual_in.shape
    model = norm_gain.shape[0]
    taps, inner = conv_weight.shape
    states = decay_log.shape[0]
    rank = step_weight.shape[0]
    rows = seqs * toks
    chunk = math.gcd(toks, 16)
    seq_count = lax.axis_size("seq")
    own_in = residual_in.swapaxes(0, 1).reshape(rows, share)
    own_out_grad = out_grad.swapaxes(0, 1).reshape(rows, share)
    full_in = gathered(own_in, "chan")
    grad_whole = gathered(own_out_grad, "chan")
    wide_in = full_in.astype(f32)
    inv_rms = lax.rsqrt(jnp.mean(wide_in * wide_in, axis=-1, keepdims=True) + EPSILON)
    gain_full = norm_gain.astype(f32)
    normed = (wide_in * inv_rms * gain_full).astype(bf16)
    conv_weights, gate_weights = in_weight[:, 0], in_weight[:, 1]
    conv_in = dot(normed, conv_weights, out=bf16)
    gate_pre = dot(normed, gate_weights)
    halo = (taps - 1) * seqs
    previous = moved(conv_in[rows - halo :], "seq", 1)
    padded = jnp.concatenate([previous, conv_in], axis=0).astype(f32)
    conv_taps = conv_weight.astype(f32)
    conv_out = conv_bias.astype(f32) + sum(
        conv_taps[k] * padded[k * seqs : k * seqs + rows] for k in range(taps)
    )
    mixed = jax.nn.silu(conv_out).astype(bf16)
    projected = summed(dot(proj_weight, mixed, CONTRACT_LAST), "chan", 1)
    step_low = projected[:rank].astype(bf16)
    bc = jnp.pad(projected[rank:].T, ((0, 0), (0, LANES - 2 * states)))
    step_pre = dot(step_low, step_weight, CONTRACT_FIRST) + step_bias.astype(f32)
    step = jax.nn.softplus(step_pre)
    step_slope = jax.nn.sigmoid(step_pre)
    decay_rate = -jnp.exp(decay_log)
    rate = jnp.broadcast_to((decay_rate * LOG2E)[:, None], (states, seqs, inner))
    skip = jnp.broadcast_to(skip_gain, (seqs, inner))
    gated_grad = dot(grad_whole, out_weight)
    y_grad = gated_grad * jax.nn.silu(gate_pre)
    local_end, local_start = prepass(step, mixed, y_grad, bc, rate, chunk)
    step_total = jnp.sum(step.reshape(toks, seqs, inner), axis=0)
    enter_h = entering(local_end, step_total, rate, "seq", 1)
    enter_g = entering(local_start, step_total, rate, "seq", -1)
    history, starts, gated_out, gate_grad = forward(
        step, mixed, gate_pre, gated_grad, bc, rate, enter_h, skip, chunk
    )
    branch = dot(gated_out, out_weight, CONTRACT_LAST, out=bf16)
    chan_bits = bits_of("chan")
    by_owner = lambda value: value.reshape(rows, -1, share).swapaxes(0, 1)
    branch_share = scattered(by_owner(branch), "chan")
    block_rows = (own_in.astype(f32) + branch_share).astype(bf16)
    block_out = block_rows.reshape(toks, seqs, share).swapaxes(0, 1)
    out_weight_part = dot(grad_whole, gated_out, CONTRACT_FIRST, out=bf16)
    out_weight_grad = scattered(out_weight_part.reshape(seq_count, -1, inner), "seq")
    gate_weight_part = dot(normed, gate_grad, CONTRACT_FIRST, out=bf16)
    gate_weight_grad = scattered(gate_weight_part.reshape(seq_count, -1, inner), "seq")
    pre_grad, mixed_part, bc_grads, decay_parts, bias_parts, skip_parts = backward(
        step, step_slope, mixed, y_grad, bc, rate, enter_g, skip, history, starts, chunk
    )
    low_grad = dot(step_weight, pre_grad, CONTRACT_LAST)
    proj_grad = summed(jnp.concatenate([low_grad, bc_grads], axis=0), "chan", 1).astype(bf16)
    proj_weight_part = dot(proj_grad, mixed, out=bf16)
    step_weight_part = dot(step_low, pre_grad, out=bf16)
    mixed_grad = mixed_part + dot(proj_grad, proj_weight, CONTRACT_FIRST)
    conv_grad = mixed_grad * silu_slope(conv_out)
    conv_bias_grad = jnp.sum(conv_grad, axis=0)
    conv_weight_grad = jnp.stack(
        [jnp.sum(conv_grad * padded[k * seqs : k * seqs + rows], axis=0) for k in range(taps)]
    )
    incoming = moved(conv_grad[:halo], "seq", -1)
    extended = jnp.concatenate([conv_grad, incoming], axis=0)
    conv_in_grad = sum(
        conv_taps[k] * extended[(taps - 1 - k) * seqs : (taps - 1 - k) * seqs + rows] for k in range(taps)
    ).astype(bf16)
    conv_weights_part = dot(normed, conv_in_grad, CONTRACT_FIRST, out=bf16)
    conv_weights_grad = scattered(conv_weights_part.reshape(seq_count, -1, inner), "seq")
    small_weights = scattered(
        jnp.concatenate(
            [proj_weight_part.reshape(seq_count, -1, inner), step_weight_part.reshape(seq_count, -1, inner)], axis=1
        ),
        "seq",
    )
    proj_share = proj_weight.shape[0] // seq_count
    normed_part = (dot(conv_in_grad, conv_weights, CONTRACT_LAST) + dot(gate_grad, gate_weights, CONTRACT_LAST)).astype(bf16)
    normed_grad = scattered(by_owner(normed_part), "chan")
    row_dots = jnp.sum(
        conv_in_grad.astype(f32) * conv_in.astype(f32) + gate_grad.astype(f32) * gate_pre, axis=1
    )
    row_dots = summed(row_dots, "chan", chan_bits)[:, None]
    wide_own = own_in.astype(f32)
    own_gain = lax.dynamic_slice_in_dim(gain_full, lax.axis_index("chan") * share, share, 0)
    in_rows = (
        own_out_grad.astype(f32)
        + inv_rms * own_gain * normed_grad
        - wide_own * (inv_rms * inv_rms / model) * row_dots
    ).astype(bf16)
    in_grad = in_rows.reshape(toks, seqs, share).swapaxes(0, 1)
    gain_grad = summed(jnp.sum(normed_grad * wide_own * inv_rms, axis=0), "seq", bits_of("seq"))
    sums = summed(
        jnp.concatenate(
            [
                jnp.sum(decay_parts, axis=1) * decay_rate,
                conv_weight_grad,
                conv_bias_grad[None],
                jnp.sum(bias_parts, axis=0)[None],
                jnp.sum(skip_parts, axis=0)[None],
            ],
            axis=0,
        ),
        "seq",
        bits_of("seq"),
    )
    return (
        block_out,
        in_grad,
        gain_grad,
        jnp.stack([conv_weights_grad, gate_weight_grad], axis=1),
        sums[states : states + taps],
        sums[states + taps],
        small_weights[:proj_share],
        small_weights[proj_share:],
        sums[states + taps + 1],
        sums[:states],
        sums[states + taps + 2],
        out_weight_grad,
    )


def solution(mesh):
    in_specs = (
        P(None, "seq", "chan"),
        P(),
        P(None, None, "chan"),
        P(None, "chan"),
        P("chan"),
        P(None, "chan"),
        P(None, "chan"),
        P("chan"),
        P(None, "chan"),
        P("chan"),
        P(None, "chan"),
        P(None, "seq", "chan"),
    )
    out_specs = (
        P(None, "seq", "chan"),
        P(None, "seq", "chan"),
        P("chan"),
        P("seq", None, "chan"),
        P(None, "chan"),
        P("chan"),
        P("seq", "chan"),
        P("seq", "chan"),
        P("chan"),
        P(None, "chan"),
        P("chan"),
        P("seq", "chan"),
    )
    return jax.shard_map(shards, mesh=mesh, in_specs=in_specs, out_specs=out_specs, check_vma=False)
```

```python
import functools, math
import jax, jax.numpy as jnp
from jax import lax
from jax.sharding import PartitionSpec as P
from jax.experimental import pallas as pl
from jax.experimental.pallas import tpu as pltpu

LANES = 128
LOG2E = 1.4426950408889634
VM = 56 * 1024 * 1024
F32, BF16 = jnp.float32, jnp.bfloat16


def spread(rows_ref, select_ref, spread_ref, chunk, count, seqs):
    left, parts = rows_ref[...], []
    for _ in range(3):
        parts.append(left.astype(BF16))
        left = left - parts[-1].astype(F32)
    stacked = jnp.concatenate(parts, axis=0)
    for col in range(0, count, 2):
        wide = lax.dot_general(
            stacked, select_ref[:, col * LANES : (col + 2) * LANES], (((0,), (0,)), ((), ())), preferred_element_type=F32
        )
        for tok in range(chunk):
            for i in range(2):
                spread_ref[tok, col + i] = wide[tok * seqs : (tok + 1) * seqs, i * LANES : (i + 1) * LANES]


def ends_kernel(chunk, step_ref, mixed_ref, rows_ref, rate_ref, h_ref, spread_ref, select_ref):
    states, seqs, width = rate_ref.shape

    @pl.when(pl.program_id(0) == 0)
    def _():
        h_ref[...] = jnp.zeros_like(h_ref)
        row = lax.broadcasted_iota(jnp.int32, select_ref.shape, 0)
        col = lax.broadcasted_iota(jnp.int32, select_ref.shape, 1)
        select_ref[...] = (row % (2 * states) == col // LANES).astype(BF16)

    spread(rows_ref, select_ref, spread_ref, chunk, 2 * states, seqs)

    def tile_step(j, _):
        lanes = pl.ds(pl.multiple_of(j * LANES, LANES), LANES)
        h = [h_ref[n, :, lanes] for n in range(states)]
        for tok in range(0, chunk, 2):
            m = mixed_ref[pl.ds(tok * seqs, 2 * seqs), lanes].astype(F32)
            for k in range(2):
                s = step_ref[pl.ds((tok + k) * seqs, seqs), lanes]
                x = s * m[k * seqs : (k + 1) * seqs]
                for n in range(states):
                    h[n] = jnp.exp2(s * rate_ref[n, :, lanes]) * h[n] + spread_ref[tok + k, n] * x
        for n in range(states):
            h_ref[n, :, lanes] = h[n]
        return 0

    lax.fori_loop(0, width // LANES, tile_step, 0, unroll=2)


def starts_kernel(chunk, step_ref, yg_ref, spread_ref, rate_ref, q_ref):
    states, seqs, width = rate_ref.shape

    @pl.when(pl.program_id(0) == 0)
    def _():
        q_ref[...] = jnp.zeros_like(q_ref)

    def tile_step(j, _):
        lanes = pl.ds(pl.multiple_of(j * LANES, LANES), LANES)
        q = [q_ref[n, :, lanes] for n in range(states)]
        for tok in reversed(range(chunk)):
            rows = pl.ds(tok * seqs, seqs)
            s, y = step_ref[rows, lanes], yg_ref[rows, lanes]
            for n in range(states):
                q[n] = jnp.exp2(s * rate_ref[n, :, lanes]) * (q[n] + spread_ref[tok, states + n] * y)
        for n in range(states):
            q_ref[n, :, lanes] = q[n]
        return 0

    lax.fori_loop(0, width // LANES, tile_step, 0, unroll=2)


def spread_spec(chunk, states, seqs, at):
    return pl.BlockSpec((chunk, 2 * states, seqs, LANES), lambda i: (at(i), 0, 0, 0))


def local_ends(step, mixed, rows_t, rate, chunk):
    rows, width = step.shape
    states, seqs, _ = rate.shape
    elements = rows * width * states
    grid = rows // (chunk * seqs)
    row_spec = pl.BlockSpec((chunk * seqs, width), lambda i: (i, 0))
    whole = pl.BlockSpec((states, seqs, width), lambda i: (0, 0, 0))
    return pl.pallas_call(
        functools.partial(ends_kernel, chunk),
        grid=(grid,),
        in_specs=[row_spec, row_spec, pl.BlockSpec((2 * states, chunk * seqs), lambda i: (0, i)), whole],
        out_specs=[whole, spread_spec(chunk, states, seqs, lambda i: i)],
        out_shape=[jax.ShapeDtypeStruct(rate.shape, F32), jax.ShapeDtypeStruct((rows // seqs, 2 * states, seqs, LANES), F32)],
        scratch_shapes=[pltpu.VMEM((6 * states, 2 * states * LANES), BF16)],
        compiler_params=pltpu.CompilerParams(vmem_limit_bytes=VM),
        cost_estimate=pl.CostEstimate(flops=elements, bytes_accessed=elements, transcendentals=0),
        name="local_ends",
    )(step, mixed, rows_t, rate)


def local_starts(step, yg, wide_rows, rate, chunk):
    rows, width = step.shape
    states, seqs, _ = rate.shape
    elements = rows * width * states
    grid = rows // (chunk * seqs)
    at = lambda i: grid - 1 - i
    row_spec = pl.BlockSpec((chunk * seqs, width), lambda i: (at(i), 0))
    whole = pl.BlockSpec((states, seqs, width), lambda i: (0, 0, 0))
    return pl.pallas_call(
        functools.partial(starts_kernel, chunk),
        grid=(grid,),
        in_specs=[row_spec, row_spec, spread_spec(chunk, states, seqs, at), whole],
        out_specs=whole,
        out_shape=jax.ShapeDtypeStruct(rate.shape, F32),
        compiler_params=pltpu.CompilerParams(vmem_limit_bytes=VM),
        cost_estimate=pl.CostEstimate(flops=elements, bytes_accessed=elements, transcendentals=0),
        name="local_starts",
    )(step, yg, wide_rows, rate)


def fwd_kernel(chunk, step_ref, mixed_ref, gate_ref, gg_ref, spread_ref, rate_ref, skip_ref,
               hin_ref, *refs):
    state_ref, hist_ref, start_ref, gated_ref, ggrad_ref = refs[-5:]
    states, seqs, width = rate_ref.shape

    @pl.when(pl.program_id(0) == 0)
    def _():
        state_ref[...] = hin_ref[...]

    start_ref[0] = state_ref[...].astype(BF16)

    def tile_step(j, _):
        lanes = pl.ds(pl.multiple_of(j * LANES, LANES), LANES)
        h = [state_ref[n, :, lanes] for n in range(states)]
        skip = skip_ref[:, lanes]
        for tok in range(0, chunk, 2):
            pair_rows = pl.ds(tok * seqs, 2 * seqs)
            pair = mixed_ref[pair_rows, lanes].astype(F32)
            gated, ggrad = [], []
            for k in range(2):
                rows = pl.ds((tok + k) * seqs, seqs)
                s = step_ref[rows, lanes]
                m = pair[k * seqs : (k + 1) * seqs]
                x = s * m
                y = skip * m
                for n in range(states):
                    h[n] = jnp.exp2(s * rate_ref[n, :, lanes]) * h[n] + spread_ref[tok + k, n] * x
                    y = y + spread_ref[tok + k, states + n] * h[n]
                for n in range(0, states, 2):
                    hist_ref[tok + k, j, pl.ds(n * seqs, 2 * seqs), :] = jnp.concatenate([h[n], h[n + 1]], axis=0).astype(BF16)
                v = gate_ref[rows, lanes]
                sig = 1.0 / (1.0 + jnp.exp2(v * (-LOG2E)))
                gated.append(y * (v * sig))
                ggrad.append(gg_ref[rows, lanes] * y * (sig * (1.0 + v * (1.0 - sig))))
            gated_ref[pair_rows, lanes] = jnp.concatenate(gated, axis=0).astype(BF16)
            ggrad_ref[pair_rows, lanes] = jnp.concatenate(ggrad, axis=0).astype(BF16)
        for n in range(states):
            state_ref[n, :, lanes] = h[n]
        return 0

    lax.fori_loop(0, width // LANES, tile_step, 0, unroll=2)


def forward(arrays, skip, carried, filled, shapes, chunk, first, last):
    step, mixed, gate, gg, wide_rows, rate = arrays
    rows, width = step.shape
    states, seqs, _ = rate.shape
    at = lambda i: first + i
    row_spec = pl.BlockSpec((chunk * seqs, width), lambda i: (at(i), 0))
    whole = pl.BlockSpec((states, seqs, width), lambda i: (0, 0, 0))
    anywhere = pl.BlockSpec(memory_space=pl.ANY)
    elements = (last - first) * chunk * seqs * width * states
    return pl.pallas_call(
        functools.partial(fwd_kernel, chunk),
        grid=(last - first,),
        in_specs=[row_spec, row_spec, row_spec, row_spec, spread_spec(chunk, states, seqs, at), whole,
                  pl.BlockSpec((seqs, width), lambda i: (0, 0)), whole] + [anywhere] * len(filled),
        out_specs=[whole, pl.BlockSpec((chunk, width // LANES, states * seqs, LANES), lambda i: (at(i), 0, 0, 0)),
                   pl.BlockSpec((1, states, seqs, width), lambda i: (at(i), 0, 0, 0)), row_spec, row_spec],
        out_shape=[jax.ShapeDtypeStruct(*shape) for shape in shapes],
        input_output_aliases={7 + i: i for i in range(len(filled) + 1)},
        compiler_params=pltpu.CompilerParams(vmem_limit_bytes=VM),
        cost_estimate=pl.CostEstimate(flops=elements, bytes_accessed=elements, transcendentals=0),
        name="scan_forward",
    )(step, mixed, gate, gg, wide_rows, rate, skip, carried, *filled)


def bwd_kernel(chunk, step_ref, mixed_ref, yg_ref, spread_ref, rate_ref, skip_ref, hist_ref, start_ref, gin_ref,
               decay_ref, bias_ref, skipg_ref, pre_ref, part_ref, bcg_ref, state_ref, b_ref, c_ref):
    states, seqs, width = rate_ref.shape
    span = states * seqs

    @pl.when(pl.program_id(0) == 0)
    def _():
        state_ref[...] = gin_ref[...]
        decay_ref[...] = jnp.zeros_like(decay_ref)
        bias_ref[...] = jnp.zeros_like(bias_ref)
        skipg_ref[...] = jnp.zeros_like(skipg_ref)

    b_ref[...] = jnp.zeros_like(b_ref)
    c_ref[...] = jnp.zeros_like(c_ref)
    contract = (((1,), (1,)), ((), ()))

    def tile_step(j, _):
        lanes = pl.ds(pl.multiple_of(j * LANES, LANES), LANES)
        q = [state_ref[n, :, lanes] for n in range(states)]
        acc = [decay_ref[n, :, lanes] for n in range(states)]
        skip = skip_ref[:, lanes]
        bias = bias_ref[:, lanes]
        skipg = skipg_ref[:, lanes]
        for tok in range(chunk - 2, -1, -2):
            pair_rows = pl.ds(tok * seqs, 2 * seqs)
            pair = mixed_ref[pair_rows, lanes].astype(F32)
            pre, xs, packed = [None, None], [None, None], [None, None]
            for k in (1, 0):
                now = tok + k
                rows = pl.ds(now * seqs, seqs)
                s = step_ref[rows, lanes]
                y = yg_ref[rows, lanes]
                m = pair[k * seqs : (k + 1) * seqs]
                along = jnp.zeros_like(s)
                size = jnp.zeros_like(s)
                gs = []
                for n in range(0, states, 2):
                    if now > 0:
                        both = hist_ref[now - 1, j, pl.ds(n * seqs, 2 * seqs), :].astype(F32)
                        before = [both[:seqs], both[seqs:]]
                    else:
                        before = [start_ref[0, n + i, :, lanes].astype(F32) for i in range(2)]
                    for i in range(2):
                        z = s * rate_ref[n + i, :, lanes]
                        g = spread_ref[now, states + n + i] * y + q[n + i]
                        along = along + g * spread_ref[now, n + i]
                        q[n + i] = jnp.exp2(z) * g
                        r = q[n + i] * before[i] * z
                        acc[n + i] = acc[n + i] + r
                        size = size + r
                        gs.append(g)
                packed[k] = jnp.concatenate(gs, axis=0).astype(BF16)
                part_ref[rows, lanes] = s * along + skip * y
                skipg = skipg + y * m
                xs[k] = s * m
                series = 1.0 - s * (1.0 / 2) * (1.0 - s * (1.0 / 3) * (1.0 - s * (1.0 / 4) * (1.0 - s * (1.0 / 5))))
                ratio = jnp.where(s < 0.1, series, (1.0 - jnp.exp2(s * (-LOG2E))) / jnp.maximum(s, 0.1))
                pre[k] = ratio * (size * (1.0 / LOG2E) + xs[k] * along)
            rounded = jnp.concatenate(pre, axis=0).astype(BF16)
            pre_ref[pair_rows, lanes] = rounded
            wide = rounded.astype(F32)
            bias = bias + wide[:seqs] + wide[seqs:]
            x = jnp.concatenate(xs, axis=0).astype(BF16)
            pair_hist = jnp.concatenate([hist_ref[tok, j], hist_ref[tok + 1, j]], axis=0)
            b_ref[tok // 2] += lax.dot_general(x, jnp.concatenate(packed, axis=0), contract, preferred_element_type=F32)
            c_ref[tok // 2] += lax.dot_general(
                yg_ref[pair_rows, lanes].astype(BF16), pair_hist, contract, preferred_element_type=F32
            )
        for n in range(states):
            state_ref[n, :, lanes] = q[n]
            decay_ref[n, :, lanes] = acc[n]
        bias_ref[:, lanes] = bias
        skipg_ref[:, lanes] = skipg
        return 0

    lax.fori_loop(0, width // LANES, tile_step, 0, unroll=2)
    wide = 2 * span
    row = lax.broadcasted_iota(jnp.int32, (2 * seqs, wide), 0)
    col = lax.broadcasted_iota(jnp.int32, (2 * seqs, wide), 1)
    match = (row // seqs == col // span) & (row % seqs == col % seqs)
    b_rows = [jnp.where(match, b_ref[i], 0.0) for i in range(chunk // 2)]
    c_rows = [jnp.where(match, c_ref[i], 0.0) for i in range(chunk // 2)]
    src = lax.broadcasted_iota(jnp.int32, (2 * states, wide), 1) // seqs % states
    dst = lax.broadcasted_iota(jnp.int32, (2 * states, wide), 0)
    fold_b = (src == dst).astype(BF16)
    fold_c = (src + states == dst).astype(BF16)
    bcg_ref[...] = lax.dot_general(
        fold_b, jnp.concatenate(b_rows, axis=0).astype(BF16), contract, preferred_element_type=F32
    ) + lax.dot_general(fold_c, jnp.concatenate(c_rows, axis=0).astype(BF16), contract, preferred_element_type=F32)


def backward(step, mixed, yg, wide_rows, rate, skip, hist, start, gin, chunk):
    rows, width = step.shape
    states, seqs, _ = rate.shape
    grid = rows // (chunk * seqs)
    elements = rows * width * states
    at = lambda i: grid - 1 - i
    row_spec = pl.BlockSpec((chunk * seqs, width), lambda i: (at(i), 0))
    col_spec = pl.BlockSpec((2 * states, chunk * seqs), lambda i: (0, at(i)))
    whole = pl.BlockSpec((states, seqs, width), lambda i: (0, 0, 0))
    one = pl.BlockSpec((seqs, width), lambda i: (0, 0))
    return pl.pallas_call(
        functools.partial(bwd_kernel, chunk),
        grid=(grid,),
        in_specs=[row_spec, row_spec, row_spec, spread_spec(chunk, states, seqs, at), whole, one,
                  pl.BlockSpec((chunk, width // LANES, states * seqs, LANES), lambda i: (at(i), 0, 0, 0)),
                  pl.BlockSpec((1, states, seqs, width), lambda i: (at(i), 0, 0, 0)), whole],
        out_specs=[whole, one, one, row_spec, row_spec, col_spec],
        out_shape=[jax.ShapeDtypeStruct(rate.shape, F32), jax.ShapeDtypeStruct((seqs, width), F32),
                   jax.ShapeDtypeStruct((seqs, width), F32), jax.ShapeDtypeStruct((rows, width), BF16),
                   jax.ShapeDtypeStruct((rows, width), F32), jax.ShapeDtypeStruct((2 * states, rows), F32)],
        scratch_shapes=[pltpu.VMEM(rate.shape, F32)] + [pltpu.VMEM((chunk // 2, 2 * seqs, 2 * states * seqs), F32)] * 2,
        compiler_params=pltpu.CompilerParams(vmem_limit_bytes=VM),
        cost_estimate=pl.CostEstimate(flops=elements, bytes_accessed=elements, transcendentals=0),
        name="scan_backward",
    )(step, mixed, yg, wide_rows, rate, skip, hist, start, gin)


EPSILON = 1e-05
CONTRACT_LAST = (((1,), (1,)), ((), ()))
CONTRACT_FIRST = (((0,), (0,)), ((), ()))


def dot(a, b, dims=(((1,), (0,)), ((), ())), out=F32):
    return lax.dot_general(a, b, dims, preferred_element_type=out)


def after(value, *done):
    return lax.optimization_barrier((value, done))[0]


def swapped(value, axis, bit):
    count = lax.axis_size(axis)
    return lax.ppermute(value, axis, [(i, i ^ (1 << bit)) for i in range(count)])


def moved(value, axis, distance):
    count = lax.axis_size(axis)
    return lax.ppermute(value, axis, [(i, i + distance) for i in range(count) if 0 <= i + distance < count])


def bits_of(axis):
    return lax.axis_size(axis).bit_length() - 1


def own_bit(axis, bit):
    return (lax.axis_index(axis) >> bit) & 1


def gathered(value, axis, meanwhile=()):
    count = lax.axis_size(axis)
    parts = {0: value}
    for bit in reversed(range(bits_of(axis))):
        fresh = {mask | (1 << bit): swapped(part, axis, bit) for mask, part in parts.items()}
        if len(parts) == 1:
            fresh, meanwhile = lax.optimization_barrier((fresh, meanwhile))
        parts |= fresh
    for bit in range(bits_of(axis)):
        high = own_bit(axis, bit) == 1
        parts = {m: jnp.where(high, parts[m ^ (1 << bit)], parts[m]) for m in range(count)}
    return jnp.concatenate([parts[m] for m in range(count)], axis=-1), meanwhile


def summed(value, axis, narrow_from):
    for bit in range(bits_of(axis)):
        sent = value.astype(BF16) if bit >= narrow_from else value
        value = value + swapped(sent, axis, bit).astype(F32)
    return value


def pick(value, dim, index):
    return lax.dynamic_index_in_dim(value, index, dim, keepdims=False)


class Scattered:
    def __init__(self, blocks, axis, order=None, halves=None):
        bits = bits_of(axis)
        self.axis, self.left, self.order = axis, list(range(bits)), list(order or range(bits))
        self.got, self.kept, self.sent = None, None, None
        if halves:
            self.kept, self.sent = halves
        else:
            self.value = blocks.reshape((2,) * bits + blocks.shape[1:])

    def split(self):
        if self.sent is not None:
            return
        bit = self.order[0]
        dim = len(self.left) - 1 - self.left.index(bit)
        mine = own_bit(self.axis, bit)
        self.kept, self.sent = pick(self.value, dim, mine), pick(self.value, dim, 1 - mine)

    def send(self):
        self.got = swapped(self.sent, self.axis, self.order[0])

    def add(self):
        bit = self.order.pop(0)
        self.left.remove(bit)
        value = self.kept.astype(F32) + self.got.astype(F32)
        self.value = value.astype(BF16) if self.left else value
        self.got, self.kept, self.sent = None, None, None


def start_all(sums, *values):
    sums = [s for s in sums if s.order]
    for s in sums:
        s.split()
    sent, values = lax.optimization_barrier(([s.sent for s in sums], values))
    for s, message in zip(sums, sent):
        s.sent = message
        s.send()
    return values


def end_all(sums, *values):
    sums = [s for s in sums if s.got is not None]
    got, values = lax.optimization_barrier(([s.got for s in sums], values))
    for s, message in zip(sums, got):
        s.got = message
        s.add()
    return values


def padded_rows(value, dim, multiple):
    width = -value.shape[dim] % multiple
    return jnp.pad(value, [(0, width if i == dim else 0) for i in range(value.ndim)])


class ScatteredWith(Scattered):
    def __init__(self, blocks, axis, order, extra):
        super().__init__(blocks, axis, order)
        self.extra = extra

    def split(self):
        super().split()
        upper = self.extra.astype(BF16)
        lower = (self.extra - upper.astype(F32)).astype(BF16)
        self.extra = upper.astype(F32) + lower.astype(F32)
        self.shape = self.sent.shape
        self.sent = jnp.concatenate([self.sent.reshape(-1, self.shape[-1]), upper, lower], axis=0)

    def add(self):
        count = self.extra.shape[0]
        upper, lower = self.got[-2 * count : -count], self.got[-count:]
        self.extra = self.extra + (upper.astype(F32) + lower.astype(F32))
        self.got = self.got[: -2 * count].reshape(self.shape)
        super().add()


def columns_by(value, axis, bit):
    count = lax.axis_size(axis)
    width = value.shape[1] // (count >> bit)
    parts = [value[:, i * width : (i + 1) * width] for i in range(count >> bit)]
    high = own_bit(axis, bit) == 1
    low, up = parts[0::2], parts[1::2]
    return [
        jnp.concatenate([jnp.where(high, b, a) for a, b in zip(one, two)], axis=1) for one, two in ((low, up), (up, low))
    ]


def rest_scattered(value, axis, bit):
    count = lax.axis_size(axis)
    groups = [[i for i in range(count) if (i >> bit) & 1 == side] for side in range(2)]
    value = value.reshape(-1, value.shape[-1])
    return lax.psum_scatter(value, axis, scatter_dimension=0, tiled=True, axis_index_groups=groups).astype(F32)


def finished_on_the_way(s):
    if s.got is not None:
        s.add()
    while s.order:
        s.split()
        s.send()
        s.add()
    return s.value


def entering(local, total, rate, axis, direction, fillers):
    states = rate.shape[0]
    enter, enter_sum = jnp.zeros_like(local), jnp.zeros_like(total)
    through, through_sum = local, total
    distance = 1
    filled, fillers = [], list(fillers)
    while distance < lax.axis_size(axis):
        upper = through_sum.astype(BF16)
        lower = (through_sum - upper.astype(F32)).astype(BF16)
        packet = jnp.concatenate([through.astype(BF16), upper[None], lower[None]], axis=0)
        got = moved(packet, axis, distance * direction)
        if fillers:
            out = fillers.pop(0)(packet, filled)
            got, out = lax.optimization_barrier((got, out))
            filled.append(out)
        got = got.astype(F32)
        state, step_sum = got[:states], got[states] + got[states + 1]
        enter, enter_sum = enter + jnp.exp2(rate * enter_sum) * state, enter_sum + step_sum
        through, through_sum = through + jnp.exp2(rate * through_sum) * state, through_sum + step_sum
        distance *= 2
    for filler in fillers:
        filled.append(filler(enter, filled))
    return enter, filled


def silu_slope(pre_value):
    sigmoid_value = jax.nn.sigmoid(pre_value)
    return sigmoid_value * (1.0 + pre_value * (1.0 - sigmoid_value))


def shards(
    residual_in,
    norm_gain,
    in_weight,
    conv_weight,
    conv_bias,
    proj_weight,
    step_weight,
    step_bias,
    decay_log,
    skip_gain,
    out_weight,
    out_grad,
):
    seqs, toks, share = residual_in.shape
    model = norm_gain.shape[0]
    taps, inner = conv_weight.shape
    states = decay_log.shape[0]
    rank = step_weight.shape[0]
    rows = seqs * toks
    chunk = math.gcd(toks, 16)
    chunks = toks // chunk
    seq_count = lax.axis_size("seq")
    chan_bits = bits_of("chan")
    own_in = residual_in.swapaxes(0, 1).reshape(rows, share)
    own_out_grad = out_grad.swapaxes(0, 1).reshape(rows, share)
    full_in, (conv_weights, gate_weights) = gathered(own_in, "chan", (in_weight[:, 0], in_weight[:, 1]))
    wide_in = full_in.astype(F32)
    inv_rms = lax.rsqrt(jnp.mean(wide_in * wide_in, axis=-1, keepdims=True) + EPSILON)
    gain_full = norm_gain.astype(F32)
    normed = (wide_in * inv_rms * gain_full).astype(BF16)
    conv_in = dot(normed, conv_weights, out=BF16)
    halo = (taps - 1) * seqs
    normed_halo = moved(normed[rows - halo :], "seq", 1)
    previous = dot(normed_halo, conv_weights, out=BF16)
    padded = jnp.concatenate([previous, conv_in], axis=0).astype(F32)
    conv_taps = conv_weight.astype(F32)
    conv_out = conv_bias.astype(F32) + sum(
        conv_taps[k] * padded[k * seqs : k * seqs + rows] for k in range(taps)
    )
    mixed = jax.nn.silu(conv_out).astype(BF16)
    proj_part = dot(proj_weight, mixed, CONTRACT_LAST)
    for bit in range(chan_bits):
        received = swapped(proj_part.astype(BF16) if bit else proj_part, "chan", bit)
        if bit == chan_bits - 1:
            gate_pre = dot(after(normed, proj_part), gate_weights)
            extended_normed = jnp.concatenate([normed_halo, after(normed, gate_pre)], axis=0)
            received, gate_pre, extended_normed = lax.optimization_barrier((received, gate_pre, extended_normed))
        proj_part = proj_part + received.astype(F32)
    projected = proj_part
    step_low = projected[:rank].astype(BF16)
    step_pre = dot(step_low, step_weight, CONTRACT_FIRST) + step_bias.astype(F32)
    step = jax.nn.softplus(step_pre)
    decay_rate = -jnp.exp(decay_log)
    rate = jnp.broadcast_to((decay_rate * LOG2E)[:, None], (states, seqs, inner))
    skip = jnp.broadcast_to(skip_gain, (seqs, inner))
    local_end, wide_rows = local_ends(step, mixed, projected[rank:], rate, chunk)
    step_total = jnp.sum(step.reshape(toks, seqs, inner), axis=0)
    grad_whole, _ = gathered(after(own_out_grad, gate_pre), "chan", local_end)

    def output_side(sent, _):
        gated_grad = dot(after(grad_whole, sent), out_weight)
        return gated_grad, gated_grad * jax.nn.silu(gate_pre)

    def starts_side(sent, filled):
        return local_starts(step, after(filled[0][1], sent), wide_rows, rate, chunk)

    seq_bits = list(range(bits_of("seq")))
    other_bits = [1, 0] + seq_bits[2:] if len(seq_bits) > 1 else seq_bits
    def columns_side(sent, _):
        return columns_by(after(grad_whole, sent), "seq", 0), columns_by(after(normed, sent), "seq", other_bits[0])

    enter_h, filled = entering(local_end, step_total, rate, "seq", 1, [output_side, starts_side, columns_side])
    (gated_grad, y_grad), local_start, sides = filled[:3]
    shapes = [
        (rate.shape, F32),
        ((toks, inner // LANES, states * seqs, LANES), BF16),
        ((chunks, states, seqs, inner), BF16),
        ((rows, inner), BF16),
        ((rows, inner), BF16),
    ]
    arrays = (step, mixed, gate_pre, gated_grad, wide_rows, rate)
    middle = chunks // 2

    def first_side(sent, _):
        return forward(arrays, skip, after(enter_h, sent), (), shapes, chunk, 0, middle)

    def second_side(sent, filled):
        state, *done = after(filled[1], sent)
        return forward(arrays, skip, state, done, shapes, chunk, middle, chunks)

    enter_g, filled = entering(
        local_start, step_total, rate, "seq", -1, [lambda sent, _: enter_h, first_side, second_side]
    )
    _, history, starts, gated_out, gate_grad = filled[2]
    by_owner = lambda value: value.reshape(rows, -1, share).swapaxes(0, 1)
    by_part = lambda value: value.reshape(seq_count, -1, value.shape[-1])
    first_product = lambda columns, value: dot(columns, value, CONTRACT_FIRST, out=BF16).reshape(
        (2,) * (len(seq_bits) - 1) + (-1, inner)
    )
    out_weight_sum = Scattered(None, "seq", seq_bits, (None, first_product(sides[0][1], gated_out)))
    gate_weight_sum = Scattered(None, "seq", other_bits, (None, first_product(sides[1][1], gate_grad)))
    weight_sums = [out_weight_sum, gate_weight_sum]
    start_all(weight_sums)
    for s, columns, value in zip(weight_sums, (sides[0][0], sides[1][0]), (gated_out, gate_grad)):
        s.kept = first_product(columns, after(value, *[s.sent for s in weight_sums]))
    enter_g = after(enter_g, [s.kept for s in weight_sums])
    decay_parts, bias_parts, skip_parts, pre_grad, mixed_part, bc_grads = backward(
        step, mixed, y_grad, wide_rows, rate, skip, history, starts, enter_g, chunk
    )
    pre_grad, bc_grads = end_all(weight_sums, pre_grad, bc_grads)
    out_weight_grad = rest_scattered(out_weight_sum.value, "seq", seq_bits[0])
    gate_weight_grad = rest_scattered(after(gate_weight_sum.value, out_weight_grad), "seq", other_bits[0])
    low_grad = dot(step_weight, pre_grad, CONTRACT_LAST)
    proj_sum = jnp.concatenate([low_grad, bc_grads], axis=0)
    for bit in range(chan_bits):
        received = swapped(proj_sum.astype(BF16) if bit else proj_sum, "chan", bit)
        if bit == chan_bits - 1:
            branch = dot(after(gated_out, proj_sum), out_weight, CONTRACT_LAST, out=BF16)
            received, branch = lax.optimization_barrier((received, branch))
        proj_sum = proj_sum + received.astype(F32)
    proj_grad = proj_sum.astype(BF16)
    branch_sum = Scattered(by_owner(branch), "chan")
    (proj_grad,) = start_all([branch_sum], proj_grad)
    proj_weight_part = dot(proj_grad, mixed, out=BF16)
    step_weight_part = dot(step_low, pre_grad, out=BF16)
    mixed_grad = mixed_part + dot(proj_grad, proj_weight, CONTRACT_FIRST)
    conv_grad = mixed_grad * silu_slope(conv_out)
    conv_bias_grad = jnp.sum(conv_grad, axis=0)
    conv_weight_grad = jnp.stack(
        [jnp.sum(conv_grad * padded[k * seqs : k * seqs + rows], axis=0) for k in range(taps)]
    )
    incoming = moved(conv_grad[:halo], "seq", -1)

    def spread_back(grads, count):
        return sum(conv_taps[k] * grads[(taps - 1 - k) * seqs : (taps - 1 - k) * seqs + count] for k in range(taps))

    none = jnp.zeros((halo, inner), F32)
    own_spread = spread_back(jnp.concatenate([none, conv_grad, none], axis=0), rows + halo).astype(BF16)
    own_spread, out_weight_grad = end_all([branch_sum], own_spread, out_weight_grad)
    half = inner // 2
    sums = jnp.concatenate(
        [
            jnp.sum(decay_parts, axis=1),
            conv_weight_grad,
            conv_bias_grad[None],
            jnp.sum(bias_parts, axis=0)[None],
            jnp.sum(skip_parts, axis=0)[None],
        ],
        axis=0,
    )

    sum_rows = sums.shape[0]
    sums = padded_rows(jnp.concatenate([sums[:, :half], sums[:, half:]], axis=0), 0, 16)

    def last_blocks(columns):
        conv_weights_part = dot(extended_normed, own_spread[:, columns], CONTRACT_FIRST, out=BF16)
        blocks = [by_part(conv_weights_part), by_part(proj_weight_part[:, columns]), by_part(step_weight_part[:, columns])]
        return padded_rows(jnp.concatenate(blocks, axis=1), 1, 16)

    last_sums = [
        ScatteredWith(last_blocks(slice(0, half)), "seq", seq_bits, sums),
        Scattered(last_blocks(slice(half, inner)), "seq", other_bits),
    ]
    last_sent = start_all([*last_sums, branch_sum], conv_grad, incoming)
    conv_grad, incoming = last_sent
    conv_in_grad = spread_back(jnp.concatenate([conv_grad, incoming], axis=0), rows).astype(BF16)
    gate_side = dot(gate_grad, after(gate_weights, [s.sent for s in last_sums]), CONTRACT_LAST)
    normed_part = (dot(conv_in_grad, conv_weights, CONTRACT_LAST) + gate_side).astype(BF16)
    (normed_part,) = end_all([*last_sums, branch_sum], normed_part)
    normed_sum = Scattered(by_owner(normed_part), "chan")
    conv_in_grad, row_gate = start_all([normed_sum, *last_sums], conv_in_grad, gate_grad)
    row_dots = jnp.sum(
        conv_in_grad.astype(F32) * conv_in.astype(F32) + row_gate.astype(F32) * gate_pre, axis=1
    )
    row_dots = summed(row_dots, "chan", chan_bits)[:, None]
    row_dots, gate_weight_grad = end_all([normed_sum, *last_sums], row_dots, gate_weight_grad)
    (row_dots,) = start_all([normed_sum, *last_sums], row_dots)
    (row_dots,) = end_all([normed_sum, *last_sums], row_dots)
    normed_grad = finished_on_the_way(normed_sum)
    wide_own = own_in.astype(F32)
    own_gain = lax.dynamic_slice_in_dim(gain_full, lax.axis_index("chan") * share, share, 0)
    in_rows = (
        own_out_grad.astype(F32)
        + inv_rms * own_gain * normed_grad
        - wide_own * (inv_rms * inv_rms / model) * row_dots
    ).astype(BF16)
    in_grad = in_rows.reshape(toks, seqs, share).swapaxes(0, 1)
    gain_grad = summed(jnp.sum(normed_grad * wide_own * inv_rms, axis=0), "seq", bits_of("seq"))
    last = jnp.concatenate([finished_on_the_way(s) for s in last_sums], axis=-1)
    sums = last_sums[0].extra
    sums = jnp.concatenate([sums[:sum_rows], sums[sum_rows : 2 * sum_rows]], axis=1)
    weight_share, proj_share, step_share = (count // seq_count for count in (model, proj_weight.shape[0], rank))
    block_rows = (own_in.astype(F32) + finished_on_the_way(branch_sum)).astype(BF16)
    block_out = block_rows.reshape(toks, seqs, share).swapaxes(0, 1)
    return (
        block_out,
        in_grad,
        gain_grad,
        jnp.stack([last[:weight_share], gate_weight_grad], axis=1),
        sums[states : states + taps],
        sums[states + taps],
        last[weight_share : weight_share + proj_share],
        last[weight_share + proj_share : weight_share + proj_share + step_share],
        sums[states + taps + 1],
        sums[:states] * (1.0 / LOG2E),
        sums[states + taps + 2],
        out_weight_grad.astype(F32),
    )


def solution(mesh):
    in_specs = (
        P(None, "seq", "chan"),
        P(),
        P(None, None, "chan"),
        P(None, "chan"),
        P("chan"),
        P(None, "chan"),
        P(None, "chan"),
        P("chan"),
        P(None, "chan"),
        P("chan"),
        P(None, "chan"),
        P(None, "seq", "chan"),
    )
    out_specs = (
        P(None, "seq", "chan"),
        P(None, "seq", "chan"),
        P("chan"),
        P("seq", None, "chan"),
        P(None, "chan"),
        P("chan"),
        P("seq", "chan"),
        P("seq", "chan"),
        P("chan"),
        P(None, "chan"),
        P("chan"),
        P("seq", "chan"),
    )
    return jax.shard_map(shards, mesh=mesh, in_specs=in_specs, out_specs=out_specs, check_vma=False)
```

```python
import functools, math
import jax, jax.numpy as jnp
from jax import lax
from jax.sharding import PartitionSpec as P
from jax.experimental import pallas as pl
from jax.experimental.pallas import tpu as pltpu

LANES = 128
LOG2E = 1.4426950408889634
VM = 56 * 1024 * 1024
F32, BF16 = jnp.float32, jnp.bfloat16


def spread(rows_ref, select_ref, spread_ref, chunk, count, seqs):
    left, parts = rows_ref[...], []
    for _ in range(3):
        parts.append(left.astype(BF16))
        left = left - parts[-1].astype(F32)
    stacked = jnp.concatenate(parts, axis=0)
    for col in range(0, count, 2):
        wide = lax.dot_general(
            stacked, select_ref[:, col * LANES : (col + 2) * LANES], (((0,), (0,)), ((), ())), preferred_element_type=F32
        )
        for tok in range(chunk):
            for i in range(2):
                spread_ref[tok, col + i] = wide[tok * seqs : (tok + 1) * seqs, i * LANES : (i + 1) * LANES]


def ends_kernel(chunk, step_ref, mixed_ref, rows_ref, rate_ref, h_ref, spread_ref, select_ref):
    states, seqs, width = rate_ref.shape

    @pl.when(pl.program_id(0) == 0)
    def _():
        h_ref[...] = jnp.zeros_like(h_ref)
        row = lax.broadcasted_iota(jnp.int32, select_ref.shape, 0)
        col = lax.broadcasted_iota(jnp.int32, select_ref.shape, 1)
        select_ref[...] = (row % (2 * states) == col // LANES).astype(BF16)

    spread(rows_ref, select_ref, spread_ref, chunk, 2 * states, seqs)

    def tile_step(j, _):
        lanes = pl.ds(pl.multiple_of(j * LANES, LANES), LANES)
        h = [h_ref[n, :, lanes] for n in range(states)]
        for tok in range(0, chunk, 2):
            m = mixed_ref[pl.ds(tok * seqs, 2 * seqs), lanes].astype(F32)
            for k in range(2):
                s = step_ref[pl.ds((tok + k) * seqs, seqs), lanes]
                x = s * m[k * seqs : (k + 1) * seqs]
                for n in range(states):
                    h[n] = jnp.exp2(s * rate_ref[n, :, lanes]) * h[n] + spread_ref[tok + k, n] * x
        for n in range(states):
            h_ref[n, :, lanes] = h[n]
        return 0

    lax.fori_loop(0, width // LANES, tile_step, 0, unroll=2)


def starts_kernel(chunk, step_ref, yg_ref, spread_ref, rate_ref, q_ref):
    states, seqs, width = rate_ref.shape

    @pl.when(pl.program_id(0) == 0)
    def _():
        q_ref[...] = jnp.zeros_like(q_ref)

    def tile_step(j, _):
        lanes = pl.ds(pl.multiple_of(j * LANES, LANES), LANES)
        q = [q_ref[n, :, lanes] for n in range(states)]
        for tok in reversed(range(chunk)):
            rows = pl.ds(tok * seqs, seqs)
            s, y = step_ref[rows, lanes], yg_ref[rows, lanes]
            for n in range(states):
                q[n] = jnp.exp2(s * rate_ref[n, :, lanes]) * (q[n] + spread_ref[tok, states + n] * y)
        for n in range(states):
            q_ref[n, :, lanes] = q[n]
        return 0

    lax.fori_loop(0, width // LANES, tile_step, 0, unroll=2)


def spread_spec(chunk, states, seqs, at):
    return pl.BlockSpec((chunk, 2 * states, seqs, LANES), lambda i: (at(i), 0, 0, 0))


def local_ends(step, mixed, rows_t, rate, chunk):
    rows, width = step.shape
    states, seqs, _ = rate.shape
    elements = rows * width * states
    grid = rows // (chunk * seqs)
    row_spec = pl.BlockSpec((chunk * seqs, width), lambda i: (i, 0))
    whole = pl.BlockSpec((states, seqs, width), lambda i: (0, 0, 0))
    return pl.pallas_call(
        functools.partial(ends_kernel, chunk),
        grid=(grid,),
        in_specs=[row_spec, row_spec, pl.BlockSpec((2 * states, chunk * seqs), lambda i: (0, i)), whole],
        out_specs=[whole, spread_spec(chunk, states, seqs, lambda i: i)],
        out_shape=[jax.ShapeDtypeStruct(rate.shape, F32), jax.ShapeDtypeStruct((rows // seqs, 2 * states, seqs, LANES), F32)],
        scratch_shapes=[pltpu.VMEM((6 * states, 2 * states * LANES), BF16)],
        compiler_params=pltpu.CompilerParams(vmem_limit_bytes=VM),
        cost_estimate=pl.CostEstimate(flops=elements, bytes_accessed=elements, transcendentals=0),
        name="local_ends",
    )(step, mixed, rows_t, rate)


def local_starts(step, yg, wide_rows, rate, chunk):
    rows, width = step.shape
    states, seqs, _ = rate.shape
    elements = rows * width * states
    grid = rows // (chunk * seqs)
    at = lambda i: grid - 1 - i
    row_spec = pl.BlockSpec((chunk * seqs, width), lambda i: (at(i), 0))
    whole = pl.BlockSpec((states, seqs, width), lambda i: (0, 0, 0))
    return pl.pallas_call(
        functools.partial(starts_kernel, chunk),
        grid=(grid,),
        in_specs=[row_spec, row_spec, spread_spec(chunk, states, seqs, at), whole],
        out_specs=whole,
        out_shape=jax.ShapeDtypeStruct(rate.shape, F32),
        compiler_params=pltpu.CompilerParams(vmem_limit_bytes=VM),
        cost_estimate=pl.CostEstimate(flops=elements, bytes_accessed=elements, transcendentals=0),
        name="local_starts",
    )(step, yg, wide_rows, rate)


def fwd_kernel(chunk, step_ref, mixed_ref, gate_ref, gg_ref, spread_ref, rate_ref, skip_ref,
               hin_ref, *refs):
    state_ref, hist_ref, start_ref, gated_ref, ggrad_ref = refs[-5:]
    states, seqs, width = rate_ref.shape

    @pl.when(pl.program_id(0) == 0)
    def _():
        state_ref[...] = hin_ref[...]

    start_ref[0] = state_ref[...].astype(BF16)

    def tile_step(j, _):
        lanes = pl.ds(pl.multiple_of(j * LANES, LANES), LANES)
        h = [state_ref[n, :, lanes] for n in range(states)]
        skip = skip_ref[:, lanes]
        for tok in range(0, chunk, 2):
            pair_rows = pl.ds(tok * seqs, 2 * seqs)
            pair = mixed_ref[pair_rows, lanes].astype(F32)
            gated, ggrad = [], []
            for k in range(2):
                rows = pl.ds((tok + k) * seqs, seqs)
                s = step_ref[rows, lanes]
                m = pair[k * seqs : (k + 1) * seqs]
                x = s * m
                y = skip * m
                for n in range(states):
                    h[n] = jnp.exp2(s * rate_ref[n, :, lanes]) * h[n] + spread_ref[tok + k, n] * x
                    y = y + spread_ref[tok + k, states + n] * h[n]
                for n in range(0, states, 2):
                    hist_ref[tok + k, j, pl.ds(n * seqs, 2 * seqs), :] = jnp.concatenate([h[n], h[n + 1]], axis=0).astype(BF16)
                v = gate_ref[rows, lanes]
                sig = 1.0 / (1.0 + jnp.exp2(v * (-LOG2E)))
                gated.append(y * (v * sig))
                ggrad.append(gg_ref[rows, lanes] * y * (sig * (1.0 + v * (1.0 - sig))))
            gated_ref[pair_rows, lanes] = jnp.concatenate(gated, axis=0).astype(BF16)
            ggrad_ref[pair_rows, lanes] = jnp.concatenate(ggrad, axis=0).astype(BF16)
        for n in range(states):
            state_ref[n, :, lanes] = h[n]
        return 0

    lax.fori_loop(0, width // LANES, tile_step, 0, unroll=2)


def forward(arrays, skip, carried, filled, shapes, chunk, first, last):
    step, mixed, gate, gg, wide_rows, rate = arrays
    rows, width = step.shape
    states, seqs, _ = rate.shape
    at = lambda i: first + i
    row_spec = pl.BlockSpec((chunk * seqs, width), lambda i: (at(i), 0))
    whole = pl.BlockSpec((states, seqs, width), lambda i: (0, 0, 0))
    anywhere = pl.BlockSpec(memory_space=pl.ANY)
    elements = (last - first) * chunk * seqs * width * states
    return pl.pallas_call(
        functools.partial(fwd_kernel, chunk),
        grid=(last - first,),
        in_specs=[row_spec, row_spec, row_spec, row_spec, spread_spec(chunk, states, seqs, at), whole,
                  pl.BlockSpec((seqs, width), lambda i: (0, 0)), whole] + [anywhere] * len(filled),
        out_specs=[whole, pl.BlockSpec((chunk, width // LANES, states * seqs, LANES), lambda i: (at(i), 0, 0, 0)),
                   pl.BlockSpec((1, states, seqs, width), lambda i: (at(i), 0, 0, 0)), row_spec, row_spec],
        out_shape=[jax.ShapeDtypeStruct(*shape) for shape in shapes],
        input_output_aliases={7 + i: i for i in range(len(filled) + 1)},
        compiler_params=pltpu.CompilerParams(vmem_limit_bytes=VM),
        cost_estimate=pl.CostEstimate(flops=elements, bytes_accessed=elements, transcendentals=0),
        name="scan_forward",
    )(step, mixed, gate, gg, wide_rows, rate, skip, carried, *filled)


def bwd_kernel(chunk, step_ref, mixed_ref, yg_ref, spread_ref, rate_ref, skip_ref, low_ref, hist_ref, start_ref, gin_ref,
               sums_ref, pre_ref, part_ref, proj_ref, decay_ref, bias_ref, skipg_ref, state_ref, b_ref, c_ref):
    states, seqs, width = rate_ref.shape
    span = states * seqs

    @pl.when(pl.program_id(0) == 0)
    def _():
        state_ref[...] = gin_ref[...]
        decay_ref[...] = jnp.zeros_like(decay_ref)
        bias_ref[...] = jnp.zeros_like(bias_ref)
        skipg_ref[...] = jnp.zeros_like(skipg_ref)

    b_ref[...] = jnp.zeros_like(b_ref)
    c_ref[...] = jnp.zeros_like(c_ref)
    contract = (((1,), (1,)), ((), ()))

    def tile_step(j, _):
        lanes = pl.ds(pl.multiple_of(j * LANES, LANES), LANES)
        q = [state_ref[n, :, lanes] for n in range(states)]
        acc = [decay_ref[n, :, lanes] for n in range(states)]
        skip = skip_ref[:, lanes]
        bias = bias_ref[:, lanes]
        skipg = skipg_ref[:, lanes]
        for tok in range(chunk - 2, -1, -2):
            pair_rows = pl.ds(tok * seqs, 2 * seqs)
            pair = mixed_ref[pair_rows, lanes].astype(F32)
            pre, xs, packed = [None, None], [None, None], [None, None]
            for k in (1, 0):
                now = tok + k
                rows = pl.ds(now * seqs, seqs)
                s = step_ref[rows, lanes]
                y = yg_ref[rows, lanes]
                m = pair[k * seqs : (k + 1) * seqs]
                along = jnp.zeros_like(s)
                size = jnp.zeros_like(s)
                gs = []
                for n in range(0, states, 2):
                    if now > 0:
                        both = hist_ref[now - 1, j, pl.ds(n * seqs, 2 * seqs), :].astype(F32)
                        before = [both[:seqs], both[seqs:]]
                    else:
                        before = [start_ref[0, n + i, :, lanes].astype(F32) for i in range(2)]
                    for i in range(2):
                        z = s * rate_ref[n + i, :, lanes]
                        g = spread_ref[now, states + n + i] * y + q[n + i]
                        along = along + g * spread_ref[now, n + i]
                        q[n + i] = jnp.exp2(z) * g
                        r = q[n + i] * before[i] * z
                        acc[n + i] = acc[n + i] + r
                        size = size + r
                        gs.append(g)
                packed[k] = jnp.concatenate(gs, axis=0).astype(BF16)
                part_ref[rows, lanes] = s * along + skip * y
                skipg = skipg + y * m
                xs[k] = s * m
                series = 1.0 - s * (1.0 / 2) * (1.0 - s * (1.0 / 3) * (1.0 - s * (1.0 / 4) * (1.0 - s * (1.0 / 5))))
                ratio = jnp.where(s < 0.1, series, (1.0 - jnp.exp2(s * (-LOG2E))) / jnp.maximum(s, 0.1))
                pre[k] = ratio * (size * (1.0 / LOG2E) + xs[k] * along)
            rounded = jnp.concatenate(pre, axis=0).astype(BF16)
            pre_ref[pair_rows, lanes] = rounded
            wide = rounded.astype(F32)
            bias = bias + wide[:seqs] + wide[seqs:]
            x = jnp.concatenate(xs, axis=0).astype(BF16)
            pair_hist = jnp.concatenate([hist_ref[tok, j], hist_ref[tok + 1, j]], axis=0)
            b_ref[tok // 2] += lax.dot_general(x, jnp.concatenate(packed, axis=0), contract, preferred_element_type=F32)
            c_ref[tok // 2] += lax.dot_general(
                yg_ref[pair_rows, lanes].astype(BF16), pair_hist, contract, preferred_element_type=F32
            )
        for n in range(states):
            state_ref[n, :, lanes] = q[n]
            decay_ref[n, :, lanes] = acc[n]
        bias_ref[:, lanes] = bias
        skipg_ref[:, lanes] = skipg
        return 0

    lax.fori_loop(0, width // LANES, tile_step, 0, unroll=2)
    wide = 2 * span
    row = lax.broadcasted_iota(jnp.int32, (2 * seqs, wide), 0)
    col = lax.broadcasted_iota(jnp.int32, (2 * seqs, wide), 1)
    match = (row // seqs == col // span) & (row % seqs == col % seqs)
    b_rows = [jnp.where(match, b_ref[i], 0.0) for i in range(chunk // 2)]
    c_rows = [jnp.where(match, c_ref[i], 0.0) for i in range(chunk // 2)]
    src = lax.broadcasted_iota(jnp.int32, (2 * states, wide), 1) // seqs % states
    dst = lax.broadcasted_iota(jnp.int32, (2 * states, wide), 0)
    fold_b = (src == dst).astype(BF16)
    fold_c = (src + states == dst).astype(BF16)
    rank = low_ref.shape[0]
    proj_ref[:rank] = lax.dot_general(low_ref[...], pre_ref[...], contract, preferred_element_type=F32)
    proj_ref[rank:] = lax.dot_general(
        fold_b, jnp.concatenate(b_rows, axis=0).astype(BF16), contract, preferred_element_type=F32
    ) + lax.dot_general(fold_c, jnp.concatenate(c_rows, axis=0).astype(BF16), contract, preferred_element_type=F32)

    @pl.when(pl.program_id(0) == pl.num_programs(0) - 1)
    def _():
        sums_ref[:states] = jnp.sum(decay_ref[...], axis=1) * (1.0 / LOG2E)
        sums_ref[states : states + 1] = jnp.sum(bias_ref[...], axis=0, keepdims=True)
        sums_ref[states + 1 : states + 2] = jnp.sum(skipg_ref[...], axis=0, keepdims=True)


def backward(step, mixed, yg, wide_rows, rate, skip, low_weight, hist, start, gin, chunk):
    rows, width = step.shape
    states, seqs, _ = rate.shape
    grid = rows // (chunk * seqs)
    elements = rows * width * states
    at = lambda i: grid - 1 - i
    row_spec = pl.BlockSpec((chunk * seqs, width), lambda i: (at(i), 0))
    rank = low_weight.shape[0]
    whole = pl.BlockSpec((states, seqs, width), lambda i: (0, 0, 0))
    one = pl.BlockSpec((seqs, width), lambda i: (0, 0))
    return pl.pallas_call(
        functools.partial(bwd_kernel, chunk),
        grid=(grid,),
        in_specs=[row_spec, row_spec, row_spec, spread_spec(chunk, states, seqs, at), whole, one,
                  pl.BlockSpec((rank, width), lambda i: (0, 0)),
                  pl.BlockSpec((chunk, width // LANES, states * seqs, LANES), lambda i: (at(i), 0, 0, 0)),
                  pl.BlockSpec((1, states, seqs, width), lambda i: (at(i), 0, 0, 0)), whole],
        out_specs=[pl.BlockSpec((states + 2, width), lambda i: (0, 0)), row_spec, row_spec,
                   pl.BlockSpec((rank + 2 * states, chunk * seqs), lambda i: (0, at(i)))],
        out_shape=[jax.ShapeDtypeStruct((states + 2, width), F32), jax.ShapeDtypeStruct((rows, width), BF16),
                   jax.ShapeDtypeStruct((rows, width), F32), jax.ShapeDtypeStruct((rank + 2 * states, rows), F32)],
        scratch_shapes=[pltpu.VMEM(rate.shape, F32), pltpu.VMEM((seqs, width), F32), pltpu.VMEM((seqs, width), F32),
                        pltpu.VMEM(rate.shape, F32)] + [pltpu.VMEM((chunk // 2, 2 * seqs, 2 * states * seqs), F32)] * 2,
        compiler_params=pltpu.CompilerParams(vmem_limit_bytes=VM),
        cost_estimate=pl.CostEstimate(flops=elements, bytes_accessed=elements, transcendentals=0),
        name="scan_backward",
    )(step, mixed, yg, wide_rows, rate, skip, low_weight, hist, start, gin)


def conv_kernel(chunk, taps, proj_ref, weight_ref, part_ref, conv_ref, in_ref, before_ref, taps_ref,
                spread_ref, first_ref, sums_ref, grad_ref, back_ref):
    rows, width = part_ref.shape
    seqs = rows // chunk
    halo = (taps - 1) * seqs
    lead = before_ref.shape[0]
    step = pl.program_id(0)
    block = pl.num_programs(0) - 1 - step

    @pl.when(step == 0)
    def _():
        grad_ref[rows:] = jnp.zeros_like(grad_ref[rows:])
        sums_ref[...] = jnp.zeros_like(sums_ref)

    @pl.when(step > 0)
    def _():
        grad_ref[rows : rows + halo] = grad_ref[:halo]

    back_ref[...] = lax.dot_general(
        proj_ref[...], weight_ref[...], (((0,), (0,)), ((), ())), preferred_element_type=F32
    )

    def tile_step(j, _):
        lanes = pl.ds(pl.multiple_of(j * LANES, LANES), LANES)
        tap = [taps_ref[k : k + 1, lanes] for k in range(taps)]
        sums = [sums_ref[k, :, lanes] for k in range(taps + 1)]
        for tok in reversed(range(0, chunk, 2)):
            at = pl.ds(tok * seqs, 2 * seqs)
            v = conv_ref[at, lanes]
            sig = 1.0 / (1.0 + jnp.exp2(v * (-LOG2E)))
            grad = (part_ref[at, lanes] + back_ref[at, lanes]) * (sig * (1.0 + v * (1.0 - sig)))
            grad_ref[at, lanes] = grad
            given = in_ref[at, lanes].astype(F32)
            spread = jnp.zeros_like(grad)
            for k in range(taps):
                later = grad_ref[pl.ds((tok + taps - 1 - k) * seqs, 2 * seqs), lanes]
                spread = spread + tap[k] * later
                use = given * later
                sums[k] = sums[k] + use[:seqs] + use[seqs:]
            sums[taps] = sums[taps] + grad[:seqs] + grad[seqs:]
            out_at = pl.multiple_of(lead + block * rows + tok * seqs, 2 * seqs)
            spread_ref[pl.ds(out_at, 2 * seqs), lanes] = spread.astype(BF16)
        for k in range(taps + 1):
            sums_ref[k, :, lanes] = sums[k]
        return 0

    lax.fori_loop(0, width // LANES, tile_step, 0, unroll=2)

    @pl.when(block == 0)
    def _():
        first_ref[...] = grad_ref[:halo]
        given = before_ref[...].astype(F32)
        parts = [jnp.zeros((lead - halo, width), F32)]
        for tok in range(taps - 1):
            spread = jnp.zeros((seqs, width), F32)
            own = given[lead - halo + tok * seqs : lead - halo + (tok + 1) * seqs]
            for k in range(tok + 1):
                later = grad_ref[(tok - k) * seqs : (tok - k + 1) * seqs]
                spread = spread + taps_ref[k : k + 1] * later
                sums_ref[k] = sums_ref[k] + own * later
            parts.append(spread)
        spread_ref[:lead] = jnp.concatenate(parts, axis=0).astype(BF16)


def conv_back(proj_grad, weight, part, conv_out, conv_in, before, conv_taps, chunk):
    rows, width = part.shape
    taps = conv_taps.shape[0]
    columns = proj_grad.shape[0]
    seqs, lead = 8, before.shape[0]
    halo = (taps - 1) * seqs
    grid = rows // (chunk * seqs)
    at = lambda i: grid - 1 - i
    row_spec = pl.BlockSpec((chunk * seqs, width), lambda i: (at(i), 0))
    fixed = lambda *shape: pl.BlockSpec(shape, lambda i: (0,) * len(shape))
    return pl.pallas_call(
        functools.partial(conv_kernel, chunk, taps),
        grid=(grid,),
        in_specs=[pl.BlockSpec((columns, chunk * seqs), lambda i: (0, at(i))), fixed(columns, width), row_spec, row_spec, row_spec,
                  fixed(lead, width), fixed(taps, width)],
        out_specs=[fixed(rows + lead, width), fixed(halo, width), fixed(taps + 1, seqs, width)],
        out_shape=[jax.ShapeDtypeStruct((rows + lead, width), BF16), jax.ShapeDtypeStruct((halo, width), F32),
                   jax.ShapeDtypeStruct((taps + 1, seqs, width), F32)],
        scratch_shapes=[pltpu.VMEM((chunk * seqs + lead, width), F32), pltpu.VMEM((chunk * seqs, width), F32)],
        compiler_params=pltpu.CompilerParams(vmem_limit_bytes=VM),
        cost_estimate=pl.CostEstimate(flops=rows * width, bytes_accessed=rows * width, transcendentals=0),
        name="conv_backward",
    )(proj_grad, weight, part, conv_out, conv_in, before, conv_taps)


def merge_kernel(plan, messages, bits_ref, *refs):
    refs = list(refs)
    inputs = [[refs.pop(0) for _ in range(len(sizes) + 1 + (extra > 0))] for _, _, sizes, extra, *_ in plan]
    outputs = [[refs.pop(0) for _ in range(len(sizes) + (extra > 0))] for _, _, sizes, extra, *_ in plan]
    sent = [refs.pop(0) for _ in range(messages)]
    for index, (levels, dim, sizes, extra, got_at, message, sent_at) in enumerate(plan):
        bit = bits_ref[index]
        kept, got, whole = inputs[index][: len(sizes)], inputs[index][len(sizes)], inputs[index][-1]
        kept_out, whole_out, sent_out = outputs[index][: len(sizes)], outputs[index][-1], sent[message]
        after_dim = 1 << (levels - 1 - dim)
        for size, source, target in zip(sizes, kept, kept_out):
            for rest in range(1 << (levels - 1)):
                high, low = divmod(rest, after_dim)
                for side in range(2):
                    own = bit if side == 0 else 1 - bit
                    at = pl.multiple_of(((high * 2 + own) * after_dim + low) * size, 16)
                    total = source[pl.ds(at, size), :].astype(F32) + got[pl.ds(got_at + at, size), :].astype(F32)
                    if side == 0:
                        target[rest * size : (rest + 1) * size, :] = total.astype(BF16)
                    else:
                        sent_out[sent_at + rest * size : sent_at + (rest + 1) * size, :] = total.astype(BF16)
            got_at += size << levels
            sent_at += size << (levels - 1)
        if extra:
            other = got[got_at : got_at + extra, :].astype(F32) + got[got_at + extra : got_at + 2 * extra, :].astype(F32)
            total = whole[...] + other
            upper = total.astype(BF16)
            lower = (total - upper.astype(F32)).astype(BF16)
            sent_out[sent_at : sent_at + extra, :] = upper
            sent_out[sent_at + extra : sent_at + 2 * extra, :] = lower
            whole_out[...] = upper.astype(F32) + lower.astype(F32)


def product_kernel(count, core_ref, *refs):
    del core_ref
    kept_ref, sent_ref = refs[-2:]
    total = None
    for a_ref, b_ref in zip(refs[:count], refs[count : 2 * count]):
        part = lax.dot_general(a_ref[...], b_ref[...], (((1,), (1,)), ((), ())), preferred_element_type=F32)
        total = part if total is None else total + part
    side = pl.program_id(1)

    @pl.when(side == 0)
    def _():
        kept_ref[0] = total.astype(BF16)

    @pl.when(side == 1)
    def _():
        sent_ref[0] = total.astype(BF16)


def product_sides(core, share, *pairs):
    rows, columns = pairs[0][0].shape[0], pairs[0][1].shape[0]
    chips = columns // share // 2
    mine = lambda far, side, core_ref: (far * 2 + jnp.where(side == 0, core_ref[0], 1 - core_ref[0]), 0)
    out_spec = pl.BlockSpec((1, rows, share), lambda far, side, core_ref: (far, 0, 0))
    return pl.pallas_call(
        functools.partial(product_kernel, len(pairs)),
        grid_spec=pltpu.PrefetchScalarGridSpec(
            num_scalar_prefetch=1,
            grid=(chips, 2),
            in_specs=[pl.BlockSpec(a.shape, lambda far, side, core_ref: (0, 0)) for a, _ in pairs]
            + [pl.BlockSpec((share, b.shape[1]), mine) for _, b in pairs],
            out_specs=[out_spec, out_spec],
        ),
        out_shape=[jax.ShapeDtypeStruct((chips, rows, share), BF16)] * 2,
        compiler_params=pltpu.CompilerParams(vmem_limit_bytes=VM),
        cost_estimate=pl.CostEstimate(flops=1024, bytes_accessed=1024, transcendentals=0),
        name="product_sides",
    )(core.reshape(1).astype(jnp.int32), *[a for a, _ in pairs], *[b for _, b in pairs])


EPSILON = 1e-05
CONTRACT_LAST = (((1,), (1,)), ((), ()))
CONTRACT_FIRST = (((0,), (0,)), ((), ()))


def dot(a, b, dims=(((1,), (0,)), ((), ())), out=F32):
    return lax.dot_general(a, b, dims, preferred_element_type=out)


def after(value, *done):
    return lax.optimization_barrier((value, done))[0]


def swapped(value, axis, bit):
    count = lax.axis_size(axis)
    return lax.ppermute(value, axis, [(i, i ^ (1 << bit)) for i in range(count)])


def moved(value, axis, distance):
    count = lax.axis_size(axis)
    return lax.ppermute(value, axis, [(i, i + distance) for i in range(count) if 0 <= i + distance < count])


def bits_of(axis):
    return lax.axis_size(axis).bit_length() - 1


def own_bit(axis, bit):
    return (lax.axis_index(axis) >> bit) & 1


def gathered(value, axis, meanwhile=()):
    count = lax.axis_size(axis)
    parts = {0: value}
    for bit in reversed(range(bits_of(axis))):
        fresh = {mask | (1 << bit): swapped(part, axis, bit) for mask, part in parts.items()}
        if len(parts) == 1:
            fresh, meanwhile = lax.optimization_barrier((fresh, meanwhile))
        parts |= fresh
    for bit in range(bits_of(axis)):
        high = own_bit(axis, bit) == 1
        parts = {m: jnp.where(high, parts[m ^ (1 << bit)], parts[m]) for m in range(count)}
    return jnp.concatenate([parts[m] for m in range(count)], axis=-1), meanwhile


def summed(value, axis, narrow_from):
    for bit in range(bits_of(axis)):
        sent = value.astype(BF16) if bit >= narrow_from else value
        value = value + swapped(sent, axis, bit).astype(F32)
    return value


def pick(value, dim, index):
    return lax.dynamic_index_in_dim(value, index, dim, keepdims=False)


class Scattered:
    def __init__(self, blocks, axis, order=None, halves=None):
        bits = bits_of(axis)
        self.axis, self.left, self.order = axis, list(range(bits)), list(order or range(bits))
        self.got, self.kept, self.sent = None, None, None
        if halves:
            self.kept, self.sent = halves
        else:
            self.value = blocks.reshape((2,) * bits + blocks.shape[1:])

    def split(self):
        if self.sent is not None:
            return
        bit = self.order[0]
        dim = len(self.left) - 1 - self.left.index(bit)
        mine = own_bit(self.axis, bit)
        self.kept, self.sent = pick(self.value, dim, mine), pick(self.value, dim, 1 - mine)

    def send(self):
        self.got = swapped(self.sent, self.axis, self.order[0])

    def add(self):
        bit = self.order.pop(0)
        self.left.remove(bit)
        value = self.kept.astype(F32) + self.got.astype(F32)
        self.value = value.astype(BF16) if self.left else value
        self.got, self.kept, self.sent = None, None, None


def start_all(sums, *values):
    sums = [s for s in sums if s.order]
    for s in sums:
        s.split()
    sent, values = lax.optimization_barrier(([s.sent for s in sums], values))
    for s, message in zip(sums, sent):
        s.sent = message
        s.send()
    return values


def end_all(sums, *values):
    sums = [s for s in sums if s.got is not None]
    got, values = lax.optimization_barrier(([s.got for s in sums], values))
    for s, message in zip(sums, got):
        s.got = message
        s.add()
    return values


def padded_rows(value, dim, multiple):
    width = -value.shape[dim] % multiple
    return jnp.pad(value, [(0, width if i == dim else 0) for i in range(value.ndim)])


def two_parts(value):
    upper = value.astype(BF16)
    return upper, (value - upper.astype(F32)).astype(BF16)


class Chain:
    def __init__(self, pieces, axis, order, whole=None, halves=None):
        bits = bits_of(axis)
        self.axis, self.order, self.left, self.whole, self.at = axis, list(order), list(range(bits)), [], 0
        if halves:
            self.sizes = [halves[1].shape[0] >> (bits - 1)]
            self.kept, self.sent = [halves[0]], halves[1]
            return
        self.sizes = [piece.shape[1] for piece in pieces]
        dim = bits - 1 - self.order[0]
        mine = own_bit(axis, self.order[0])
        halves = [piece.reshape((2,) * bits + piece.shape[1:]) for piece in pieces]
        flat = lambda value: value.reshape(-1, value.shape[-1])
        self.kept = [flat(pick(value, dim, mine)) for value in halves]
        message = [flat(pick(value, dim, 1 - mine)) for value in halves]
        if whole is not None:
            upper, lower = two_parts(whole)
            self.whole = [upper.astype(F32) + lower.astype(F32)]
            message += [upper, lower]
        self.sent = jnp.concatenate(message, axis=0) if len(message) > 1 else message[0]

    def finish(self):
        rows, values = self.at, []
        for size, kept in zip(self.sizes, self.kept):
            values.append(kept.astype(F32) + self.got[rows : rows + size].astype(F32))
            rows += size
        if self.whole:
            count = self.whole[0].shape[0]
            upper, lower = (self.got[rows + i * count : rows + (i + 1) * count].astype(F32) for i in range(2))
            values.append(self.whole[0] + (upper + lower))
        return values


def send_chains(groups, messages, *values):
    messages, values = lax.optimization_barrier((messages, values))
    for group, message in zip(groups, messages):
        got = swapped(message, group[0].axis, group[0].order[0])
        for c in group:
            c.got = got
            c.left.remove(c.order.pop(0))
    return values


def end_chains(groups, *values):
    got, values = lax.optimization_barrier(([group[0].got for group in groups], values))
    for group, message in zip(groups, got):
        for c in group:
            c.got = message
    return values


def last_of(chain):
    while chain.order:
        send_chains([[chain]], merge([[chain]]))
    return chain.finish()


def merge(groups):
    plan, operands, outputs, messages = [], [], [], []
    for number, group in enumerate(groups):
        rows = 0
        for c in group:
            levels, extra = len(c.left), c.whole[0].shape[0] if c.whole else 0
            columns = c.got.shape[1]
            plan.append((levels, levels - 1 - c.left.index(c.order[0]), tuple(c.sizes), extra, c.at, number, rows))
            operands += [*c.kept, c.got, *c.whole]
            outputs += [((size << (levels - 1), columns), BF16) for size in c.sizes] + [((extra, columns), F32)] * (extra > 0)
            c.at = rows
            rows += sum(size << (levels - 1) for size in c.sizes) + 2 * extra
        messages.append(((rows, columns), BF16))
    chains = [c for group in groups for c in group]
    bits = jnp.stack([own_bit(c.axis, c.order[0]) for c in chains]).astype(jnp.int32)
    outs = list(
        pl.pallas_call(
            functools.partial(merge_kernel, plan, len(messages)),
            in_specs=[pl.BlockSpec(memory_space=pltpu.SMEM)] + [pl.BlockSpec(memory_space=pltpu.VMEM)] * len(operands),
            out_specs=[pl.BlockSpec(memory_space=pltpu.VMEM)] * (len(outputs) + len(messages)),
            out_shape=[jax.ShapeDtypeStruct(*shape) for shape in outputs + messages],
            compiler_params=pltpu.CompilerParams(vmem_limit_bytes=VM),
            cost_estimate=pl.CostEstimate(flops=1024, bytes_accessed=1024, transcendentals=0),
            name="merge_messages",
        )(bits, *operands)
    )
    for c in chains:
        c.kept = [outs.pop(0) for _ in c.sizes]
        c.whole = [outs.pop(0) for _ in c.whole]
    return outs


def columns_by(value, axis, bit):
    count = lax.axis_size(axis)
    width = value.shape[1] // (count >> bit)
    parts = [value[:, i * width : (i + 1) * width] for i in range(count >> bit)]
    high = own_bit(axis, bit) == 1
    low, up = parts[0::2], parts[1::2]
    return [
        jnp.concatenate([jnp.where(high, b, a) for a, b in zip(one, two)], axis=1) for one, two in ((low, up), (up, low))
    ]


def finished_on_the_way(s):
    if s.got is not None:
        s.add()
    while s.order:
        s.split()
        s.send()
        s.add()
    return s.value


def entering(local, total, rate, axis, direction, fillers):
    states = rate.shape[0]
    enter, enter_sum = jnp.zeros_like(local), jnp.zeros_like(total)
    through, through_sum = local, total
    distance = 1
    filled, fillers = [], list(fillers)
    while distance < lax.axis_size(axis):
        upper = through_sum.astype(BF16)
        lower = (through_sum - upper.astype(F32)).astype(BF16)
        packet = jnp.concatenate([through.astype(BF16), upper[None], lower[None]], axis=0)
        got = moved(packet, axis, distance * direction)
        if fillers:
            out = fillers.pop(0)(packet, filled)
            got, out = lax.optimization_barrier((got, out))
            filled.append(out)
        got = got.astype(F32)
        state, step_sum = got[:states], got[states] + got[states + 1]
        enter, enter_sum = enter + jnp.exp2(rate * enter_sum) * state, enter_sum + step_sum
        through, through_sum = through + jnp.exp2(rate * through_sum) * state, through_sum + step_sum
        distance *= 2
    for filler in fillers:
        filled.append(filler(enter, filled))
    return enter, filled


def silu_slope(pre_value):
    sigmoid_value = jax.nn.sigmoid(pre_value)
    return sigmoid_value * (1.0 + pre_value * (1.0 - sigmoid_value))


def shards(
    residual_in,
    norm_gain,
    in_weight,
    conv_weight,
    conv_bias,
    proj_weight,
    step_weight,
    step_bias,
    decay_log,
    skip_gain,
    out_weight,
    out_grad,
):
    seqs, toks, share = residual_in.shape
    model = norm_gain.shape[0]
    taps, inner = conv_weight.shape
    states = decay_log.shape[0]
    rank = step_weight.shape[0]
    rows = seqs * toks
    chunk = math.gcd(toks, 16)
    chunks = toks // chunk
    seq_count = lax.axis_size("seq")
    chan_bits = bits_of("chan")
    own_in = residual_in.swapaxes(0, 1).reshape(rows, share)
    own_out_grad = out_grad.swapaxes(0, 1).reshape(rows, share)
    full_in, (conv_weights, gate_weights) = gathered(own_in, "chan", (in_weight[:, 0], in_weight[:, 1]))
    wide_in = full_in.astype(F32)
    inv_rms = lax.rsqrt(jnp.mean(wide_in * wide_in, axis=-1, keepdims=True) + EPSILON)
    gain_full = norm_gain.astype(F32)
    normed = (wide_in * inv_rms * gain_full).astype(BF16)
    conv_in = dot(normed, conv_weights, out=BF16)
    halo = (taps - 1) * seqs
    lead = halo + -halo % 16
    normed_halo = moved(normed[rows - lead :], "seq", 1)
    previous = dot(normed_halo, conv_weights, out=BF16)
    padded = jnp.concatenate([previous[lead - halo :], conv_in], axis=0).astype(F32)
    conv_taps = conv_weight.astype(F32)
    conv_out = conv_bias.astype(F32) + sum(
        conv_taps[k] * padded[k * seqs : k * seqs + rows] for k in range(taps)
    )
    mixed = jax.nn.silu(conv_out).astype(BF16)
    proj_part = dot(proj_weight, mixed, CONTRACT_LAST)
    for bit in range(chan_bits):
        received = swapped(proj_part.astype(BF16) if bit else proj_part, "chan", bit)
        if bit == chan_bits - 1:
            gate_pre = dot(after(normed, proj_part), gate_weights)
            extended_normed = jnp.concatenate([normed_halo, after(normed, gate_pre)], axis=0)
            received, gate_pre, extended_normed = lax.optimization_barrier((received, gate_pre, extended_normed))
        proj_part = proj_part + received.astype(F32)
    projected = proj_part
    step_low = projected[:rank].astype(BF16)
    step_pre = dot(step_low, step_weight, CONTRACT_FIRST) + step_bias.astype(F32)
    step = jax.nn.softplus(step_pre)
    decay_rate = -jnp.exp(decay_log)
    rate = jnp.broadcast_to((decay_rate * LOG2E)[:, None], (states, seqs, inner))
    skip = jnp.broadcast_to(skip_gain, (seqs, inner))
    local_end, wide_rows = local_ends(step, mixed, projected[rank:], rate, chunk)
    step_total = jnp.sum(step.reshape(toks, seqs, inner), axis=0)
    grad_whole, _ = gathered(after(own_out_grad, gate_pre), "chan", local_end)

    def output_side(sent, _):
        gated_grad = dot(after(grad_whole, sent), out_weight)
        return gated_grad, gated_grad * jax.nn.silu(gate_pre)

    def starts_side(sent, filled):
        return local_starts(step, after(filled[0][1], sent), wide_rows, rate, chunk)

    seq_bits = list(range(bits_of("seq")))
    other_bits = [1, 0] + seq_bits[2:] if len(seq_bits) > 1 else seq_bits
    def columns_side(sent, _):
        return columns_by(after(grad_whole, sent), "seq", 0), columns_by(after(normed, sent), "seq", other_bits[0])

    enter_h, filled = entering(local_end, step_total, rate, "seq", 1, [output_side, starts_side, columns_side])
    (gated_grad, y_grad), local_start, sides = filled[:3]
    shapes = [
        (rate.shape, F32),
        ((toks, inner // LANES, states * seqs, LANES), BF16),
        ((chunks, states, seqs, inner), BF16),
        ((rows, inner), BF16),
        ((rows, inner), BF16),
    ]
    arrays = (step, mixed, gate_pre, gated_grad, wide_rows, rate)
    middle = chunks // 2

    def first_side(sent, _):
        return forward(arrays, skip, after(enter_h, sent), (), shapes, chunk, 0, middle)

    def second_side(sent, filled):
        state, *done = after(filled[1], sent)
        return forward(arrays, skip, state, done, shapes, chunk, middle, chunks)

    enter_g, filled = entering(
        local_start, step_total, rate, "seq", -1, [lambda sent, _: enter_h, first_side, second_side]
    )
    _, history, starts, gated_out, gate_grad = filled[2]
    by_part = lambda value: value.reshape(seq_count, -1, value.shape[-1])
    first_product = lambda columns, value: dot(columns, value, CONTRACT_FIRST, out=BF16)
    out_sent, gate_sent = (
        first_product(columns[1], value) for columns, value in zip(sides, (gated_out, gate_grad))
    )
    out_kept, gate_kept = (
        first_product(columns[0], after(value, out_sent, gate_sent)) for columns, value in zip(sides, (gated_out, gate_grad))
    )
    out_chain = Chain(None, "seq", seq_bits, halves=(out_kept, out_sent))
    gate_chain = Chain(None, "seq", other_bits, halves=(gate_kept, gate_sent))
    apart, joint = [[out_chain], [gate_chain]], [[out_chain, gate_chain]]
    (enter_g,) = send_chains(apart, [out_sent, gate_sent], enter_g)
    enter_g = after(enter_g, out_kept, gate_kept)
    chips = (2,) * (chan_bits - 1)

    def features(*pairs):
        sides = product_sides(own_bit("chan", 0), share, *pairs)
        return tuple(side.reshape(chips + side.shape[1:]) for side in sides)

    scan_sums, pre_grad, mixed_part, proj_sum = backward(
        step, mixed, y_grad, wide_rows, rate, skip, step_weight, history, starts, enter_g, chunk
    )
    pre_grad, proj_sum = end_chains(apart, pre_grad, proj_sum)
    for bit in range(chan_bits):
        received = swapped(proj_sum.astype(BF16) if bit else proj_sum, "chan", bit)
        if bit == 0:
            (received,) = send_chains(apart, merge(apart), received)
        if bit == chan_bits - 1:
            branch_sum = Scattered(None, "chan", halves=features((after(gated_out, proj_sum), out_weight)))
            received, branch_sum.kept, branch_sum.sent = lax.optimization_barrier(
                (received, branch_sum.kept, branch_sum.sent)
            )
        proj_sum = proj_sum + received.astype(F32)
    proj_grad = proj_sum.astype(BF16)
    own_spread, first_grad, conv_sums = conv_back(
        proj_grad, proj_weight, mixed_part, conv_out, conv_in, previous, conv_taps, chunk
    )
    incoming = moved(first_grad, "seq", -1)
    (own_spread,) = end_chains(apart, own_spread)
    half = inner // 2
    first_last, second_last = (
        by_part(dot(extended_normed, own_spread[:, at : at + half], CONTRACT_FIRST, out=BF16)) for at in (0, half)
    )
    first, second = Chain([first_last], "seq", seq_bits), Chain([second_last], "seq", other_bits)
    weight_message = merge(apart)
    in_window = [[first], [second], [out_chain]]
    (own_spread,) = start_all([branch_sum], own_spread)
    own_spread, incoming = send_chains(in_window, [first.sent, second.sent, weight_message[0]], own_spread, incoming)
    zeros = jnp.zeros((halo, inner), F32)
    from_after = jnp.concatenate([zeros, incoming, zeros], axis=0)
    late = sum(
        conv_taps[k] * from_after[(2 * taps - 2 - k) * seqs - halo : (2 * taps - 2 - k) * seqs] for k in range(taps)
    )
    conv_in_grad = jnp.concatenate(
        [own_spread[lead : lead + rows - halo], (own_spread[lead + rows - halo :].astype(F32) + late).astype(BF16)], axis=0
    )
    late_proj, late_pre, late_sums = after((proj_grad, pre_grad, conv_sums), own_spread)
    proj_weight_part = dot(late_proj, mixed, out=BF16)
    step_weight_part = dot(step_low, late_pre, out=BF16)
    sums = jnp.concatenate([scan_sums, jnp.sum(late_sums, axis=1)], axis=0)
    sum_rows = sums.shape[0]
    sums = padded_rows(jnp.concatenate([sums[:, :half], sums[:, half:]], axis=0), 0, 16)
    small_blocks = jnp.concatenate([by_part(proj_weight_part), by_part(step_weight_part)], axis=1)
    small_blocks = padded_rows(jnp.concatenate([small_blocks[..., :half], small_blocks[..., half:]], axis=1), 1, 16)
    third = Chain([small_blocks], "seq", seq_bits, sums)
    row_dots = jnp.sum(
        conv_in_grad.astype(F32) * conv_in.astype(F32) + gate_grad.astype(F32) * gate_pre, axis=1
    )
    last_pair = (gate_grad, after(gate_weights, third.sent, row_dots))
    normed_sum = Scattered(None, "chan", halves=features((conv_in_grad, conv_weights), last_pair))
    normed_sum.sent, normed_sum.kept, third.sent = end_chains(
        in_window, normed_sum.sent, normed_sum.kept, third.sent
    )
    row_dots, third.sent = end_all([branch_sum], row_dots, third.sent)
    groups = [[first], [second]]
    messages = merge(groups)
    (row_dots,) = start_all([normed_sum, branch_sum], row_dots)
    in_window = [*groups, [third], [gate_chain]]
    (row_dots,) = send_chains(in_window, [*messages, third.sent, weight_message[1]], row_dots)
    row_dots = row_dots + swapped(row_dots, "chan", 0)
    (row_dots,) = end_all([normed_sum, branch_sum], row_dots)
    (row_dots,) = end_chains(in_window, row_dots)
    groups = [[first], [second], [third]]
    messages = merge(groups)
    (row_dots,) = start_all([normed_sum], row_dots)
    (row_dots,) = send_chains(groups, messages, row_dots)
    for bit in range(1, chan_bits):
        row_dots = row_dots + swapped(row_dots, "chan", bit)
    (row_dots,) = end_all([normed_sum], row_dots)
    (row_dots,) = end_chains(groups, row_dots)
    normed_grad = finished_on_the_way(normed_sum)
    row_dots = row_dots[:, None]
    wide_own = own_in.astype(F32)
    own_gain = lax.dynamic_slice_in_dim(gain_full, lax.axis_index("chan") * share, share, 0)
    in_rows = (
        own_out_grad.astype(F32)
        + inv_rms * own_gain * normed_grad
        - wide_own * (inv_rms * inv_rms / model) * row_dots
    ).astype(BF16)
    in_grad = in_rows.reshape(toks, seqs, share).swapaxes(0, 1)
    gain_grad = summed(jnp.sum(normed_grad * wide_own * inv_rms, axis=0), "seq", bits_of("seq"))
    (first_last,), (second_last,), (small, sums) = last_of(first), last_of(second), last_of(third)
    (out_weight_grad,), (gate_weight_grad,) = last_of(out_chain), last_of(gate_chain)
    last = jnp.concatenate([first_last, second_last], axis=1)
    sums = jnp.concatenate([sums[:sum_rows], sums[sum_rows : 2 * sum_rows]], axis=1)
    proj_share, step_share = proj_weight.shape[0] // seq_count, rank // seq_count
    each = proj_share + step_share
    small_of = lambda start, count: jnp.concatenate([small[start : start + count], small[each + start : each + start + count]], axis=1)
    block_rows = (own_in.astype(F32) + finished_on_the_way(branch_sum)).astype(BF16)
    block_out = block_rows.reshape(toks, seqs, share).swapaxes(0, 1)
    return (
        block_out,
        in_grad,
        gain_grad,
        jnp.stack([last, gate_weight_grad], axis=1),
        sums[states + 2 : states + 2 + taps],
        sums[states + 2 + taps],
        small_of(0, proj_share),
        small_of(proj_share, step_share),
        sums[states],
        sums[:states],
        sums[states + 1],
        out_weight_grad,
    )


def solution(mesh):
    in_specs = (
        P(None, "seq", "chan"),
        P(),
        P(None, None, "chan"),
        P(None, "chan"),
        P("chan"),
        P(None, "chan"),
        P(None, "chan"),
        P("chan"),
        P(None, "chan"),
        P("chan"),
        P(None, "chan"),
        P(None, "seq", "chan"),
    )
    out_specs = (
        P(None, "seq", "chan"),
        P(None, "seq", "chan"),
        P("chan"),
        P("seq", None, "chan"),
        P(None, "chan"),
        P("chan"),
        P("seq", "chan"),
        P("seq", "chan"),
        P("chan"),
        P(None, "chan"),
        P("chan"),
        P("seq", "chan"),
    )
    return jax.shard_map(shards, mesh=mesh, in_specs=in_specs, out_specs=out_specs, check_vma=False)
```

```python
import functools, math
import jax, jax.numpy as jnp
from jax import lax
from jax.sharding import PartitionSpec as P
from jax.experimental import pallas as pl
from jax.experimental.pallas import tpu as pltpu

LANES = 128
LOG2E = 1.4426950408889634
VM = 56 * 1024 * 1024
F32, BF16 = jnp.float32, jnp.bfloat16


def spread(rows_ref, select_ref, spread_ref, narrow_ref, chunk, count, seqs):
    left, parts = rows_ref[...], []
    for _ in range(3):
        parts.append(left.astype(BF16))
        left = left - parts[-1].astype(F32)
    stacked = jnp.concatenate(parts, axis=0)
    for col in range(0, count, 2):
        wide = lax.dot_general(
            stacked, select_ref[:, col * LANES : (col + 2) * LANES], (((0,), (0,)), ((), ())), preferred_element_type=F32
        )
        for tok in range(chunk):
            both = [wide[tok * seqs : (tok + 1) * seqs, i * LANES : (i + 1) * LANES] for i in range(2)]
            for i in range(2):
                spread_ref[tok, col + i] = both[i]
            narrow_ref[tok, pl.ds(col * seqs, 2 * seqs), :] = jnp.concatenate(both, axis=0).astype(BF16)


def ends_kernel(chunk, step_ref, mixed_ref, rows_ref, rate_ref, h_ref, spread_ref, narrow_ref, select_ref):
    states, seqs, width = rate_ref.shape

    @pl.when(pl.program_id(0) == 0)
    def _():
        h_ref[...] = jnp.zeros_like(h_ref)
        row = lax.broadcasted_iota(jnp.int32, select_ref.shape, 0)
        col = lax.broadcasted_iota(jnp.int32, select_ref.shape, 1)
        select_ref[...] = (row % (2 * states) == col // LANES).astype(BF16)

    spread(rows_ref, select_ref, spread_ref, narrow_ref, chunk, 2 * states, seqs)

    def tile_step(j, _):
        lanes = pl.ds(pl.multiple_of(j * LANES, LANES), LANES)
        h = [h_ref[n, :, lanes] for n in range(states)]
        for tok in range(0, chunk, 2):
            m = mixed_ref[pl.ds(tok * seqs, 2 * seqs), lanes].astype(F32)
            for k in range(2):
                s = step_ref[pl.ds((tok + k) * seqs, seqs), lanes]
                x = s * m[k * seqs : (k + 1) * seqs]
                for n in range(states):
                    h[n] = jnp.exp2(s * rate_ref[n, :, lanes]) * h[n] + spread_ref[tok + k, n] * x
        for n in range(states):
            h_ref[n, :, lanes] = h[n]
        return 0

    lax.fori_loop(0, width // LANES, tile_step, 0, unroll=2)


def starts_kernel(chunk, step_ref, yg_ref, spread_ref, rate_ref, q_ref):
    states, seqs, width = rate_ref.shape

    @pl.when(pl.program_id(0) == 0)
    def _():
        q_ref[...] = jnp.zeros_like(q_ref)

    def tile_step(j, _):
        lanes = pl.ds(pl.multiple_of(j * LANES, LANES), LANES)
        q = [q_ref[n, :, lanes] for n in range(states)]
        for tok in reversed(range(chunk)):
            rows = pl.ds(tok * seqs, seqs)
            s, y = step_ref[rows, lanes], yg_ref[rows, lanes]
            for n in range(states):
                q[n] = jnp.exp2(s * rate_ref[n, :, lanes]) * (q[n] + spread_ref[tok, n] * y)
        for n in range(states):
            q_ref[n, :, lanes] = q[n]
        return 0

    lax.fori_loop(0, width // LANES, tile_step, 0, unroll=2)


def spread_spec(chunk, count, seqs, part, at):
    return pl.BlockSpec((chunk, count, seqs, LANES), lambda i: (at(i), part, 0, 0))


def narrow_spec(chunk, count, seqs, part, at):
    return pl.BlockSpec((chunk, count * seqs, LANES), lambda i: (at(i), part, 0))


def halves_sum(parts):
    while len(parts) > 1:
        parts = [a + b for a, b in zip(parts[::2], parts[1::2])]
    total = parts[0].astype(F32)
    seqs = total.shape[0] // 2
    return total[:seqs] + total[seqs:]


def local_ends(step, mixed, rows_t, rate, chunk):
    rows, width = step.shape
    states, seqs, _ = rate.shape
    elements = rows * width * states
    grid = rows // (chunk * seqs)
    row_spec = pl.BlockSpec((chunk * seqs, width), lambda i: (i, 0))
    whole = pl.BlockSpec((states, seqs, width), lambda i: (0, 0, 0))
    return pl.pallas_call(
        functools.partial(ends_kernel, chunk),
        grid=(grid,),
        in_specs=[row_spec, row_spec, pl.BlockSpec((2 * states, chunk * seqs), lambda i: (0, i)), whole],
        out_specs=[whole, spread_spec(chunk, 2 * states, seqs, 0, lambda i: i), narrow_spec(chunk, 2 * states, seqs, 0, lambda i: i)],
        out_shape=[jax.ShapeDtypeStruct(rate.shape, F32), jax.ShapeDtypeStruct((rows // seqs, 2 * states, seqs, LANES), F32),
                   jax.ShapeDtypeStruct((rows // seqs, 2 * states * seqs, LANES), BF16)],
        scratch_shapes=[pltpu.VMEM((6 * states, 2 * states * LANES), BF16)],
        compiler_params=pltpu.CompilerParams(vmem_limit_bytes=VM),
        cost_estimate=pl.CostEstimate(flops=elements, bytes_accessed=elements, transcendentals=0),
        name="local_ends",
    )(step, mixed, rows_t, rate)


def local_starts(step, yg, wide_rows, rate, chunk):
    rows, width = step.shape
    states, seqs, _ = rate.shape
    elements = rows * width * states
    grid = rows // (chunk * seqs)
    at = lambda i: grid - 1 - i
    row_spec = pl.BlockSpec((chunk * seqs, width), lambda i: (at(i), 0))
    whole = pl.BlockSpec((states, seqs, width), lambda i: (0, 0, 0))
    return pl.pallas_call(
        functools.partial(starts_kernel, chunk),
        grid=(grid,),
        in_specs=[row_spec, row_spec, spread_spec(chunk, states, seqs, 1, at), whole],
        out_specs=whole,
        out_shape=jax.ShapeDtypeStruct(rate.shape, F32),
        compiler_params=pltpu.CompilerParams(vmem_limit_bytes=VM),
        cost_estimate=pl.CostEstimate(flops=elements, bytes_accessed=elements, transcendentals=0),
        name="local_starts",
    )(step, yg, wide_rows, rate)


def fwd_kernel(chunk, step_ref, mixed_ref, gate_ref, gg_ref, spread_ref, narrow_ref, rate_ref, skip_ref,
               hin_ref, *refs):
    state_ref, hist_ref, start_ref, gated_ref, ggrad_ref = refs[-5:]
    states, seqs, width = rate_ref.shape

    @pl.when(pl.program_id(0) == 0)
    def _():
        state_ref[...] = hin_ref[...]

    start_ref[0] = state_ref[...].astype(BF16)

    def tile_step(j, _):
        lanes = pl.ds(pl.multiple_of(j * LANES, LANES), LANES)
        h = [state_ref[n, :, lanes] for n in range(states)]
        skip = skip_ref[:, lanes]
        for tok in range(0, chunk, 2):
            pair_rows = pl.ds(tok * seqs, 2 * seqs)
            pair = mixed_ref[pair_rows, lanes].astype(F32)
            gated, ggrad = [], []
            for k in range(2):
                rows = pl.ds((tok + k) * seqs, seqs)
                s = step_ref[rows, lanes]
                m = pair[k * seqs : (k + 1) * seqs]
                x = s * m
                terms = []
                for n in range(0, states, 2):
                    for i in (n, n + 1):
                        h[i] = jnp.exp2(s * rate_ref[i, :, lanes]) * h[i] + spread_ref[tok + k, i] * x
                    both = jnp.concatenate([h[n], h[n + 1]], axis=0).astype(BF16)
                    hist_ref[tok + k, j, pl.ds(n * seqs, 2 * seqs), :] = both
                    terms.append(both * narrow_ref[tok + k, pl.ds(n * seqs, 2 * seqs), :])
                y = skip * m + halves_sum(terms)
                v = gate_ref[rows, lanes]
                sig = 1.0 / (1.0 + jnp.exp2(v * (-LOG2E)))
                gated.append(y * (v * sig))
                ggrad.append(gg_ref[rows, lanes] * y * (sig * (1.0 + v * (1.0 - sig))))
            gated_ref[pair_rows, lanes] = jnp.concatenate(gated, axis=0).astype(BF16)
            ggrad_ref[pair_rows, lanes] = jnp.concatenate(ggrad, axis=0).astype(BF16)
        for n in range(states):
            state_ref[n, :, lanes] = h[n]
        return 0

    lax.fori_loop(0, width // LANES, tile_step, 0, unroll=2)


def forward(arrays, skip, carried, filled, shapes, chunk, first, last):
    step, mixed, gate, gg, wide_rows, narrow_rows, rate = arrays
    rows, width = step.shape
    states, seqs, _ = rate.shape
    at = lambda i: first + i
    row_spec = pl.BlockSpec((chunk * seqs, width), lambda i: (at(i), 0))
    whole = pl.BlockSpec((states, seqs, width), lambda i: (0, 0, 0))
    anywhere = pl.BlockSpec(memory_space=pl.ANY)
    elements = (last - first) * chunk * seqs * width * states
    return pl.pallas_call(
        functools.partial(fwd_kernel, chunk),
        grid=(last - first,),
        in_specs=[row_spec, row_spec, row_spec, row_spec, spread_spec(chunk, states, seqs, 0, at), narrow_spec(chunk, states, seqs, 1, at), whole,
                  pl.BlockSpec((seqs, width), lambda i: (0, 0)), whole] + [anywhere] * len(filled),
        out_specs=[whole, pl.BlockSpec((chunk, width // LANES, states * seqs, LANES), lambda i: (at(i), 0, 0, 0)),
                   pl.BlockSpec((1, states, seqs, width), lambda i: (at(i), 0, 0, 0)), row_spec, row_spec],
        out_shape=[jax.ShapeDtypeStruct(*shape) for shape in shapes],
        input_output_aliases={8 + i: i for i in range(len(filled) + 1)},
        compiler_params=pltpu.CompilerParams(vmem_limit_bytes=VM),
        cost_estimate=pl.CostEstimate(flops=elements, bytes_accessed=elements, transcendentals=0),
        name="scan_forward",
    )(step, mixed, gate, gg, wide_rows, narrow_rows, rate, skip, carried, *filled)


def bwd_kernel(chunk, step_ref, mixed_ref, yg_ref, spread_ref, narrow_ref, rate_ref, skip_ref, low_ref, hist_ref, start_ref, gin_ref,
               sums_ref, pre_ref, part_ref, proj_ref, decay_ref, bias_ref, skipg_ref, state_ref, b_ref, c_ref):
    states, seqs, width = rate_ref.shape
    span = states * seqs

    @pl.when(pl.program_id(0) == 0)
    def _():
        state_ref[...] = gin_ref[...]
        decay_ref[...] = jnp.zeros_like(decay_ref)
        bias_ref[...] = jnp.zeros_like(bias_ref)
        skipg_ref[...] = jnp.zeros_like(skipg_ref)

    b_ref[...] = jnp.zeros_like(b_ref)
    c_ref[...] = jnp.zeros_like(c_ref)
    contract = (((1,), (1,)), ((), ()))

    def tile_step(j, _):
        lanes = pl.ds(pl.multiple_of(j * LANES, LANES), LANES)
        q = [state_ref[n, :, lanes] for n in range(states)]
        acc = [decay_ref[n, :, lanes] for n in range(states)]
        skip = skip_ref[:, lanes]
        bias = bias_ref[:, lanes]
        skipg = skipg_ref[:, lanes]
        for tok in range(chunk - 2, -1, -2):
            pair_rows = pl.ds(tok * seqs, 2 * seqs)
            pair = mixed_ref[pair_rows, lanes].astype(F32)
            pre, xs, packed, weights = [None, None], [None, None], [None, None], [None, None]
            for k in (1, 0):
                now = tok + k
                rows = pl.ds(now * seqs, seqs)
                s = step_ref[rows, lanes]
                y = yg_ref[rows, lanes]
                m = pair[k * seqs : (k + 1) * seqs]
                gs, along_terms, size_terms = [], [], []
                for n in range(0, states, 2):
                    if now > 0:
                        before = hist_ref[now - 1, j, pl.ds(n * seqs, 2 * seqs), :]
                    else:
                        before = jnp.concatenate([start_ref[0, n + i, :, lanes] for i in range(2)], axis=0)
                    both, moves = [], []
                    for i in (n, n + 1):
                        z = s * rate_ref[i, :, lanes]
                        g = spread_ref[now, i] * y + q[i]
                        q[i] = jnp.exp2(z) * g
                        both.append(g)
                        moves.append(q[i] * z)
                    gs.append(jnp.concatenate(both, axis=0).astype(BF16))
                    along_terms.append(gs[-1] * narrow_ref[now, pl.ds(n * seqs, 2 * seqs), :])
                    size_terms.append(jnp.concatenate(moves, axis=0).astype(BF16) * before)
                packed[k] = jnp.concatenate(gs, axis=0)
                weights[k] = size_terms
                along, size = halves_sum(along_terms), halves_sum(size_terms)
                part_ref[rows, lanes] = s * along + skip * y
                skipg = skipg + y * m
                xs[k] = s * m
                series = 1.0 - s * (1.0 / 2) * (1.0 - s * (1.0 / 3) * (1.0 - s * (1.0 / 4) * (1.0 - s * (1.0 / 5))))
                ratio = jnp.where(s < 0.1, series, (1.0 - jnp.exp2(s * (-LOG2E))) / jnp.maximum(s, 0.1))
                pre[k] = ratio * (size * (1.0 / LOG2E) + xs[k] * along)
            for n in range(0, states, 2):
                total = (weights[0][n // 2] + weights[1][n // 2]).astype(F32)
                acc[n] = acc[n] + total[:seqs]
                acc[n + 1] = acc[n + 1] + total[seqs:]
            rounded = jnp.concatenate(pre, axis=0).astype(BF16)
            pre_ref[pair_rows, lanes] = rounded
            wide = rounded.astype(F32)
            bias = bias + wide[:seqs] + wide[seqs:]
            x = jnp.concatenate(xs, axis=0).astype(BF16)
            pair_hist = jnp.concatenate([hist_ref[tok, j], hist_ref[tok + 1, j]], axis=0)
            b_ref[tok // 2] += lax.dot_general(x, jnp.concatenate(packed, axis=0), contract, preferred_element_type=F32)
            c_ref[tok // 2] += lax.dot_general(
                yg_ref[pair_rows, lanes].astype(BF16), pair_hist, contract, preferred_element_type=F32
            )
        for n in range(states):
            state_ref[n, :, lanes] = q[n]
            decay_ref[n, :, lanes] = acc[n]
        bias_ref[:, lanes] = bias
        skipg_ref[:, lanes] = skipg
        return 0

    lax.fori_loop(0, width // LANES, tile_step, 0, unroll=2)
    wide = 2 * span
    row = lax.broadcasted_iota(jnp.int32, (2 * seqs, wide), 0)
    col = lax.broadcasted_iota(jnp.int32, (2 * seqs, wide), 1)
    match = (row // seqs == col // span) & (row % seqs == col % seqs)
    b_rows = [jnp.where(match, b_ref[i], 0.0) for i in range(chunk // 2)]
    c_rows = [jnp.where(match, c_ref[i], 0.0) for i in range(chunk // 2)]
    src = lax.broadcasted_iota(jnp.int32, (2 * states, wide), 1) // seqs % states
    dst = lax.broadcasted_iota(jnp.int32, (2 * states, wide), 0)
    fold_b = (src == dst).astype(BF16)
    fold_c = (src + states == dst).astype(BF16)
    rank = low_ref.shape[0]
    proj_ref[:rank] = lax.dot_general(low_ref[...], pre_ref[...], contract, preferred_element_type=F32)
    proj_ref[rank:] = lax.dot_general(
        fold_b, jnp.concatenate(b_rows, axis=0).astype(BF16), contract, preferred_element_type=F32
    ) + lax.dot_general(fold_c, jnp.concatenate(c_rows, axis=0).astype(BF16), contract, preferred_element_type=F32)

    @pl.when(pl.program_id(0) == pl.num_programs(0) - 1)
    def _():
        sums_ref[:states] = jnp.sum(decay_ref[...], axis=1) * (1.0 / LOG2E)
        sums_ref[states : states + 1] = jnp.sum(bias_ref[...], axis=0, keepdims=True)
        sums_ref[states + 1 : states + 2] = jnp.sum(skipg_ref[...], axis=0, keepdims=True)


def backward(step, mixed, yg, wide_rows, narrow_rows, rate, skip, low_weight, hist, start, gin, chunk):
    rows, width = step.shape
    states, seqs, _ = rate.shape
    grid = rows // (chunk * seqs)
    elements = rows * width * states
    at = lambda i: grid - 1 - i
    row_spec = pl.BlockSpec((chunk * seqs, width), lambda i: (at(i), 0))
    rank = low_weight.shape[0]
    whole = pl.BlockSpec((states, seqs, width), lambda i: (0, 0, 0))
    one = pl.BlockSpec((seqs, width), lambda i: (0, 0))
    return pl.pallas_call(
        functools.partial(bwd_kernel, chunk),
        grid=(grid,),
        in_specs=[row_spec, row_spec, row_spec, spread_spec(chunk, states, seqs, 1, at),
                  narrow_spec(chunk, states, seqs, 0, at), whole, one,
                  pl.BlockSpec((rank, width), lambda i: (0, 0)),
                  pl.BlockSpec((chunk, width // LANES, states * seqs, LANES), lambda i: (at(i), 0, 0, 0)),
                  pl.BlockSpec((1, states, seqs, width), lambda i: (at(i), 0, 0, 0)), whole],
        out_specs=[pl.BlockSpec((states + 2, width), lambda i: (0, 0)), row_spec, row_spec,
                   pl.BlockSpec((rank + 2 * states, chunk * seqs), lambda i: (0, at(i)))],
        out_shape=[jax.ShapeDtypeStruct((states + 2, width), F32), jax.ShapeDtypeStruct((rows, width), BF16),
                   jax.ShapeDtypeStruct((rows, width), F32), jax.ShapeDtypeStruct((rank + 2 * states, rows), F32)],
        scratch_shapes=[pltpu.VMEM(rate.shape, F32), pltpu.VMEM((seqs, width), F32), pltpu.VMEM((seqs, width), F32),
                        pltpu.VMEM(rate.shape, F32)] + [pltpu.VMEM((chunk // 2, 2 * seqs, 2 * states * seqs), F32)] * 2,
        compiler_params=pltpu.CompilerParams(vmem_limit_bytes=VM),
        cost_estimate=pl.CostEstimate(flops=elements, bytes_accessed=elements, transcendentals=0),
        name="scan_backward",
    )(step, mixed, yg, wide_rows, narrow_rows, rate, skip, low_weight, hist, start, gin)


def conv_kernel(chunk, taps, proj_ref, weight_ref, part_ref, conv_ref, in_ref, before_ref, taps_ref,
                spread_ref, first_ref, sums_ref, grad_ref, back_ref):
    rows, width = part_ref.shape
    seqs = rows // chunk
    halo = (taps - 1) * seqs
    lead = before_ref.shape[0]
    step = pl.program_id(0)
    block = pl.num_programs(0) - 1 - step

    @pl.when(step == 0)
    def _():
        grad_ref[rows:] = jnp.zeros_like(grad_ref[rows:])
        sums_ref[...] = jnp.zeros_like(sums_ref)

    @pl.when(step > 0)
    def _():
        grad_ref[rows : rows + halo] = grad_ref[:halo]

    back_ref[...] = lax.dot_general(
        proj_ref[...], weight_ref[...], (((0,), (0,)), ((), ())), preferred_element_type=F32
    )

    def tile_step(j, _):
        lanes = pl.ds(pl.multiple_of(j * LANES, LANES), LANES)
        tap = [taps_ref[k : k + 1, lanes] for k in range(taps)]
        sums = [sums_ref[k, :, lanes] for k in range(taps + 1)]
        for tok in reversed(range(0, chunk, 2)):
            at = pl.ds(tok * seqs, 2 * seqs)
            v = conv_ref[at, lanes]
            sig = 1.0 / (1.0 + jnp.exp2(v * (-LOG2E)))
            grad = (part_ref[at, lanes] + back_ref[at, lanes]) * (sig * (1.0 + v * (1.0 - sig)))
            grad_ref[at, lanes] = grad
            given = in_ref[at, lanes].astype(F32)
            spread = jnp.zeros_like(grad)
            for k in range(taps):
                later = grad_ref[pl.ds((tok + taps - 1 - k) * seqs, 2 * seqs), lanes]
                spread = spread + tap[k] * later
                use = given * later
                sums[k] = sums[k] + use[:seqs] + use[seqs:]
            sums[taps] = sums[taps] + grad[:seqs] + grad[seqs:]
            out_at = pl.multiple_of(lead + block * rows + tok * seqs, 2 * seqs)
            spread_ref[pl.ds(out_at, 2 * seqs), lanes] = spread.astype(BF16)
        for k in range(taps + 1):
            sums_ref[k, :, lanes] = sums[k]
        return 0

    lax.fori_loop(0, width // LANES, tile_step, 0, unroll=2)

    @pl.when(block == 0)
    def _():
        first_ref[...] = grad_ref[:halo]
        given = before_ref[...].astype(F32)
        parts = [jnp.zeros((lead - halo, width), F32)]
        for tok in range(taps - 1):
            spread = jnp.zeros((seqs, width), F32)
            own = given[lead - halo + tok * seqs : lead - halo + (tok + 1) * seqs]
            for k in range(tok + 1):
                later = grad_ref[(tok - k) * seqs : (tok - k + 1) * seqs]
                spread = spread + taps_ref[k : k + 1] * later
                sums_ref[k] = sums_ref[k] + own * later
            parts.append(spread)
        spread_ref[:lead] = jnp.concatenate(parts, axis=0).astype(BF16)


def conv_back(proj_grad, weight, part, conv_out, conv_in, before, conv_taps, chunk):
    rows, width = part.shape
    taps = conv_taps.shape[0]
    columns = proj_grad.shape[0]
    seqs, lead = 8, before.shape[0]
    halo = (taps - 1) * seqs
    grid = rows // (chunk * seqs)
    at = lambda i: grid - 1 - i
    row_spec = pl.BlockSpec((chunk * seqs, width), lambda i: (at(i), 0))
    fixed = lambda *shape: pl.BlockSpec(shape, lambda i: (0,) * len(shape))
    return pl.pallas_call(
        functools.partial(conv_kernel, chunk, taps),
        grid=(grid,),
        in_specs=[pl.BlockSpec((columns, chunk * seqs), lambda i: (0, at(i))), fixed(columns, width), row_spec, row_spec, row_spec,
                  fixed(lead, width), fixed(taps, width)],
        out_specs=[fixed(rows + lead, width), fixed(halo, width), fixed(taps + 1, seqs, width)],
        out_shape=[jax.ShapeDtypeStruct((rows + lead, width), BF16), jax.ShapeDtypeStruct((halo, width), F32),
                   jax.ShapeDtypeStruct((taps + 1, seqs, width), F32)],
        scratch_shapes=[pltpu.VMEM((chunk * seqs + lead, width), F32), pltpu.VMEM((chunk * seqs, width), F32)],
        compiler_params=pltpu.CompilerParams(vmem_limit_bytes=VM),
        cost_estimate=pl.CostEstimate(flops=rows * width, bytes_accessed=rows * width, transcendentals=0),
        name="conv_backward",
    )(proj_grad, weight, part, conv_out, conv_in, before, conv_taps)


def merge_kernel(plan, messages, bits_ref, *refs):
    refs = list(refs)
    inputs = [[refs.pop(0) for _ in range(len(sizes) + 1 + (extra > 0))] for _, _, sizes, extra, *_ in plan]
    outputs = [[refs.pop(0) for _ in range(len(sizes) + (extra > 0))] for _, _, sizes, extra, *_ in plan]
    sent = [refs.pop(0) for _ in range(messages)]
    for index, (levels, dim, sizes, extra, got_at, message, sent_at) in enumerate(plan):
        bit = bits_ref[index]
        kept, got, whole = inputs[index][: len(sizes)], inputs[index][len(sizes)], inputs[index][-1]
        kept_out, whole_out, sent_out = outputs[index][: len(sizes)], outputs[index][-1], sent[message]
        after_dim = 1 << (levels - 1 - dim)
        for size, source, target in zip(sizes, kept, kept_out):
            for rest in range(1 << (levels - 1)):
                high, low = divmod(rest, after_dim)
                for side in range(2):
                    own = bit if side == 0 else 1 - bit
                    at = pl.multiple_of(((high * 2 + own) * after_dim + low) * size, 16)
                    total = source[pl.ds(at, size), :].astype(F32) + got[pl.ds(got_at + at, size), :].astype(F32)
                    if side == 0:
                        target[rest * size : (rest + 1) * size, :] = total.astype(BF16)
                    else:
                        sent_out[sent_at + rest * size : sent_at + (rest + 1) * size, :] = total.astype(BF16)
            got_at += size << levels
            sent_at += size << (levels - 1)
        if extra:
            other = got[got_at : got_at + extra, :].astype(F32) + got[got_at + extra : got_at + 2 * extra, :].astype(F32)
            total = whole[...] + other
            upper = total.astype(BF16)
            lower = (total - upper.astype(F32)).astype(BF16)
            sent_out[sent_at : sent_at + extra, :] = upper
            sent_out[sent_at + extra : sent_at + 2 * extra, :] = lower
            whole_out[...] = upper.astype(F32) + lower.astype(F32)


def product_kernel(count, core_ref, *refs):
    del core_ref
    kept_ref, sent_ref = refs[-2:]
    total = None
    for a_ref, b_ref in zip(refs[:count], refs[count : 2 * count]):
        part = lax.dot_general(a_ref[...], b_ref[...], (((1,), (1,)), ((), ())), preferred_element_type=F32)
        total = part if total is None else total + part
    side = pl.program_id(1)

    @pl.when(side == 0)
    def _():
        kept_ref[0] = total.astype(BF16)

    @pl.when(side == 1)
    def _():
        sent_ref[0] = total.astype(BF16)


def product_sides(core, share, *pairs):
    rows, columns = pairs[0][0].shape[0], pairs[0][1].shape[0]
    chips = columns // share // 2
    mine = lambda far, side, core_ref: (far * 2 + jnp.where(side == 0, core_ref[0], 1 - core_ref[0]), 0)
    out_spec = pl.BlockSpec((1, rows, share), lambda far, side, core_ref: (far, 0, 0))
    return pl.pallas_call(
        functools.partial(product_kernel, len(pairs)),
        grid_spec=pltpu.PrefetchScalarGridSpec(
            num_scalar_prefetch=1,
            grid=(chips, 2),
            in_specs=[pl.BlockSpec(a.shape, lambda far, side, core_ref: (0, 0)) for a, _ in pairs]
            + [pl.BlockSpec((share, b.shape[1]), mine) for _, b in pairs],
            out_specs=[out_spec, out_spec],
        ),
        out_shape=[jax.ShapeDtypeStruct((chips, rows, share), BF16)] * 2,
        compiler_params=pltpu.CompilerParams(vmem_limit_bytes=VM),
        cost_estimate=pl.CostEstimate(flops=1024, bytes_accessed=1024, transcendentals=0),
        name="product_sides",
    )(core.reshape(1).astype(jnp.int32), *[a for a, _ in pairs], *[b for _, b in pairs])


EPSILON = 1e-05
CONTRACT_LAST = (((1,), (1,)), ((), ()))
CONTRACT_FIRST = (((0,), (0,)), ((), ()))


def dot(a, b, dims=(((1,), (0,)), ((), ())), out=F32):
    return lax.dot_general(a, b, dims, preferred_element_type=out)


def after(value, *done):
    return lax.optimization_barrier((value, done))[0]


def swapped(value, axis, bit):
    count = lax.axis_size(axis)
    return lax.ppermute(value, axis, [(i, i ^ (1 << bit)) for i in range(count)])


def moved(value, axis, distance):
    count = lax.axis_size(axis)
    return lax.ppermute(value, axis, [(i, i + distance) for i in range(count) if 0 <= i + distance < count])


def bits_of(axis):
    return lax.axis_size(axis).bit_length() - 1


def own_bit(axis, bit):
    return (lax.axis_index(axis) >> bit) & 1


def gathered(value, axis, meanwhile=()):
    count = lax.axis_size(axis)
    parts = {0: value}
    for bit in reversed(range(bits_of(axis))):
        fresh = {mask | (1 << bit): swapped(part, axis, bit) for mask, part in parts.items()}
        if len(parts) == 1:
            fresh, meanwhile = lax.optimization_barrier((fresh, meanwhile))
        parts |= fresh
    for bit in range(bits_of(axis)):
        high = own_bit(axis, bit) == 1
        parts = {m: jnp.where(high, parts[m ^ (1 << bit)], parts[m]) for m in range(count)}
    return jnp.concatenate([parts[m] for m in range(count)], axis=-1), meanwhile


def summed(value, axis, narrow_from):
    for bit in range(bits_of(axis)):
        sent = value.astype(BF16) if bit >= narrow_from else value
        value = value + swapped(sent, axis, bit).astype(F32)
    return value


def summed_near(value, axis, narrow_from):
    if bits_of(axis) > 1 and narrow_from > 1:
        count = lax.axis_size(axis)
        near = [lax.ppermute(value, axis, [(i, i ^ mask) for i in range(count)]) for mask in (1, 2, 3)]
        value = (value + near[0]) + (near[1] + near[2])
        for bit in range(2, bits_of(axis)):
            value = value + swapped(value, axis, bit)
        return value
    return summed(value, axis, narrow_from)


def pick(value, dim, index):
    return lax.dynamic_index_in_dim(value, index, dim, keepdims=False)


class Scattered:
    def __init__(self, blocks, axis, order=None, halves=None):
        bits = bits_of(axis)
        self.axis, self.left, self.order = axis, list(range(bits)), list(order or range(bits))
        self.got, self.kept, self.sent = None, None, None
        if halves:
            self.kept, self.sent = halves
        else:
            self.value = blocks.reshape((2,) * bits + blocks.shape[1:])

    def split(self):
        if self.sent is not None:
            return
        bit = self.order[0]
        dim = len(self.left) - 1 - self.left.index(bit)
        mine = own_bit(self.axis, bit)
        self.kept, self.sent = pick(self.value, dim, mine), pick(self.value, dim, 1 - mine)

    def send(self):
        self.got = swapped(self.sent, self.axis, self.order[0])

    def add(self):
        bit = self.order.pop(0)
        self.left.remove(bit)
        value = self.kept.astype(F32) + self.got.astype(F32)
        self.value = value.astype(BF16) if self.left else value
        self.got, self.kept, self.sent = None, None, None


def start_all(sums, *values):
    sums = [s for s in sums if s.order]
    for s in sums:
        s.split()
    sent, values = lax.optimization_barrier(([s.sent for s in sums], values))
    for s, message in zip(sums, sent):
        s.sent = message
        s.send()
    return values


def end_all(sums, *values):
    sums = [s for s in sums if s.got is not None]
    got, values = lax.optimization_barrier(([s.got for s in sums], values))
    for s, message in zip(sums, got):
        s.got = message
        s.add()
    return values


def padded_rows(value, dim, multiple):
    width = -value.shape[dim] % multiple
    return jnp.pad(value, [(0, width if i == dim else 0) for i in range(value.ndim)])


def two_parts(value):
    upper = value.astype(BF16)
    return upper, (value - upper.astype(F32)).astype(BF16)


class Chain:
    def __init__(self, pieces, axis, order, whole=None, halves=None):
        bits = bits_of(axis)
        self.axis, self.order, self.left, self.whole, self.at = axis, list(order), list(range(bits)), [], 0
        if halves:
            self.sizes = [halves[1].shape[0] >> (bits - 1)]
            self.kept, self.sent = [halves[0]], halves[1]
            return
        self.sizes = [piece.shape[1] for piece in pieces]
        dim = bits - 1 - self.order[0]
        mine = own_bit(axis, self.order[0])
        halves = [piece.reshape((2,) * bits + piece.shape[1:]) for piece in pieces]
        flat = lambda value: value.reshape(-1, value.shape[-1])
        self.kept = [flat(pick(value, dim, mine)) for value in halves]
        message = [flat(pick(value, dim, 1 - mine)) for value in halves]
        if whole is not None:
            upper, lower = two_parts(whole)
            self.whole = [upper.astype(F32) + lower.astype(F32)]
            message += [upper, lower]
        self.sent = jnp.concatenate(message, axis=0) if len(message) > 1 else message[0]

    def finish(self):
        rows, values = self.at, []
        for size, kept in zip(self.sizes, self.kept):
            values.append(kept.astype(F32) + self.got[rows : rows + size].astype(F32))
            rows += size
        if self.whole:
            count = self.whole[0].shape[0]
            upper, lower = (self.got[rows + i * count : rows + (i + 1) * count].astype(F32) for i in range(2))
            values.append(self.whole[0] + (upper + lower))
        return values


def send_chains(groups, messages, *values):
    messages, values = lax.optimization_barrier((messages, values))
    for group, message in zip(groups, messages):
        got = swapped(message, group[0].axis, group[0].order[0])
        for c in group:
            c.got = got
            c.left.remove(c.order.pop(0))
    return values


def end_chains(groups, *values):
    got, values = lax.optimization_barrier(([group[0].got for group in groups], values))
    for group, message in zip(groups, got):
        for c in group:
            c.got = message
    return values


def last_of(chain):
    while chain.order:
        send_chains([[chain]], merge([[chain]]))
    return chain.finish()


def merge(groups):
    plan, operands, outputs, messages = [], [], [], []
    for number, group in enumerate(groups):
        rows = 0
        for c in group:
            levels, extra = len(c.left), c.whole[0].shape[0] if c.whole else 0
            columns = c.got.shape[1]
            plan.append((levels, levels - 1 - c.left.index(c.order[0]), tuple(c.sizes), extra, c.at, number, rows))
            operands += [*c.kept, c.got, *c.whole]
            outputs += [((size << (levels - 1), columns), BF16) for size in c.sizes] + [((extra, columns), F32)] * (extra > 0)
            c.at = rows
            rows += sum(size << (levels - 1) for size in c.sizes) + 2 * extra
        messages.append(((rows, columns), BF16))
    chains = [c for group in groups for c in group]
    bits = jnp.stack([own_bit(c.axis, c.order[0]) for c in chains]).astype(jnp.int32)
    outs = list(
        pl.pallas_call(
            functools.partial(merge_kernel, plan, len(messages)),
            in_specs=[pl.BlockSpec(memory_space=pltpu.SMEM)] + [pl.BlockSpec(memory_space=pltpu.VMEM)] * len(operands),
            out_specs=[pl.BlockSpec(memory_space=pltpu.VMEM)] * (len(outputs) + len(messages)),
            out_shape=[jax.ShapeDtypeStruct(*shape) for shape in outputs + messages],
            compiler_params=pltpu.CompilerParams(vmem_limit_bytes=VM),
            cost_estimate=pl.CostEstimate(flops=1024, bytes_accessed=1024, transcendentals=0),
            name="merge_messages",
        )(bits, *operands)
    )
    for c in chains:
        c.kept = [outs.pop(0) for _ in c.sizes]
        c.whole = [outs.pop(0) for _ in c.whole]
    return outs


def columns_by(value, axis, bit):
    count = lax.axis_size(axis)
    width = value.shape[1] // (count >> bit)
    parts = [value[:, i * width : (i + 1) * width] for i in range(count >> bit)]
    high = own_bit(axis, bit) == 1
    low, up = parts[0::2], parts[1::2]
    return [
        jnp.concatenate([jnp.where(high, b, a) for a, b in zip(one, two)], axis=1) for one, two in ((low, up), (up, low))
    ]


def finished_on_the_way(s):
    if s.got is not None:
        s.add()
    while s.order:
        s.split()
        s.send()
        s.add()
    return s.value


def entering(local, total, rate, axis, direction, fillers):
    states = rate.shape[0]
    enter, enter_sum = jnp.zeros_like(local), jnp.zeros_like(total)
    through, through_sum = local, total
    distance = 1
    filled, fillers = [], list(fillers)
    while distance < lax.axis_size(axis):
        upper = through_sum.astype(BF16)
        lower = (through_sum - upper.astype(F32)).astype(BF16)
        packet = jnp.concatenate([through.astype(BF16), upper[None], lower[None]], axis=0)
        got = moved(packet, axis, distance * direction)
        if fillers:
            out = fillers.pop(0)(packet, filled)
            got, out = lax.optimization_barrier((got, out))
            filled.append(out)
        got = got.astype(F32)
        state, step_sum = got[:states], got[states] + got[states + 1]
        enter, enter_sum = enter + jnp.exp2(rate * enter_sum) * state, enter_sum + step_sum
        through, through_sum = through + jnp.exp2(rate * through_sum) * state, through_sum + step_sum
        distance *= 2
    for filler in fillers:
        filled.append(filler(enter, filled))
    return enter, filled


def silu_slope(pre_value):
    sigmoid_value = jax.nn.sigmoid(pre_value)
    return sigmoid_value * (1.0 + pre_value * (1.0 - sigmoid_value))


def shards(
    residual_in,
    norm_gain,
    in_weight,
    conv_weight,
    conv_bias,
    proj_weight,
    step_weight,
    step_bias,
    decay_log,
    skip_gain,
    out_weight,
    out_grad,
):
    seqs, toks, share = residual_in.shape
    model = norm_gain.shape[0]
    taps, inner = conv_weight.shape
    states = decay_log.shape[0]
    rank = step_weight.shape[0]
    rows = seqs * toks
    chunk = math.gcd(toks, 16)
    chunks = toks // chunk
    seq_count = lax.axis_size("seq")
    chan_bits = bits_of("chan")
    own_in = residual_in.swapaxes(0, 1).reshape(rows, share)
    own_out_grad = out_grad.swapaxes(0, 1).reshape(rows, share)
    full_in, (conv_weights, gate_weights) = gathered(own_in, "chan", (in_weight[:, 0], in_weight[:, 1]))
    wide_in = full_in.astype(F32)
    inv_rms = lax.rsqrt(jnp.mean(wide_in * wide_in, axis=-1, keepdims=True) + EPSILON)
    gain_full = norm_gain.astype(F32)
    normed = (wide_in * inv_rms * gain_full).astype(BF16)
    conv_in = dot(normed, conv_weights, out=BF16)
    halo = (taps - 1) * seqs
    lead = halo + -halo % 16
    normed_halo = moved(normed[rows - lead :], "seq", 1)
    previous = dot(normed_halo, conv_weights, out=BF16)
    padded = jnp.concatenate([previous[lead - halo :], conv_in], axis=0).astype(F32)
    conv_taps = conv_weight.astype(F32)
    conv_out = conv_bias.astype(F32) + sum(
        conv_taps[k] * padded[k * seqs : k * seqs + rows] for k in range(taps)
    )
    mixed = jax.nn.silu(conv_out).astype(BF16)
    proj_part = dot(proj_weight, mixed, CONTRACT_LAST)
    for bit in range(chan_bits):
        received = swapped(proj_part.astype(BF16) if bit else proj_part, "chan", bit)
        if bit == chan_bits - 1:
            gate_pre = dot(after(normed, proj_part), gate_weights)
            extended_normed = jnp.concatenate([normed_halo, after(normed, gate_pre)], axis=0)
            received, gate_pre, extended_normed = lax.optimization_barrier((received, gate_pre, extended_normed))
        proj_part = proj_part + received.astype(F32)
    projected = proj_part
    step_low = projected[:rank].astype(BF16)
    step_pre = dot(step_low, step_weight, CONTRACT_FIRST) + step_bias.astype(F32)
    step = jax.nn.softplus(step_pre)
    decay_rate = -jnp.exp(decay_log)
    rate = jnp.broadcast_to((decay_rate * LOG2E)[:, None], (states, seqs, inner))
    skip = jnp.broadcast_to(skip_gain, (seqs, inner))
    local_end, wide_rows, narrow_rows = local_ends(step, mixed, projected[rank:], rate, chunk)
    step_total = jnp.sum(step.reshape(toks, seqs, inner), axis=0)
    grad_whole, _ = gathered(after(own_out_grad, gate_pre), "chan", local_end)

    def output_side(sent, _):
        gated_grad = dot(after(grad_whole, sent), out_weight)
        return gated_grad, gated_grad * jax.nn.silu(gate_pre)

    def starts_side(sent, filled):
        return local_starts(step, after(filled[0][1], sent), wide_rows, rate, chunk)

    seq_bits = list(range(bits_of("seq")))
    other_bits = [1, 0] + seq_bits[2:] if len(seq_bits) > 1 else seq_bits
    def columns_side(sent, _):
        return columns_by(after(grad_whole, sent), "seq", 0), columns_by(after(normed, sent), "seq", other_bits[0])

    enter_h, filled = entering(local_end, step_total, rate, "seq", 1, [output_side, starts_side, columns_side])
    (gated_grad, y_grad), local_start, sides = filled[:3]
    shapes = [
        (rate.shape, F32),
        ((toks, inner // LANES, states * seqs, LANES), BF16),
        ((chunks, states, seqs, inner), BF16),
        ((rows, inner), BF16),
        ((rows, inner), BF16),
    ]
    arrays = (step, mixed, gate_pre, gated_grad, wide_rows, narrow_rows, rate)
    middle = chunks // 2

    def first_side(sent, _):
        return forward(arrays, skip, after(enter_h, sent), (), shapes, chunk, 0, middle)

    def second_side(sent, filled):
        state, *done = after(filled[1], sent)
        return forward(arrays, skip, state, done, shapes, chunk, middle, chunks)

    enter_g, filled = entering(
        local_start, step_total, rate, "seq", -1, [lambda sent, _: enter_h, first_side, second_side]
    )
    _, history, starts, gated_out, gate_grad = filled[2]
    by_part = lambda value: value.reshape(seq_count, -1, value.shape[-1])
    first_product = lambda columns, value: dot(columns, value, CONTRACT_FIRST, out=BF16)
    out_sent, gate_sent = (
        first_product(columns[1], value) for columns, value in zip(sides, (gated_out, gate_grad))
    )
    out_kept, gate_kept = (
        first_product(columns[0], after(value, out_sent, gate_sent)) for columns, value in zip(sides, (gated_out, gate_grad))
    )
    out_chain = Chain(None, "seq", seq_bits, halves=(out_kept, out_sent))
    gate_chain = Chain(None, "seq", other_bits, halves=(gate_kept, gate_sent))
    apart, joint = [[out_chain], [gate_chain]], [[out_chain, gate_chain]]
    (enter_g,) = send_chains(apart, [out_sent, gate_sent], enter_g)
    enter_g = after(enter_g, out_kept, gate_kept)
    chips = (2,) * (chan_bits - 1)

    def features(*pairs):
        sides = product_sides(own_bit("chan", 0), share, *pairs)
        return tuple(side.reshape(chips + side.shape[1:]) for side in sides)

    scan_sums, pre_grad, mixed_part, proj_sum = backward(
        step, mixed, y_grad, wide_rows, narrow_rows, rate, skip, step_weight, history, starts, enter_g, chunk
    )
    pre_grad, proj_sum = end_chains(apart, pre_grad, proj_sum)
    for bit in range(chan_bits):
        received = swapped(proj_sum.astype(BF16) if bit else proj_sum, "chan", bit)
        if bit == 0:
            (received,) = send_chains(apart, merge(apart), received)
        if bit == chan_bits - 1:
            branch_sum = Scattered(None, "chan", halves=features((after(gated_out, proj_sum), out_weight)))
            received, branch_sum.kept, branch_sum.sent = lax.optimization_barrier(
                (received, branch_sum.kept, branch_sum.sent)
            )
        proj_sum = proj_sum + received.astype(F32)
    proj_grad = proj_sum.astype(BF16)
    own_spread, first_grad, conv_sums = conv_back(
        proj_grad, proj_weight, mixed_part, conv_out, conv_in, previous, conv_taps, chunk
    )
    incoming = moved(first_grad, "seq", -1)
    (own_spread,) = end_chains(apart, own_spread)
    half = inner // 2
    first_last, second_last = (
        by_part(dot(extended_normed, own_spread[:, at : at + half], CONTRACT_FIRST, out=BF16)) for at in (0, half)
    )
    first, second = Chain([first_last], "seq", seq_bits), Chain([second_last], "seq", other_bits)
    weight_message = merge(apart)
    in_window = [[first], [second], [out_chain]]
    (own_spread,) = start_all([branch_sum], own_spread)
    own_spread, incoming = send_chains(in_window, [first.sent, second.sent, weight_message[0]], own_spread, incoming)
    zeros = jnp.zeros((halo, inner), F32)
    from_after = jnp.concatenate([zeros, incoming, zeros], axis=0)
    late = sum(
        conv_taps[k] * from_after[(2 * taps - 2 - k) * seqs - halo : (2 * taps - 2 - k) * seqs] for k in range(taps)
    )
    conv_in_grad = jnp.concatenate(
        [own_spread[lead : lead + rows - halo], (own_spread[lead + rows - halo :].astype(F32) + late).astype(BF16)], axis=0
    )
    late_proj, late_pre, late_sums = after((proj_grad, pre_grad, conv_sums), own_spread)
    proj_weight_part = dot(late_proj, mixed, out=BF16)
    step_weight_part = dot(step_low, late_pre, out=BF16)
    sums = jnp.concatenate([scan_sums, jnp.sum(late_sums, axis=1)], axis=0)
    sum_rows = sums.shape[0]
    sums = padded_rows(jnp.concatenate([sums[:, :half], sums[:, half:]], axis=0), 0, 16)
    small_blocks = jnp.concatenate([by_part(proj_weight_part), by_part(step_weight_part)], axis=1)
    small_blocks = padded_rows(jnp.concatenate([small_blocks[..., :half], small_blocks[..., half:]], axis=1), 1, 16)
    third = Chain([small_blocks], "seq", seq_bits, sums)
    row_dots = jnp.sum(
        conv_in_grad.astype(F32) * conv_in.astype(F32) + gate_grad.astype(F32) * gate_pre, axis=1
    )
    last_pair = (gate_grad, after(gate_weights, third.sent, row_dots))
    normed_sum = Scattered(None, "chan", halves=features((conv_in_grad, conv_weights), last_pair))
    normed_sum.sent, normed_sum.kept, third.sent = end_chains(
        in_window, normed_sum.sent, normed_sum.kept, third.sent
    )
    row_dots, third.sent = end_all([branch_sum], row_dots, third.sent)
    groups = [[first], [second]]
    messages = merge(groups)
    (row_dots,) = start_all([normed_sum, branch_sum], row_dots)
    in_window = [*groups, [third], [gate_chain]]
    (row_dots,) = send_chains(in_window, [*messages, third.sent, weight_message[1]], row_dots)
    row_dots = row_dots + swapped(row_dots, "chan", 0)
    (row_dots,) = end_all([normed_sum], row_dots)
    (row_dots,) = start_all([normed_sum], row_dots)
    (row_dots,) = end_all([branch_sum], row_dots)
    (row_dots,) = end_chains(in_window, row_dots)
    groups = [[first], [second], [third]]
    (row_dots,) = send_chains(groups, merge(groups), row_dots)
    for bit in range(1, chan_bits):
        row_dots = row_dots + swapped(row_dots, "chan", bit)
    (row_dots,) = end_all([normed_sum], row_dots)
    normed_grad = finished_on_the_way(normed_sum)
    row_dots = row_dots[:, None]
    wide_own = own_in.astype(F32)
    own_gain = lax.dynamic_slice_in_dim(gain_full, lax.axis_index("chan") * share, share, 0)
    in_rows = (
        own_out_grad.astype(F32)
        + inv_rms * own_gain * normed_grad
        - wide_own * (inv_rms * inv_rms / model) * row_dots
    ).astype(BF16)
    in_grad = in_rows.reshape(toks, seqs, share).swapaxes(0, 1)
    gain_grad = jnp.sum(normed_grad * wide_own * inv_rms, axis=0)
    in_grad, gain_grad = end_chains(groups, in_grad, gain_grad)
    if third.order:
        (gain_grad,) = send_chains([[third]], merge([[third]]), gain_grad)
    gain_grad = summed_near(gain_grad, "seq", bits_of("seq"))
    (first_last,), (second_last,), (small, sums) = last_of(first), last_of(second), last_of(third)
    (out_weight_grad,), (gate_weight_grad,) = last_of(out_chain), last_of(gate_chain)
    last = jnp.concatenate([first_last, second_last], axis=1)
    sums = jnp.concatenate([sums[:sum_rows], sums[sum_rows : 2 * sum_rows]], axis=1)
    proj_share, step_share = proj_weight.shape[0] // seq_count, rank // seq_count
    each = proj_share + step_share
    small_of = lambda start, count: jnp.concatenate([small[start : start + count], small[each + start : each + start + count]], axis=1)
    block_rows = (own_in.astype(F32) + finished_on_the_way(branch_sum)).astype(BF16)
    block_out = block_rows.reshape(toks, seqs, share).swapaxes(0, 1)
    return (
        block_out,
        in_grad,
        gain_grad,
        jnp.stack([last, gate_weight_grad], axis=1),
        sums[states + 2 : states + 2 + taps],
        sums[states + 2 + taps],
        small_of(0, proj_share),
        small_of(proj_share, step_share),
        sums[states],
        sums[:states],
        sums[states + 1],
        out_weight_grad,
    )


def solution(mesh):
    in_specs = (
        P(None, "seq", "chan"),
        P(),
        P(None, None, "chan"),
        P(None, "chan"),
        P("chan"),
        P(None, "chan"),
        P(None, "chan"),
        P("chan"),
        P(None, "chan"),
        P("chan"),
        P(None, "chan"),
        P(None, "seq", "chan"),
    )
    out_specs = (
        P(None, "seq", "chan"),
        P(None, "seq", "chan"),
        P("chan"),
        P("seq", None, "chan"),
        P(None, "chan"),
        P("chan"),
        P("seq", "chan"),
        P("seq", "chan"),
        P("chan"),
        P(None, "chan"),
        P("chan"),
        P("seq", "chan"),
    )
    return jax.shard_map(shards, mesh=mesh, in_specs=in_specs, out_specs=out_specs, check_vma=False)
```

```python
import functools, math
import jax, jax.numpy as jnp
from jax import lax
from jax.sharding import PartitionSpec as P
from jax.experimental import pallas as pl
from jax.experimental.pallas import tpu as pltpu

LANES = 128
LOG2E = 1.4426950408889634
VM = 56 * 1024 * 1024
F32, BF16 = jnp.float32, jnp.bfloat16


def spread(rows_ref, select_ref, spread_ref, narrow_ref, chunk, count, seqs):
    left, parts = rows_ref[...], []
    for _ in range(3):
        parts.append(left.astype(BF16))
        left = left - parts[-1].astype(F32)
    stacked = jnp.concatenate(parts, axis=0)
    for col in range(0, count, 2):
        wide = lax.dot_general(
            stacked, select_ref[:, col * LANES : (col + 2) * LANES], (((0,), (0,)), ((), ())), preferred_element_type=F32
        )
        for tok in range(chunk):
            both = [wide[tok * seqs : (tok + 1) * seqs, i * LANES : (i + 1) * LANES] for i in range(2)]
            for i in range(2):
                spread_ref[tok, col + i] = both[i]
            narrow_ref[tok, pl.ds(col * seqs, 2 * seqs), :] = jnp.concatenate(both, axis=0).astype(BF16)


def ends_kernel(chunk, step_ref, mixed_ref, rows_ref, rate_ref, h_ref, spread_ref, narrow_ref, select_ref):
    states, seqs, width = rate_ref.shape

    @pl.when(pl.program_id(0) == 0)
    def _():
        h_ref[...] = jnp.zeros_like(h_ref)
        row = lax.broadcasted_iota(jnp.int32, select_ref.shape, 0)
        col = lax.broadcasted_iota(jnp.int32, select_ref.shape, 1)
        select_ref[...] = (row % (2 * states) == col // LANES).astype(BF16)

    spread(rows_ref, select_ref, spread_ref, narrow_ref, chunk, 2 * states, seqs)

    def tile_step(j, _):
        lanes = pl.ds(pl.multiple_of(j * LANES, LANES), LANES)
        h = [h_ref[n, :, lanes] for n in range(states)]
        for tok in range(0, chunk, 2):
            m = mixed_ref[pl.ds(tok * seqs, 2 * seqs), lanes].astype(F32)
            for k in range(2):
                s = step_ref[pl.ds((tok + k) * seqs, seqs), lanes]
                x = s * m[k * seqs : (k + 1) * seqs]
                for n in range(states):
                    h[n] = jnp.exp2(s * rate_ref[n, :, lanes]) * h[n] + spread_ref[tok + k, n] * x
        for n in range(states):
            h_ref[n, :, lanes] = h[n]
        return 0

    lax.fori_loop(0, width // LANES, tile_step, 0, unroll=2)


def starts_kernel(chunk, step_ref, yg_ref, spread_ref, rate_ref, q_ref):
    states, seqs, width = rate_ref.shape

    @pl.when(pl.program_id(0) == 0)
    def _():
        q_ref[...] = jnp.zeros_like(q_ref)

    def tile_step(j, _):
        lanes = pl.ds(pl.multiple_of(j * LANES, LANES), LANES)
        q = [q_ref[n, :, lanes] for n in range(states)]
        for tok in reversed(range(chunk)):
            rows = pl.ds(tok * seqs, seqs)
            s, y = step_ref[rows, lanes], yg_ref[rows, lanes]
            for n in range(states):
                q[n] = jnp.exp2(s * rate_ref[n, :, lanes]) * (q[n] + spread_ref[tok, n] * y)
        for n in range(states):
            q_ref[n, :, lanes] = q[n]
        return 0

    lax.fori_loop(0, width // LANES, tile_step, 0, unroll=2)


def spread_spec(chunk, count, seqs, part, at):
    return pl.BlockSpec((chunk, count, seqs, LANES), lambda i: (at(i), part, 0, 0))


def narrow_spec(chunk, count, seqs, part, at):
    return pl.BlockSpec((chunk, count * seqs, LANES), lambda i: (at(i), part, 0))


def halves_sum(parts):
    while len(parts) > 1:
        parts = [a + b for a, b in zip(parts[::2], parts[1::2])]
    total = parts[0].astype(F32)
    seqs = total.shape[0] // 2
    return total[:seqs] + total[seqs:]


def local_ends(step, mixed, rows_t, rate, chunk):
    rows, width = step.shape
    states, seqs, _ = rate.shape
    elements = rows * width * states
    grid = rows // (chunk * seqs)
    row_spec = pl.BlockSpec((chunk * seqs, width), lambda i: (i, 0))
    whole = pl.BlockSpec((states, seqs, width), lambda i: (0, 0, 0))
    return pl.pallas_call(
        functools.partial(ends_kernel, chunk),
        grid=(grid,),
        in_specs=[row_spec, row_spec, pl.BlockSpec((2 * states, chunk * seqs), lambda i: (0, i)), whole],
        out_specs=[whole, spread_spec(chunk, 2 * states, seqs, 0, lambda i: i), narrow_spec(chunk, 2 * states, seqs, 0, lambda i: i)],
        out_shape=[jax.ShapeDtypeStruct(rate.shape, F32), jax.ShapeDtypeStruct((rows // seqs, 2 * states, seqs, LANES), F32),
                   jax.ShapeDtypeStruct((rows // seqs, 2 * states * seqs, LANES), BF16)],
        scratch_shapes=[pltpu.VMEM((6 * states, 2 * states * LANES), BF16)],
        compiler_params=pltpu.CompilerParams(vmem_limit_bytes=VM),
        cost_estimate=pl.CostEstimate(flops=elements, bytes_accessed=elements, transcendentals=0),
        name="local_ends",
    )(step, mixed, rows_t, rate)


def local_starts(step, yg, wide_rows, rate, chunk):
    rows, width = step.shape
    states, seqs, _ = rate.shape
    elements = rows * width * states
    grid = rows // (chunk * seqs)
    at = lambda i: grid - 1 - i
    row_spec = pl.BlockSpec((chunk * seqs, width), lambda i: (at(i), 0))
    whole = pl.BlockSpec((states, seqs, width), lambda i: (0, 0, 0))
    return pl.pallas_call(
        functools.partial(starts_kernel, chunk),
        grid=(grid,),
        in_specs=[row_spec, row_spec, spread_spec(chunk, states, seqs, 1, at), whole],
        out_specs=whole,
        out_shape=jax.ShapeDtypeStruct(rate.shape, F32),
        compiler_params=pltpu.CompilerParams(vmem_limit_bytes=VM),
        cost_estimate=pl.CostEstimate(flops=elements, bytes_accessed=elements, transcendentals=0),
        name="local_starts",
    )(step, yg, wide_rows, rate)


def fwd_kernel(chunk, step_ref, mixed_ref, gate_ref, gg_ref, spread_ref, narrow_ref, rate_ref, skip_ref,
               hin_ref, *refs):
    state_ref, hist_ref, start_ref, gated_ref, ggrad_ref = refs[-5:]
    states, seqs, width = rate_ref.shape

    @pl.when(pl.program_id(0) == 0)
    def _():
        state_ref[...] = hin_ref[...]

    start_ref[0] = state_ref[...].astype(BF16)

    def tile_step(j, _):
        lanes = pl.ds(pl.multiple_of(j * LANES, LANES), LANES)
        h = [state_ref[n, :, lanes] for n in range(states)]
        skip = skip_ref[:, lanes]
        for tok in range(0, chunk, 2):
            pair_rows = pl.ds(tok * seqs, 2 * seqs)
            pair = mixed_ref[pair_rows, lanes].astype(F32)
            gated, ggrad = [], []
            for k in range(2):
                rows = pl.ds((tok + k) * seqs, seqs)
                s = step_ref[rows, lanes]
                m = pair[k * seqs : (k + 1) * seqs]
                x = s * m
                terms = []
                for n in range(0, states, 2):
                    for i in (n, n + 1):
                        h[i] = jnp.exp2(s * rate_ref[i, :, lanes]) * h[i] + spread_ref[tok + k, i] * x
                    both = jnp.concatenate([h[n], h[n + 1]], axis=0).astype(BF16)
                    hist_ref[tok + k, j, pl.ds(n * seqs, 2 * seqs), :] = both
                    terms.append(both * narrow_ref[tok + k, pl.ds(n * seqs, 2 * seqs), :])
                y = skip * m + halves_sum(terms)
                v = gate_ref[rows, lanes]
                sig = 1.0 / (1.0 + jnp.exp2(v * (-LOG2E)))
                gated.append(y * (v * sig))
                ggrad.append(gg_ref[rows, lanes] * y * (sig * (1.0 + v * (1.0 - sig))))
            gated_ref[pair_rows, lanes] = jnp.concatenate(gated, axis=0).astype(BF16)
            ggrad_ref[pair_rows, lanes] = jnp.concatenate(ggrad, axis=0).astype(BF16)
        for n in range(states):
            state_ref[n, :, lanes] = h[n]
        return 0

    lax.fori_loop(0, width // LANES, tile_step, 0, unroll=2)


def forward(arrays, skip, carried, filled, shapes, chunk, first, last):
    step, mixed, gate, gg, wide_rows, narrow_rows, rate = arrays
    rows, width = step.shape
    states, seqs, _ = rate.shape
    at = lambda i: first + i
    row_spec = pl.BlockSpec((chunk * seqs, width), lambda i: (at(i), 0))
    whole = pl.BlockSpec((states, seqs, width), lambda i: (0, 0, 0))
    anywhere = pl.BlockSpec(memory_space=pl.ANY)
    elements = (last - first) * chunk * seqs * width * states
    return pl.pallas_call(
        functools.partial(fwd_kernel, chunk),
        grid=(last - first,),
        in_specs=[row_spec, row_spec, row_spec, row_spec, spread_spec(chunk, states, seqs, 0, at), narrow_spec(chunk, states, seqs, 1, at), whole,
                  pl.BlockSpec((seqs, width), lambda i: (0, 0)), whole] + [anywhere] * len(filled),
        out_specs=[whole, pl.BlockSpec((chunk, width // LANES, states * seqs, LANES), lambda i: (at(i), 0, 0, 0)),
                   pl.BlockSpec((1, states, seqs, width), lambda i: (at(i), 0, 0, 0)), row_spec, row_spec],
        out_shape=[jax.ShapeDtypeStruct(*shape) for shape in shapes],
        input_output_aliases={8 + i: i for i in range(len(filled) + 1)},
        compiler_params=pltpu.CompilerParams(vmem_limit_bytes=VM),
        cost_estimate=pl.CostEstimate(flops=elements, bytes_accessed=elements, transcendentals=0),
        name="scan_forward",
    )(step, mixed, gate, gg, wide_rows, narrow_rows, rate, skip, carried, *filled)


def bwd_kernel(chunk, step_ref, mixed_ref, yg_ref, spread_ref, narrow_ref, rate_ref, skip_ref, low_ref, hist_ref, start_ref, gin_ref,
               sums_ref, pre_ref, part_ref, proj_ref, decay_ref, bias_ref, skipg_ref, state_ref, b_ref, c_ref):
    states, seqs, width = rate_ref.shape
    span = states * seqs

    @pl.when(pl.program_id(0) == 0)
    def _():
        state_ref[...] = gin_ref[...]
        decay_ref[...] = jnp.zeros_like(decay_ref)
        bias_ref[...] = jnp.zeros_like(bias_ref)
        skipg_ref[...] = jnp.zeros_like(skipg_ref)

    b_ref[...] = jnp.zeros_like(b_ref)
    c_ref[...] = jnp.zeros_like(c_ref)
    contract = (((1,), (1,)), ((), ()))

    def tile_step(j, _):
        lanes = pl.ds(pl.multiple_of(j * LANES, LANES), LANES)
        q = [state_ref[n, :, lanes] for n in range(states)]
        acc = [decay_ref[n, :, lanes] for n in range(states)]
        skip = skip_ref[:, lanes]
        bias = bias_ref[:, lanes]
        skipg = skipg_ref[:, lanes]
        for tok in range(chunk - 2, -1, -2):
            pair_rows = pl.ds(tok * seqs, 2 * seqs)
            pair = mixed_ref[pair_rows, lanes].astype(F32)
            pre, xs, packed, weights = [None, None], [None, None], [None, None], [None, None]
            for k in (1, 0):
                now = tok + k
                rows = pl.ds(now * seqs, seqs)
                s = step_ref[rows, lanes]
                y = yg_ref[rows, lanes]
                m = pair[k * seqs : (k + 1) * seqs]
                gs, along_terms, size_terms = [], [], []
                for n in range(0, states, 2):
                    if now > 0:
                        before = hist_ref[now - 1, j, pl.ds(n * seqs, 2 * seqs), :]
                    else:
                        before = jnp.concatenate([start_ref[0, n + i, :, lanes] for i in range(2)], axis=0)
                    both, moves = [], []
                    for i in (n, n + 1):
                        z = s * rate_ref[i, :, lanes]
                        g = spread_ref[now, i] * y + q[i]
                        q[i] = jnp.exp2(z) * g
                        both.append(g)
                        moves.append(q[i] * z)
                    gs.append(jnp.concatenate(both, axis=0).astype(BF16))
                    along_terms.append(gs[-1] * narrow_ref[now, pl.ds(n * seqs, 2 * seqs), :])
                    size_terms.append(jnp.concatenate(moves, axis=0).astype(BF16) * before)
                packed[k] = jnp.concatenate(gs, axis=0)
                weights[k] = size_terms
                along, size = halves_sum(along_terms), halves_sum(size_terms)
                part_ref[rows, lanes] = s * along + skip * y
                skipg = skipg + y * m
                xs[k] = s * m
                series = 1.0 - s * (1.0 / 2) * (1.0 - s * (1.0 / 3) * (1.0 - s * (1.0 / 4) * (1.0 - s * (1.0 / 5))))
                ratio = jnp.where(s < 0.1, series, (1.0 - jnp.exp2(s * (-LOG2E))) / jnp.maximum(s, 0.1))
                pre[k] = ratio * (size * (1.0 / LOG2E) + xs[k] * along)
            for n in range(0, states, 2):
                total = (weights[0][n // 2] + weights[1][n // 2]).astype(F32)
                acc[n] = acc[n] + total[:seqs]
                acc[n + 1] = acc[n + 1] + total[seqs:]
            rounded = jnp.concatenate(pre, axis=0).astype(BF16)
            pre_ref[pair_rows, lanes] = rounded
            wide = rounded.astype(F32)
            bias = bias + wide[:seqs] + wide[seqs:]
            x = jnp.concatenate(xs, axis=0).astype(BF16)
            pair_hist = jnp.concatenate([hist_ref[tok, j], hist_ref[tok + 1, j]], axis=0)
            b_ref[tok // 2] += lax.dot_general(x, jnp.concatenate(packed, axis=0), contract, preferred_element_type=F32)
            c_ref[tok // 2] += lax.dot_general(
                yg_ref[pair_rows, lanes].astype(BF16), pair_hist, contract, preferred_element_type=F32
            )
        for n in range(states):
            state_ref[n, :, lanes] = q[n]
            decay_ref[n, :, lanes] = acc[n]
        bias_ref[:, lanes] = bias
        skipg_ref[:, lanes] = skipg
        return 0

    lax.fori_loop(0, width // LANES, tile_step, 0, unroll=2)
    wide = 2 * span
    row = lax.broadcasted_iota(jnp.int32, (2 * seqs, wide), 0)
    col = lax.broadcasted_iota(jnp.int32, (2 * seqs, wide), 1)
    match = (row // seqs == col // span) & (row % seqs == col % seqs)
    b_rows = [jnp.where(match, b_ref[i], 0.0) for i in range(chunk // 2)]
    c_rows = [jnp.where(match, c_ref[i], 0.0) for i in range(chunk // 2)]
    src = lax.broadcasted_iota(jnp.int32, (2 * states, wide), 1) // seqs % states
    dst = lax.broadcasted_iota(jnp.int32, (2 * states, wide), 0)
    fold_b = (src == dst).astype(BF16)
    fold_c = (src + states == dst).astype(BF16)
    rank = low_ref.shape[0]
    proj_ref[:rank] = lax.dot_general(low_ref[...], pre_ref[...], contract, preferred_element_type=F32)
    proj_ref[rank:] = lax.dot_general(
        fold_b, jnp.concatenate(b_rows, axis=0).astype(BF16), contract, preferred_element_type=F32
    ) + lax.dot_general(fold_c, jnp.concatenate(c_rows, axis=0).astype(BF16), contract, preferred_element_type=F32)

    @pl.when(pl.program_id(0) == pl.num_programs(0) - 1)
    def _():
        sums_ref[:states] = jnp.sum(decay_ref[...], axis=1) * (1.0 / LOG2E)
        sums_ref[states : states + 1] = jnp.sum(bias_ref[...], axis=0, keepdims=True)
        sums_ref[states + 1 : states + 2] = jnp.sum(skipg_ref[...], axis=0, keepdims=True)


def backward(step, mixed, yg, wide_rows, narrow_rows, rate, skip, low_weight, hist, start, gin, chunk):
    rows, width = step.shape
    states, seqs, _ = rate.shape
    grid = rows // (chunk * seqs)
    elements = rows * width * states
    at = lambda i: grid - 1 - i
    row_spec = pl.BlockSpec((chunk * seqs, width), lambda i: (at(i), 0))
    rank = low_weight.shape[0]
    whole = pl.BlockSpec((states, seqs, width), lambda i: (0, 0, 0))
    one = pl.BlockSpec((seqs, width), lambda i: (0, 0))
    return pl.pallas_call(
        functools.partial(bwd_kernel, chunk),
        grid=(grid,),
        in_specs=[row_spec, row_spec, row_spec, spread_spec(chunk, states, seqs, 1, at),
                  narrow_spec(chunk, states, seqs, 0, at), whole, one,
                  pl.BlockSpec((rank, width), lambda i: (0, 0)),
                  pl.BlockSpec((chunk, width // LANES, states * seqs, LANES), lambda i: (at(i), 0, 0, 0)),
                  pl.BlockSpec((1, states, seqs, width), lambda i: (at(i), 0, 0, 0)), whole],
        out_specs=[pl.BlockSpec((states + 2, width), lambda i: (0, 0)), row_spec, row_spec,
                   pl.BlockSpec((rank + 2 * states, chunk * seqs), lambda i: (0, at(i)))],
        out_shape=[jax.ShapeDtypeStruct((states + 2, width), F32), jax.ShapeDtypeStruct((rows, width), BF16),
                   jax.ShapeDtypeStruct((rows, width), F32), jax.ShapeDtypeStruct((rank + 2 * states, rows), F32)],
        scratch_shapes=[pltpu.VMEM(rate.shape, F32), pltpu.VMEM((seqs, width), F32), pltpu.VMEM((seqs, width), F32),
                        pltpu.VMEM(rate.shape, F32)] + [pltpu.VMEM((chunk // 2, 2 * seqs, 2 * states * seqs), F32)] * 2,
        compiler_params=pltpu.CompilerParams(vmem_limit_bytes=VM),
        cost_estimate=pl.CostEstimate(flops=elements, bytes_accessed=elements, transcendentals=0),
        name="scan_backward",
    )(step, mixed, yg, wide_rows, narrow_rows, rate, skip, low_weight, hist, start, gin)


def conv_kernel(chunk, taps, proj_ref, weight_ref, part_ref, conv_ref, in_ref, before_ref, taps_ref,
                spread_ref, first_ref, sums_ref, grad_ref, back_ref):
    rows, width = part_ref.shape
    seqs = rows // chunk
    halo = (taps - 1) * seqs
    lead = before_ref.shape[0]
    step = pl.program_id(0)
    block = pl.num_programs(0) - 1 - step

    @pl.when(step == 0)
    def _():
        grad_ref[rows:] = jnp.zeros_like(grad_ref[rows:])
        sums_ref[...] = jnp.zeros_like(sums_ref)

    @pl.when(step > 0)
    def _():
        grad_ref[rows : rows + halo] = grad_ref[:halo]

    back_ref[...] = lax.dot_general(
        proj_ref[...], weight_ref[...], (((0,), (0,)), ((), ())), preferred_element_type=F32
    )

    def tile_step(j, _):
        lanes = pl.ds(pl.multiple_of(j * LANES, LANES), LANES)
        tap = [taps_ref[k : k + 1, lanes] for k in range(taps)]
        sums = [sums_ref[k, :, lanes] for k in range(taps + 1)]
        for tok in reversed(range(0, chunk, 2)):
            at = pl.ds(tok * seqs, 2 * seqs)
            v = conv_ref[at, lanes]
            sig = 1.0 / (1.0 + jnp.exp2(v * (-LOG2E)))
            grad = (part_ref[at, lanes] + back_ref[at, lanes]) * (sig * (1.0 + v * (1.0 - sig)))
            grad_ref[at, lanes] = grad
            given = in_ref[at, lanes].astype(F32)
            spread = jnp.zeros_like(grad)
            for k in range(taps):
                later = grad_ref[pl.ds((tok + taps - 1 - k) * seqs, 2 * seqs), lanes]
                spread = spread + tap[k] * later
                use = given * later
                sums[k] = sums[k] + use[:seqs] + use[seqs:]
            sums[taps] = sums[taps] + grad[:seqs] + grad[seqs:]
            out_at = pl.multiple_of(lead + block * rows + tok * seqs, 2 * seqs)
            spread_ref[pl.ds(out_at, 2 * seqs), lanes] = spread.astype(BF16)
        for k in range(taps + 1):
            sums_ref[k, :, lanes] = sums[k]
        return 0

    lax.fori_loop(0, width // LANES, tile_step, 0, unroll=2)

    @pl.when(block == 0)
    def _():
        first_ref[...] = grad_ref[:halo]
        given = before_ref[...].astype(F32)
        parts = [jnp.zeros((lead - halo, width), F32)]
        for tok in range(taps - 1):
            spread = jnp.zeros((seqs, width), F32)
            own = given[lead - halo + tok * seqs : lead - halo + (tok + 1) * seqs]
            for k in range(tok + 1):
                later = grad_ref[(tok - k) * seqs : (tok - k + 1) * seqs]
                spread = spread + taps_ref[k : k + 1] * later
                sums_ref[k] = sums_ref[k] + own * later
            parts.append(spread)
        spread_ref[:lead] = jnp.concatenate(parts, axis=0).astype(BF16)


def conv_back(proj_grad, weight, part, conv_out, conv_in, before, conv_taps, chunk):
    rows, width = part.shape
    taps = conv_taps.shape[0]
    columns = proj_grad.shape[0]
    seqs, lead = 8, before.shape[0]
    halo = (taps - 1) * seqs
    grid = rows // (chunk * seqs)
    at = lambda i: grid - 1 - i
    row_spec = pl.BlockSpec((chunk * seqs, width), lambda i: (at(i), 0))
    fixed = lambda *shape: pl.BlockSpec(shape, lambda i: (0,) * len(shape))
    return pl.pallas_call(
        functools.partial(conv_kernel, chunk, taps),
        grid=(grid,),
        in_specs=[pl.BlockSpec((columns, chunk * seqs), lambda i: (0, at(i))), fixed(columns, width), row_spec, row_spec, row_spec,
                  fixed(lead, width), fixed(taps, width)],
        out_specs=[fixed(rows + lead, width), fixed(halo, width), fixed(taps + 1, seqs, width)],
        out_shape=[jax.ShapeDtypeStruct((rows + lead, width), BF16), jax.ShapeDtypeStruct((halo, width), F32),
                   jax.ShapeDtypeStruct((taps + 1, seqs, width), F32)],
        scratch_shapes=[pltpu.VMEM((chunk * seqs + lead, width), F32), pltpu.VMEM((chunk * seqs, width), F32)],
        compiler_params=pltpu.CompilerParams(vmem_limit_bytes=VM),
        cost_estimate=pl.CostEstimate(flops=rows * width, bytes_accessed=rows * width, transcendentals=0),
        name="conv_backward",
    )(proj_grad, weight, part, conv_out, conv_in, before, conv_taps)


def merge_kernel(plan, messages, bits_ref, *refs):
    refs = list(refs)
    inputs = [[refs.pop(0) for _ in range(len(sizes) + 1 + (extra > 0))] for _, _, sizes, extra, *_ in plan]
    outputs = [[refs.pop(0) for _ in range(len(sizes) + (extra > 0))] for _, _, sizes, extra, *_ in plan]
    sent = [refs.pop(0) for _ in range(messages)]
    for index, (levels, dim, sizes, extra, got_at, message, sent_at) in enumerate(plan):
        bit = bits_ref[index]
        kept, got, whole = inputs[index][: len(sizes)], inputs[index][len(sizes)], inputs[index][-1]
        kept_out, whole_out, sent_out = outputs[index][: len(sizes)], outputs[index][-1], sent[message]
        after_dim = 1 << (levels - 1 - dim)
        for size, source, target in zip(sizes, kept, kept_out):
            for rest in range(1 << (levels - 1)):
                high, low = divmod(rest, after_dim)
                for side in range(2):
                    own = bit if side == 0 else 1 - bit
                    at = pl.multiple_of(((high * 2 + own) * after_dim + low) * size, 16)
                    total = source[pl.ds(at, size), :].astype(F32) + got[pl.ds(got_at + at, size), :].astype(F32)
                    if side == 0:
                        target[rest * size : (rest + 1) * size, :] = total.astype(BF16)
                    else:
                        sent_out[sent_at + rest * size : sent_at + (rest + 1) * size, :] = total.astype(BF16)
            got_at += size << levels
            sent_at += size << (levels - 1)
        if extra:
            other = got[got_at : got_at + extra, :].astype(F32) + got[got_at + extra : got_at + 2 * extra, :].astype(F32)
            total = whole[...] + other
            upper = total.astype(BF16)
            lower = (total - upper.astype(F32)).astype(BF16)
            sent_out[sent_at : sent_at + extra, :] = upper
            sent_out[sent_at + extra : sent_at + 2 * extra, :] = lower
            whole_out[...] = upper.astype(F32) + lower.astype(F32)


def product_kernel(count, core_ref, *refs):
    del core_ref
    kept_ref, sent_ref = refs[-2:]
    total = None
    for a_ref, b_ref in zip(refs[:count], refs[count : 2 * count]):
        part = lax.dot_general(a_ref[...], b_ref[...], (((1,), (1,)), ((), ())), preferred_element_type=F32)
        total = part if total is None else total + part
    side = pl.program_id(1)

    @pl.when(side == 0)
    def _():
        kept_ref[0] = total.astype(BF16)

    @pl.when(side == 1)
    def _():
        sent_ref[0] = total.astype(BF16)


def product_sides(core, share, *pairs):
    rows, columns = pairs[0][0].shape[0], pairs[0][1].shape[0]
    chips = columns // share // 2
    mine = lambda far, side, core_ref: (far * 2 + jnp.where(side == 0, core_ref[0], 1 - core_ref[0]), 0)
    out_spec = pl.BlockSpec((1, rows, share), lambda far, side, core_ref: (far, 0, 0))
    return pl.pallas_call(
        functools.partial(product_kernel, len(pairs)),
        grid_spec=pltpu.PrefetchScalarGridSpec(
            num_scalar_prefetch=1,
            grid=(chips, 2),
            in_specs=[pl.BlockSpec(a.shape, lambda far, side, core_ref: (0, 0)) for a, _ in pairs]
            + [pl.BlockSpec((share, b.shape[1]), mine) for _, b in pairs],
            out_specs=[out_spec, out_spec],
        ),
        out_shape=[jax.ShapeDtypeStruct((chips, rows, share), BF16)] * 2,
        compiler_params=pltpu.CompilerParams(vmem_limit_bytes=VM),
        cost_estimate=pl.CostEstimate(flops=1024, bytes_accessed=1024, transcendentals=0),
        name="product_sides",
    )(core.reshape(1).astype(jnp.int32), *[a for a, _ in pairs], *[b for _, b in pairs])


EPSILON = 1e-05
CONTRACT_LAST = (((1,), (1,)), ((), ()))
CONTRACT_FIRST = (((0,), (0,)), ((), ()))


def dot(a, b, dims=(((1,), (0,)), ((), ())), out=F32):
    return lax.dot_general(a, b, dims, preferred_element_type=out)


def after(value, *done):
    return lax.optimization_barrier((value, done))[0]


def swapped(value, axis, bit):
    count = lax.axis_size(axis)
    return lax.ppermute(value, axis, [(i, i ^ (1 << bit)) for i in range(count)])


def moved(value, axis, distance):
    count = lax.axis_size(axis)
    return lax.ppermute(value, axis, [(i, i + distance) for i in range(count) if 0 <= i + distance < count])


def bits_of(axis):
    return lax.axis_size(axis).bit_length() - 1


def own_bit(axis, bit):
    return (lax.axis_index(axis) >> bit) & 1


def gathered(value, axis, meanwhile=()):
    count = lax.axis_size(axis)
    parts = {0: value}
    for bit in reversed(range(bits_of(axis))):
        fresh = {mask | (1 << bit): swapped(part, axis, bit) for mask, part in parts.items()}
        if len(parts) == 1:
            fresh, meanwhile = lax.optimization_barrier((fresh, meanwhile))
        parts |= fresh
    for bit in range(bits_of(axis)):
        high = own_bit(axis, bit) == 1
        parts = {m: jnp.where(high, parts[m ^ (1 << bit)], parts[m]) for m in range(count)}
    return jnp.concatenate([parts[m] for m in range(count)], axis=-1), meanwhile


def summed(value, axis, narrow_from):
    for bit in range(bits_of(axis)):
        sent = value.astype(BF16) if bit >= narrow_from else value
        value = value + swapped(sent, axis, bit).astype(F32)
    return value


def summed_near(value, axis, narrow_from):
    if bits_of(axis) > 1 and narrow_from > 1:
        count = lax.axis_size(axis)
        near = [lax.ppermute(value, axis, [(i, i ^ mask) for i in range(count)]) for mask in (1, 2, 3)]
        value = (value + near[0]) + (near[1] + near[2])
        for bit in range(2, bits_of(axis)):
            value = value + swapped(value, axis, bit)
        return value
    return summed(value, axis, narrow_from)


def pick(value, dim, index):
    return lax.dynamic_index_in_dim(value, index, dim, keepdims=False)


class Scattered:
    def __init__(self, blocks, axis, order=None, halves=None):
        bits = bits_of(axis)
        self.axis, self.left, self.order = axis, list(range(bits)), list(order or range(bits))
        self.got, self.kept, self.sent = None, None, None
        if halves:
            self.kept, self.sent = halves
        else:
            self.value = blocks.reshape((2,) * bits + blocks.shape[1:])

    def split(self):
        if self.sent is not None:
            return
        bit = self.order[0]
        dim = len(self.left) - 1 - self.left.index(bit)
        mine = own_bit(self.axis, bit)
        self.kept, self.sent = pick(self.value, dim, mine), pick(self.value, dim, 1 - mine)

    def send(self):
        self.got = swapped(self.sent, self.axis, self.order[0])

    def add(self):
        bit = self.order.pop(0)
        self.left.remove(bit)
        value = self.kept.astype(F32) + self.got.astype(F32)
        self.value = value.astype(BF16) if self.left else value
        self.got, self.kept, self.sent = None, None, None


def start_all(sums, *values):
    sums = [s for s in sums if s.order]
    for s in sums:
        s.split()
    sent, values = lax.optimization_barrier(([s.sent for s in sums], values))
    for s, message in zip(sums, sent):
        s.sent = message
        s.send()
    return values


def end_all(sums, *values):
    sums = [s for s in sums if s.got is not None]
    got, values = lax.optimization_barrier(([s.got for s in sums], values))
    for s, message in zip(sums, got):
        s.got = message
        s.add()
    return values


def padded_rows(value, dim, multiple):
    width = -value.shape[dim] % multiple
    return jnp.pad(value, [(0, width if i == dim else 0) for i in range(value.ndim)])


def two_parts(value):
    upper = value.astype(BF16)
    return upper, (value - upper.astype(F32)).astype(BF16)


class Chain:
    def __init__(self, pieces, axis, order, whole=None, halves=None):
        bits = bits_of(axis)
        self.axis, self.order, self.left, self.whole, self.at = axis, list(order), list(range(bits)), [], 0
        if halves:
            self.sizes = [halves[1].shape[0] >> (bits - 1)]
            self.kept, self.sent = [halves[0]], halves[1]
            return
        self.sizes = [piece.shape[1] for piece in pieces]
        dim = bits - 1 - self.order[0]
        mine = own_bit(axis, self.order[0])
        halves = [piece.reshape((2,) * bits + piece.shape[1:]) for piece in pieces]
        flat = lambda value: value.reshape(-1, value.shape[-1])
        self.kept = [flat(pick(value, dim, mine)) for value in halves]
        message = [flat(pick(value, dim, 1 - mine)) for value in halves]
        if whole is not None:
            upper, lower = two_parts(whole)
            self.whole = [upper.astype(F32) + lower.astype(F32)]
            message += [upper, lower]
        self.sent = jnp.concatenate(message, axis=0) if len(message) > 1 else message[0]

    def finish(self):
        rows, values = self.at, []
        for size, kept in zip(self.sizes, self.kept):
            values.append(kept.astype(F32) + self.got[rows : rows + size].astype(F32))
            rows += size
        if self.whole:
            count = self.whole[0].shape[0]
            upper, lower = (self.got[rows + i * count : rows + (i + 1) * count].astype(F32) for i in range(2))
            values.append(self.whole[0] + (upper + lower))
        return values


def send_chains(groups, messages, *values):
    messages, values = lax.optimization_barrier((messages, values))
    for group, message in zip(groups, messages):
        got = swapped(message, group[0].axis, group[0].order[0])
        for c in group:
            c.got = got
            c.left.remove(c.order.pop(0))
    return values


def end_chains(groups, *values):
    got, values = lax.optimization_barrier(([group[0].got for group in groups], values))
    for group, message in zip(groups, got):
        for c in group:
            c.got = message
    return values


def last_of(chain):
    while chain.order:
        send_chains([[chain]], merge([[chain]]))
    return chain.finish()


def merge(groups):
    plan, operands, outputs, messages = [], [], [], []
    for number, group in enumerate(groups):
        rows = 0
        for c in group:
            levels, extra = len(c.left), c.whole[0].shape[0] if c.whole else 0
            columns = c.got.shape[1]
            plan.append((levels, levels - 1 - c.left.index(c.order[0]), tuple(c.sizes), extra, c.at, number, rows))
            operands += [*c.kept, c.got, *c.whole]
            outputs += [((size << (levels - 1), columns), BF16) for size in c.sizes] + [((extra, columns), F32)] * (extra > 0)
            c.at = rows
            rows += sum(size << (levels - 1) for size in c.sizes) + 2 * extra
        messages.append(((rows, columns), BF16))
    chains = [c for group in groups for c in group]
    bits = jnp.stack([own_bit(c.axis, c.order[0]) for c in chains]).astype(jnp.int32)
    outs = list(
        pl.pallas_call(
            functools.partial(merge_kernel, plan, len(messages)),
            in_specs=[pl.BlockSpec(memory_space=pltpu.SMEM)] + [pl.BlockSpec(memory_space=pltpu.VMEM)] * len(operands),
            out_specs=[pl.BlockSpec(memory_space=pltpu.VMEM)] * (len(outputs) + len(messages)),
            out_shape=[jax.ShapeDtypeStruct(*shape) for shape in outputs + messages],
            compiler_params=pltpu.CompilerParams(vmem_limit_bytes=VM),
            cost_estimate=pl.CostEstimate(flops=1024, bytes_accessed=1024, transcendentals=0),
            name="merge_messages",
        )(bits, *operands)
    )
    for c in chains:
        c.kept = [outs.pop(0) for _ in c.sizes]
        c.whole = [outs.pop(0) for _ in c.whole]
    return outs


def columns_by(value, axis, bit):
    count = lax.axis_size(axis)
    width = value.shape[1] // (count >> bit)
    parts = [value[:, i * width : (i + 1) * width] for i in range(count >> bit)]
    high = own_bit(axis, bit) == 1
    low, up = parts[0::2], parts[1::2]
    return [
        jnp.concatenate([jnp.where(high, b, a) for a, b in zip(one, two)], axis=1) for one, two in ((low, up), (up, low))
    ]


def finished_on_the_way(s):
    if s.got is not None:
        s.add()
    while s.order:
        s.split()
        s.send()
        s.add()
    return s.value


def entering(local, total, rate, axis, direction, fillers):
    states = rate.shape[0]
    enter, enter_sum = jnp.zeros_like(local), jnp.zeros_like(total)
    through, through_sum = local, total
    distance = 1
    filled, fillers = [], list(fillers)
    while distance < lax.axis_size(axis):
        upper = through_sum.astype(BF16)
        lower = (through_sum - upper.astype(F32)).astype(BF16)
        packet = jnp.concatenate([through.astype(BF16), upper[None], lower[None]], axis=0)
        got = moved(packet, axis, distance * direction)
        if fillers:
            out = fillers.pop(0)(packet, filled)
            got, out = lax.optimization_barrier((got, out))
            filled.append(out)
        got = got.astype(F32)
        state, step_sum = got[:states], got[states] + got[states + 1]
        enter, enter_sum = enter + jnp.exp2(rate * enter_sum) * state, enter_sum + step_sum
        through, through_sum = through + jnp.exp2(rate * through_sum) * state, through_sum + step_sum
        distance *= 2
    for filler in fillers:
        filled.append(filler(enter, filled))
    return enter, filled


def silu_slope(pre_value):
    sigmoid_value = jax.nn.sigmoid(pre_value)
    return sigmoid_value * (1.0 + pre_value * (1.0 - sigmoid_value))


def shards(
    residual_in,
    norm_gain,
    in_weight,
    conv_weight,
    conv_bias,
    proj_weight,
    step_weight,
    step_bias,
    decay_log,
    skip_gain,
    out_weight,
    out_grad,
):
    seqs, toks, share = residual_in.shape
    model = norm_gain.shape[0]
    taps, inner = conv_weight.shape
    states = decay_log.shape[0]
    rank = step_weight.shape[0]
    rows = seqs * toks
    chunk = math.gcd(toks, 16)
    chunks = toks // chunk
    seq_count = lax.axis_size("seq")
    chan_bits = bits_of("chan")
    own_in = residual_in.swapaxes(0, 1).reshape(rows, share)
    own_out_grad = out_grad.swapaxes(0, 1).reshape(rows, share)
    full_in, (conv_weights, gate_weights) = gathered(own_in, "chan", (in_weight[:, 0], in_weight[:, 1]))
    wide_in = full_in.astype(F32)
    inv_rms = lax.rsqrt(jnp.mean(wide_in * wide_in, axis=-1, keepdims=True) + EPSILON)
    gain_full = norm_gain.astype(F32)
    normed = (wide_in * inv_rms * gain_full).astype(BF16)
    conv_in = dot(normed, conv_weights, out=BF16)
    halo = (taps - 1) * seqs
    lead = halo + -halo % 16
    normed_halo = moved(normed[rows - lead :], "seq", 1)
    previous = dot(normed_halo, conv_weights, out=BF16)
    padded = jnp.concatenate([previous[lead - halo :], conv_in], axis=0).astype(F32)
    conv_taps = conv_weight.astype(F32)
    conv_out = conv_bias.astype(F32) + sum(
        conv_taps[k] * padded[k * seqs : k * seqs + rows] for k in range(taps)
    )
    mixed = jax.nn.silu(conv_out).astype(BF16)
    proj_part = dot(proj_weight, mixed, CONTRACT_LAST)
    for bit in range(chan_bits):
        received = swapped(proj_part.astype(BF16) if bit else proj_part, "chan", bit)
        if bit == chan_bits - 1:
            extended_normed = jnp.concatenate([normed_halo, after(normed, proj_part)], axis=0)
            gate_pre = dot(after(normed, extended_normed), gate_weights)
            received, gate_pre = lax.optimization_barrier((received, gate_pre))
        proj_part = proj_part + received.astype(F32)
    projected = proj_part
    step_low = projected[:rank].astype(BF16)
    step_pre = dot(step_low, step_weight, CONTRACT_FIRST) + step_bias.astype(F32)
    step = jax.nn.softplus(step_pre)
    decay_rate = -jnp.exp(decay_log)
    rate = jnp.broadcast_to((decay_rate * LOG2E)[:, None], (states, seqs, inner))
    skip = jnp.broadcast_to(skip_gain, (seqs, inner))
    local_end, wide_rows, narrow_rows = local_ends(step, mixed, projected[rank:], rate, chunk)
    step_total = jnp.sum(step.reshape(toks, seqs, inner), axis=0)
    grad_whole, _ = gathered(after(own_out_grad, gate_pre), "chan", local_end)

    def output_side(sent, _):
        gated_grad = dot(after(grad_whole, sent), out_weight)
        return gated_grad, gated_grad * jax.nn.silu(gate_pre)

    def starts_side(sent, filled):
        return local_starts(step, after(filled[0][1], sent), wide_rows, rate, chunk)

    seq_bits = list(range(bits_of("seq")))
    other_bits = [1, 0] + seq_bits[2:] if len(seq_bits) > 1 else seq_bits
    def columns_side(sent, _):
        return columns_by(after(grad_whole, sent), "seq", 0), columns_by(after(normed, sent), "seq", other_bits[0])

    enter_h, filled = entering(local_end, step_total, rate, "seq", 1, [output_side, starts_side, columns_side])
    (gated_grad, y_grad), local_start, sides = filled[:3]
    shapes = [
        (rate.shape, F32),
        ((toks, inner // LANES, states * seqs, LANES), BF16),
        ((chunks, states, seqs, inner), BF16),
        ((rows, inner), BF16),
        ((rows, inner), BF16),
    ]
    arrays = (step, mixed, gate_pre, gated_grad, wide_rows, narrow_rows, rate)
    middle = chunks // 2

    def first_side(sent, _):
        return forward(arrays, skip, after(enter_h, sent), (), shapes, chunk, 0, middle)

    def second_side(sent, filled):
        state, *done = after(filled[1], sent)
        return forward(arrays, skip, state, done, shapes, chunk, middle, chunks)

    enter_g, filled = entering(
        local_start, step_total, rate, "seq", -1, [lambda sent, _: enter_h, first_side, second_side]
    )
    _, history, starts, gated_out, gate_grad = filled[2]
    by_part = lambda value: value.reshape(seq_count, -1, value.shape[-1])
    first_product = lambda columns, value: dot(columns, value, CONTRACT_FIRST, out=BF16)
    out_sent, gate_sent = (
        first_product(columns[1], value) for columns, value in zip(sides, (gated_out, gate_grad))
    )
    out_kept, gate_kept = (
        first_product(columns[0], after(value, out_sent, gate_sent)) for columns, value in zip(sides, (gated_out, gate_grad))
    )
    out_chain = Chain(None, "seq", seq_bits, halves=(out_kept, out_sent))
    gate_chain = Chain(None, "seq", other_bits, halves=(gate_kept, gate_sent))
    apart, joint = [[out_chain], [gate_chain]], [[out_chain, gate_chain]]
    (enter_g,) = send_chains(apart, [out_sent, gate_sent], enter_g)
    enter_g = after(enter_g, out_kept, gate_kept)
    chips = (2,) * (chan_bits - 1)

    def features(*pairs):
        sides = product_sides(own_bit("chan", 0), share, *pairs)
        return tuple(side.reshape(chips + side.shape[1:]) for side in sides)

    scan_sums, pre_grad, mixed_part, proj_sum = backward(
        step, mixed, y_grad, wide_rows, narrow_rows, rate, skip, step_weight, history, starts, enter_g, chunk
    )
    pre_grad, proj_sum = end_chains(apart, pre_grad, proj_sum)
    for bit in range(chan_bits):
        received = swapped(proj_sum.astype(BF16) if bit else proj_sum, "chan", bit)
        if bit == 0:
            (received,) = send_chains(apart, merge(apart), received)
        if bit == chan_bits - 1:
            branch_sum = Scattered(None, "chan", halves=features((after(gated_out, proj_sum), out_weight)))
            received, branch_sum.kept, branch_sum.sent = lax.optimization_barrier(
                (received, branch_sum.kept, branch_sum.sent)
            )
        proj_sum = proj_sum + received.astype(F32)
    proj_grad = proj_sum.astype(BF16)
    own_spread, first_grad, conv_sums = conv_back(
        proj_grad, proj_weight, mixed_part, conv_out, conv_in, previous, conv_taps, math.gcd(toks, 32)
    )
    incoming = moved(first_grad, "seq", -1)
    (own_spread,) = end_chains(apart, own_spread)
    half = inner // 2
    first_last, second_last = (
        by_part(dot(extended_normed, own_spread[:, at : at + half], CONTRACT_FIRST, out=BF16)) for at in (0, half)
    )
    first, second = Chain([first_last], "seq", seq_bits), Chain([second_last], "seq", other_bits)
    out_chain.got, first.sent, second.sent = lax.optimization_barrier((out_chain.got, first.sent, second.sent))
    weight_message = merge(apart)
    in_window = [[first], [second], [out_chain]]
    (own_spread,) = start_all([branch_sum], own_spread)
    own_spread, incoming = send_chains(in_window[:2], [first.sent, second.sent], own_spread, incoming)
    (own_spread,) = send_chains(in_window[2:], weight_message[:1], own_spread)
    zeros = jnp.zeros((halo, inner), F32)
    from_after = jnp.concatenate([zeros, incoming, zeros], axis=0)
    late = sum(
        conv_taps[k] * from_after[(2 * taps - 2 - k) * seqs - halo : (2 * taps - 2 - k) * seqs] for k in range(taps)
    )
    conv_in_grad = jnp.concatenate(
        [own_spread[lead : lead + rows - halo], (own_spread[lead + rows - halo :].astype(F32) + late).astype(BF16)], axis=0
    )
    late_proj, late_pre, late_sums = after((proj_grad, pre_grad, conv_sums), own_spread)
    proj_weight_part = dot(late_proj, mixed, out=BF16)
    step_weight_part = dot(step_low, late_pre, out=BF16)
    sums = jnp.concatenate([scan_sums, jnp.sum(late_sums, axis=1)], axis=0)
    sum_rows = sums.shape[0]
    sums = padded_rows(jnp.concatenate([sums[:, :half], sums[:, half:]], axis=0), 0, 16)
    small_blocks = jnp.concatenate([by_part(proj_weight_part), by_part(step_weight_part)], axis=1)
    small_blocks = padded_rows(jnp.concatenate([small_blocks[..., :half], small_blocks[..., half:]], axis=1), 1, 16)
    third = Chain([small_blocks], "seq", seq_bits, sums)
    row_dots = jnp.sum(
        conv_in_grad.astype(F32) * conv_in.astype(F32) + gate_grad.astype(F32) * gate_pre, axis=1
    )
    last_pair = (gate_grad, after(gate_weights, third.sent, row_dots))
    normed_sum = Scattered(None, "chan", halves=features((conv_in_grad, conv_weights), last_pair))
    normed_sum.sent, normed_sum.kept, third.sent = end_chains(
        in_window, normed_sum.sent, normed_sum.kept, third.sent
    )
    row_dots, third.sent = end_all([branch_sum], row_dots, third.sent)
    groups = [[first], [second]]
    messages = merge(groups)
    (row_dots,) = start_all([normed_sum, branch_sum], row_dots)
    in_window = [*groups, [third], [gate_chain]]
    (row_dots,) = send_chains(in_window, [*messages, third.sent, weight_message[1]], row_dots)
    row_dots = row_dots + swapped(row_dots, "chan", 0)
    (row_dots,) = end_all([normed_sum], row_dots)
    (row_dots,) = start_all([normed_sum], row_dots)
    (row_dots,) = end_all([branch_sum], row_dots)
    (row_dots,) = end_chains(in_window, row_dots)
    groups = [[first], [second], [third]]
    (row_dots,) = send_chains(groups, merge(groups), row_dots)
    for bit in range(1, chan_bits):
        row_dots = row_dots + swapped(row_dots, "chan", bit)
    (row_dots,) = end_all([normed_sum], row_dots)
    normed_grad = finished_on_the_way(normed_sum)
    row_dots = row_dots[:, None]
    wide_own = own_in.astype(F32)
    own_gain = lax.dynamic_slice_in_dim(gain_full, lax.axis_index("chan") * share, share, 0)
    in_rows = (
        own_out_grad.astype(F32)
        + inv_rms * own_gain * normed_grad
        - wide_own * (inv_rms * inv_rms / model) * row_dots
    ).astype(BF16)
    in_grad = in_rows.reshape(toks, seqs, share).swapaxes(0, 1)
    gain_grad = jnp.sum(normed_grad * wide_own * inv_rms, axis=0)
    in_grad, gain_grad = end_chains(groups, in_grad, gain_grad)
    if third.order:
        (gain_grad,) = send_chains([[third]], merge([[third]]), gain_grad)
    gain_grad = summed_near(gain_grad, "seq", bits_of("seq"))
    (first_last,), (second_last,), (small, sums) = last_of(first), last_of(second), last_of(third)
    (out_weight_grad,), (gate_weight_grad,) = last_of(out_chain), last_of(gate_chain)
    last = jnp.concatenate([first_last, second_last], axis=1)
    sums = jnp.concatenate([sums[:sum_rows], sums[sum_rows : 2 * sum_rows]], axis=1)
    proj_share, step_share = proj_weight.shape[0] // seq_count, rank // seq_count
    each = proj_share + step_share
    small_of = lambda start, count: jnp.concatenate([small[start : start + count], small[each + start : each + start + count]], axis=1)
    block_rows = (own_in.astype(F32) + finished_on_the_way(branch_sum)).astype(BF16)
    block_out = block_rows.reshape(toks, seqs, share).swapaxes(0, 1)
    return (
        block_out,
        in_grad,
        gain_grad,
        jnp.stack([last, gate_weight_grad], axis=1),
        sums[states + 2 : states + 2 + taps],
        sums[states + 2 + taps],
        small_of(0, proj_share),
        small_of(proj_share, step_share),
        sums[states],
        sums[:states],
        sums[states + 1],
        out_weight_grad,
    )


def solution(mesh):
    in_specs = (
        P(None, "seq", "chan"),
        P(),
        P(None, None, "chan"),
        P(None, "chan"),
        P("chan"),
        P(None, "chan"),
        P(None, "chan"),
        P("chan"),
        P(None, "chan"),
        P("chan"),
        P(None, "chan"),
        P(None, "seq", "chan"),
    )
    out_specs = (
        P(None, "seq", "chan"),
        P(None, "seq", "chan"),
        P("chan"),
        P("seq", None, "chan"),
        P(None, "chan"),
        P("chan"),
        P("seq", "chan"),
        P("seq", "chan"),
        P("chan"),
        P(None, "chan"),
        P("chan"),
        P("seq", "chan"),
    )
    return jax.shard_map(shards, mesh=mesh, in_specs=in_specs, out_specs=out_specs, check_vma=False)
```

```python
import functools, math
import jax, jax.numpy as jnp
from jax import lax
from jax.sharding import PartitionSpec as P
from jax.experimental import pallas as pl
from jax.experimental.pallas import tpu as pltpu

LANES = 128
LOG2E = 1.4426950408889634
VM = 56 * 1024 * 1024
F32, BF16 = jnp.float32, jnp.bfloat16


def spread(rows_ref, select_ref, spread_ref, narrow_ref, chunk, count, seqs):
    left, parts = rows_ref[...], []
    for _ in range(3):
        parts.append(left.astype(BF16))
        left = left - parts[-1].astype(F32)
    stacked = jnp.concatenate(parts, axis=0)
    for col in range(0, count, 2):
        wide = lax.dot_general(
            stacked, select_ref[:, col * LANES : (col + 2) * LANES], (((0,), (0,)), ((), ())), preferred_element_type=F32
        )
        for tok in range(chunk):
            both = [wide[tok * seqs : (tok + 1) * seqs, i * LANES : (i + 1) * LANES] for i in range(2)]
            for i in range(2):
                spread_ref[tok, col + i] = both[i]
            narrow_ref[tok, pl.ds(col * seqs, 2 * seqs), :] = jnp.concatenate(both, axis=0).astype(BF16)


def ends_kernel(chunk, step_ref, mixed_ref, rows_ref, rate_ref, h_ref, spread_ref, narrow_ref, select_ref):
    states, seqs, width = rate_ref.shape

    @pl.when(pl.program_id(0) == 0)
    def _():
        h_ref[...] = jnp.zeros_like(h_ref)
        row = lax.broadcasted_iota(jnp.int32, select_ref.shape, 0)
        col = lax.broadcasted_iota(jnp.int32, select_ref.shape, 1)
        select_ref[...] = (row % (2 * states) == col // LANES).astype(BF16)

    spread(rows_ref, select_ref, spread_ref, narrow_ref, chunk, 2 * states, seqs)

    def tile_step(j, _):
        lanes = pl.ds(pl.multiple_of(j * LANES, LANES), LANES)
        h = [h_ref[n, :, lanes] for n in range(states)]
        for tok in range(0, chunk, 2):
            m = mixed_ref[pl.ds(tok * seqs, 2 * seqs), lanes].astype(F32)
            for k in range(2):
                s = step_ref[pl.ds((tok + k) * seqs, seqs), lanes]
                x = s * m[k * seqs : (k + 1) * seqs]
                for n in range(states):
                    h[n] = jnp.exp2(s * rate_ref[n, :, lanes]) * h[n] + spread_ref[tok + k, n] * x
        for n in range(states):
            h_ref[n, :, lanes] = h[n]
        return 0

    lax.fori_loop(0, width // LANES, tile_step, 0, unroll=4)


def starts_kernel(chunk, step_ref, yg_ref, spread_ref, rate_ref, q_ref):
    states, seqs, width = rate_ref.shape

    @pl.when(pl.program_id(0) == 0)
    def _():
        q_ref[...] = jnp.zeros_like(q_ref)

    def tile_step(j, _):
        lanes = pl.ds(pl.multiple_of(j * LANES, LANES), LANES)
        q = [q_ref[n, :, lanes] for n in range(states)]
        for tok in reversed(range(chunk)):
            rows = pl.ds(tok * seqs, seqs)
            s, y = step_ref[rows, lanes], yg_ref[rows, lanes]
            for n in range(states):
                q[n] = jnp.exp2(s * rate_ref[n, :, lanes]) * (q[n] + spread_ref[tok, n] * y)
        for n in range(states):
            q_ref[n, :, lanes] = q[n]
        return 0

    lax.fori_loop(0, width // LANES, tile_step, 0, unroll=4)


def spread_spec(chunk, count, seqs, part, at):
    return pl.BlockSpec((chunk, count, seqs, LANES), lambda i: (at(i), part, 0, 0))


def narrow_spec(chunk, count, seqs, part, at):
    return pl.BlockSpec((chunk, count * seqs, LANES), lambda i: (at(i), part, 0))


def halves_sum(parts):
    while len(parts) > 1:
        parts = [a + b for a, b in zip(parts[::2], parts[1::2])]
    total = parts[0].astype(F32)
    seqs = total.shape[0] // 2
    return total[:seqs] + total[seqs:]


def local_ends(step, mixed, rows_t, rate, chunk):
    rows, width = step.shape
    states, seqs, _ = rate.shape
    elements = rows * width * states
    grid = rows // (chunk * seqs)
    row_spec = pl.BlockSpec((chunk * seqs, width), lambda i: (i, 0))
    whole = pl.BlockSpec((states, seqs, width), lambda i: (0, 0, 0))
    return pl.pallas_call(
        functools.partial(ends_kernel, chunk),
        grid=(grid,),
        in_specs=[row_spec, row_spec, pl.BlockSpec((2 * states, chunk * seqs), lambda i: (0, i)), whole],
        out_specs=[whole, spread_spec(chunk, 2 * states, seqs, 0, lambda i: i), narrow_spec(chunk, 2 * states, seqs, 0, lambda i: i)],
        out_shape=[jax.ShapeDtypeStruct(rate.shape, F32), jax.ShapeDtypeStruct((rows // seqs, 2 * states, seqs, LANES), F32),
                   jax.ShapeDtypeStruct((rows // seqs, 2 * states * seqs, LANES), BF16)],
        scratch_shapes=[pltpu.VMEM((6 * states, 2 * states * LANES), BF16)],
        compiler_params=pltpu.CompilerParams(vmem_limit_bytes=VM),
        cost_estimate=pl.CostEstimate(flops=elements, bytes_accessed=elements, transcendentals=0),
        name="local_ends",
    )(step, mixed, rows_t, rate)


def local_starts(step, yg, wide_rows, rate, chunk):
    rows, width = step.shape
    states, seqs, _ = rate.shape
    elements = rows * width * states
    grid = rows // (chunk * seqs)
    at = lambda i: grid - 1 - i
    row_spec = pl.BlockSpec((chunk * seqs, width), lambda i: (at(i), 0))
    whole = pl.BlockSpec((states, seqs, width), lambda i: (0, 0, 0))
    return pl.pallas_call(
        functools.partial(starts_kernel, chunk),
        grid=(grid,),
        in_specs=[row_spec, row_spec, spread_spec(chunk, states, seqs, 1, at), whole],
        out_specs=whole,
        out_shape=jax.ShapeDtypeStruct(rate.shape, F32),
        compiler_params=pltpu.CompilerParams(vmem_limit_bytes=VM),
        cost_estimate=pl.CostEstimate(flops=elements, bytes_accessed=elements, transcendentals=0),
        name="local_starts",
    )(step, yg, wide_rows, rate)


def fwd_kernel(chunk, step_ref, mixed_ref, gate_ref, gg_ref, spread_ref, narrow_ref, rate_ref, skip_ref,
               hin_ref, *refs):
    state_ref, hist_ref, start_ref, gated_ref, ggrad_ref = refs[-5:]
    states, seqs, width = rate_ref.shape

    @pl.when(pl.program_id(0) == 0)
    def _():
        state_ref[...] = hin_ref[...]

    start_ref[0] = state_ref[...].astype(BF16)

    def tile_step(j, _):
        lanes = pl.ds(pl.multiple_of(j * LANES, LANES), LANES)
        h = [state_ref[n, :, lanes] for n in range(states)]
        skip = skip_ref[:, lanes]
        for tok in range(0, chunk, 2):
            pair_rows = pl.ds(tok * seqs, 2 * seqs)
            pair = mixed_ref[pair_rows, lanes].astype(F32)
            gated, ggrad = [], []
            for k in range(2):
                rows = pl.ds((tok + k) * seqs, seqs)
                s = step_ref[rows, lanes]
                m = pair[k * seqs : (k + 1) * seqs]
                x = s * m
                terms = []
                for n in range(0, states, 2):
                    for i in (n, n + 1):
                        h[i] = jnp.exp2(s * rate_ref[i, :, lanes]) * h[i] + spread_ref[tok + k, i] * x
                    both = jnp.concatenate([h[n], h[n + 1]], axis=0).astype(BF16)
                    hist_ref[tok + k, j, pl.ds(n * seqs, 2 * seqs), :] = both
                    terms.append(both * narrow_ref[tok + k, pl.ds(n * seqs, 2 * seqs), :])
                y = skip * m + halves_sum(terms)
                v = gate_ref[rows, lanes]
                sig = 1.0 / (1.0 + jnp.exp2(v * (-LOG2E)))
                gated.append(y * (v * sig))
                ggrad.append(gg_ref[rows, lanes] * y * (sig * (1.0 + v * (1.0 - sig))))
            gated_ref[pair_rows, lanes] = jnp.concatenate(gated, axis=0).astype(BF16)
            ggrad_ref[pair_rows, lanes] = jnp.concatenate(ggrad, axis=0).astype(BF16)
        for n in range(states):
            state_ref[n, :, lanes] = h[n]
        return 0

    lax.fori_loop(0, width // LANES, tile_step, 0, unroll=4)


def forward(arrays, skip, carried, filled, shapes, chunk, first, last):
    step, mixed, gate, gg, wide_rows, narrow_rows, rate = arrays
    rows, width = step.shape
    states, seqs, _ = rate.shape
    at = lambda i: first + i
    row_spec = pl.BlockSpec((chunk * seqs, width), lambda i: (at(i), 0))
    whole = pl.BlockSpec((states, seqs, width), lambda i: (0, 0, 0))
    anywhere = pl.BlockSpec(memory_space=pl.ANY)
    elements = (last - first) * chunk * seqs * width * states
    return pl.pallas_call(
        functools.partial(fwd_kernel, chunk),
        grid=(last - first,),
        in_specs=[row_spec, row_spec, row_spec, row_spec, spread_spec(chunk, states, seqs, 0, at), narrow_spec(chunk, states, seqs, 1, at), whole,
                  pl.BlockSpec((seqs, width), lambda i: (0, 0)), whole] + [anywhere] * len(filled),
        out_specs=[whole, pl.BlockSpec((chunk, width // LANES, states * seqs, LANES), lambda i: (at(i), 0, 0, 0)),
                   pl.BlockSpec((1, states, seqs, width), lambda i: (at(i), 0, 0, 0)), row_spec, row_spec],
        out_shape=[jax.ShapeDtypeStruct(*shape) for shape in shapes],
        input_output_aliases={8 + i: i for i in range(len(filled) + 1)},
        compiler_params=pltpu.CompilerParams(vmem_limit_bytes=VM),
        cost_estimate=pl.CostEstimate(flops=elements, bytes_accessed=elements, transcendentals=0),
        name="scan_forward",
    )(step, mixed, gate, gg, wide_rows, narrow_rows, rate, skip, carried, *filled)


def bwd_kernel(chunk, step_ref, mixed_ref, yg_ref, spread_ref, narrow_ref, rate_ref, skip_ref, low_ref, hist_ref, start_ref, gin_ref,
               sums_ref, pre_ref, part_ref, proj_ref, decay_ref, bias_ref, skipg_ref, state_ref, b_ref, c_ref):
    states, seqs, width = rate_ref.shape
    span = states * seqs

    @pl.when(pl.program_id(0) == 0)
    def _():
        state_ref[...] = gin_ref[...]
        decay_ref[...] = jnp.zeros_like(decay_ref)
        bias_ref[...] = jnp.zeros_like(bias_ref)
        skipg_ref[...] = jnp.zeros_like(skipg_ref)

    b_ref[...] = jnp.zeros_like(b_ref)
    c_ref[...] = jnp.zeros_like(c_ref)
    contract = (((1,), (1,)), ((), ()))

    def tile_step(j, _):
        lanes = pl.ds(pl.multiple_of(j * LANES, LANES), LANES)
        q = [state_ref[n, :, lanes] for n in range(states)]
        acc = [decay_ref[n, :, lanes] for n in range(states)]
        skip = skip_ref[:, lanes]
        bias = bias_ref[:, lanes]
        skipg = skipg_ref[:, lanes]
        for tok in range(chunk - 2, -1, -2):
            pair_rows = pl.ds(tok * seqs, 2 * seqs)
            pair = mixed_ref[pair_rows, lanes].astype(F32)
            pre, xs, packed, weights = [None, None], [None, None], [None, None], [None, None]
            for k in (1, 0):
                now = tok + k
                rows = pl.ds(now * seqs, seqs)
                s = step_ref[rows, lanes]
                y = yg_ref[rows, lanes]
                m = pair[k * seqs : (k + 1) * seqs]
                gs, along_terms, size_terms = [], [], []
                for n in range(0, states, 2):
                    if now > 0:
                        before = hist_ref[now - 1, j, pl.ds(n * seqs, 2 * seqs), :]
                    else:
                        before = jnp.concatenate([start_ref[0, n + i, :, lanes] for i in range(2)], axis=0)
                    both, moves = [], []
                    for i in (n, n + 1):
                        z = s * rate_ref[i, :, lanes]
                        g = spread_ref[now, i] * y + q[i]
                        q[i] = jnp.exp2(z) * g
                        both.append(g)
                        moves.append(q[i] * z)
                    gs.append(jnp.concatenate(both, axis=0).astype(BF16))
                    along_terms.append(gs[-1] * narrow_ref[now, pl.ds(n * seqs, 2 * seqs), :])
                    size_terms.append(jnp.concatenate(moves, axis=0).astype(BF16) * before)
                packed[k] = jnp.concatenate(gs, axis=0)
                weights[k] = size_terms
                along, size = halves_sum(along_terms), halves_sum(size_terms)
                part_ref[rows, lanes] = s * along + skip * y
                skipg = skipg + y * m
                xs[k] = s * m
                series = 1.0 - s * (1.0 / 2) * (1.0 - s * (1.0 / 3) * (1.0 - s * (1.0 / 4) * (1.0 - s * (1.0 / 5))))
                ratio = jnp.where(s < 0.1, series, (1.0 - jnp.exp2(s * (-LOG2E))) / jnp.maximum(s, 0.1))
                pre[k] = ratio * (size * (1.0 / LOG2E) + xs[k] * along)
            for n in range(0, states, 2):
                total = (weights[0][n // 2] + weights[1][n // 2]).astype(F32)
                acc[n] = acc[n] + total[:seqs]
                acc[n + 1] = acc[n + 1] + total[seqs:]
            rounded = jnp.concatenate(pre, axis=0).astype(BF16)
            pre_ref[pair_rows, lanes] = rounded
            wide = rounded.astype(F32)
            bias = bias + wide[:seqs] + wide[seqs:]
            x = jnp.concatenate(xs, axis=0).astype(BF16)
            pair_hist = jnp.concatenate([hist_ref[tok, j], hist_ref[tok + 1, j]], axis=0)
            b_ref[tok // 2] += lax.dot_general(x, jnp.concatenate(packed, axis=0), contract, preferred_element_type=F32)
            c_ref[tok // 2] += lax.dot_general(
                yg_ref[pair_rows, lanes].astype(BF16), pair_hist, contract, preferred_element_type=F32
            )
        for n in range(states):
            state_ref[n, :, lanes] = q[n]
            decay_ref[n, :, lanes] = acc[n]
        bias_ref[:, lanes] = bias
        skipg_ref[:, lanes] = skipg
        return 0

    lax.fori_loop(0, width // LANES, tile_step, 0, unroll=4)
    wide = 2 * span
    row = lax.broadcasted_iota(jnp.int32, (2 * seqs, wide), 0)
    col = lax.broadcasted_iota(jnp.int32, (2 * seqs, wide), 1)
    match = (row // seqs == col // span) & (row % seqs == col % seqs)
    b_rows = [jnp.where(match, b_ref[i], 0.0) for i in range(chunk // 2)]
    c_rows = [jnp.where(match, c_ref[i], 0.0) for i in range(chunk // 2)]
    src = lax.broadcasted_iota(jnp.int32, (2 * states, wide), 1) // seqs % states
    dst = lax.broadcasted_iota(jnp.int32, (2 * states, wide), 0)
    fold_b = (src == dst).astype(BF16)
    fold_c = (src + states == dst).astype(BF16)
    rank = low_ref.shape[0]
    proj_ref[:rank] = lax.dot_general(low_ref[...], pre_ref[...], contract, preferred_element_type=F32)
    proj_ref[rank:] = lax.dot_general(
        fold_b, jnp.concatenate(b_rows, axis=0).astype(BF16), contract, preferred_element_type=F32
    ) + lax.dot_general(fold_c, jnp.concatenate(c_rows, axis=0).astype(BF16), contract, preferred_element_type=F32)

    @pl.when(pl.program_id(0) == pl.num_programs(0) - 1)
    def _():
        sums_ref[:states] = jnp.sum(decay_ref[...], axis=1) * (1.0 / LOG2E)
        sums_ref[states : states + 1] = jnp.sum(bias_ref[...], axis=0, keepdims=True)
        sums_ref[states + 1 : states + 2] = jnp.sum(skipg_ref[...], axis=0, keepdims=True)


def backward(step, mixed, yg, wide_rows, narrow_rows, rate, skip, low_weight, hist, start, gin, chunk):
    rows, width = step.shape
    states, seqs, _ = rate.shape
    grid = rows // (chunk * seqs)
    elements = rows * width * states
    at = lambda i: grid - 1 - i
    row_spec = pl.BlockSpec((chunk * seqs, width), lambda i: (at(i), 0))
    rank = low_weight.shape[0]
    whole = pl.BlockSpec((states, seqs, width), lambda i: (0, 0, 0))
    one = pl.BlockSpec((seqs, width), lambda i: (0, 0))
    return pl.pallas_call(
        functools.partial(bwd_kernel, chunk),
        grid=(grid,),
        in_specs=[row_spec, row_spec, row_spec, spread_spec(chunk, states, seqs, 1, at),
                  narrow_spec(chunk, states, seqs, 0, at), whole, one,
                  pl.BlockSpec((rank, width), lambda i: (0, 0)),
                  pl.BlockSpec((chunk, width // LANES, states * seqs, LANES), lambda i: (at(i), 0, 0, 0)),
                  pl.BlockSpec((1, states, seqs, width), lambda i: (at(i), 0, 0, 0)), whole],
        out_specs=[pl.BlockSpec((states + 2, width), lambda i: (0, 0)), row_spec, row_spec,
                   pl.BlockSpec((rank + 2 * states, chunk * seqs), lambda i: (0, at(i)))],
        out_shape=[jax.ShapeDtypeStruct((states + 2, width), F32), jax.ShapeDtypeStruct((rows, width), BF16),
                   jax.ShapeDtypeStruct((rows, width), F32), jax.ShapeDtypeStruct((rank + 2 * states, rows), F32)],
        scratch_shapes=[pltpu.VMEM(rate.shape, F32), pltpu.VMEM((seqs, width), F32), pltpu.VMEM((seqs, width), F32),
                        pltpu.VMEM(rate.shape, F32)] + [pltpu.VMEM((chunk // 2, 2 * seqs, 2 * states * seqs), F32)] * 2,
        compiler_params=pltpu.CompilerParams(vmem_limit_bytes=VM),
        cost_estimate=pl.CostEstimate(flops=elements, bytes_accessed=elements, transcendentals=0),
        name="scan_backward",
    )(step, mixed, yg, wide_rows, narrow_rows, rate, skip, low_weight, hist, start, gin)


def conv_kernel(chunk, taps, proj_ref, weight_ref, part_ref, conv_ref, in_ref, before_ref, taps_ref,
                spread_ref, first_ref, sums_ref, grad_ref, back_ref):
    rows, width = part_ref.shape
    seqs = rows // chunk
    halo = (taps - 1) * seqs
    lead = before_ref.shape[0]
    step = pl.program_id(0)
    block = pl.num_programs(0) - 1 - step

    @pl.when(step == 0)
    def _():
        grad_ref[rows:] = jnp.zeros_like(grad_ref[rows:])
        sums_ref[...] = jnp.zeros_like(sums_ref)

    @pl.when(step > 0)
    def _():
        grad_ref[rows : rows + halo] = grad_ref[:halo]

    back_ref[...] = lax.dot_general(
        proj_ref[...], weight_ref[...], (((0,), (0,)), ((), ())), preferred_element_type=F32
    )

    def tile_step(j, _):
        lanes = pl.ds(pl.multiple_of(j * LANES, LANES), LANES)
        tap = [taps_ref[k : k + 1, lanes] for k in range(taps)]
        sums = [sums_ref[k, :, lanes] for k in range(taps + 1)]
        for tok in reversed(range(0, chunk, 2)):
            at = pl.ds(tok * seqs, 2 * seqs)
            v = conv_ref[at, lanes]
            sig = 1.0 / (1.0 + jnp.exp2(v * (-LOG2E)))
            grad = (part_ref[at, lanes] + back_ref[at, lanes]) * (sig * (1.0 + v * (1.0 - sig)))
            grad_ref[at, lanes] = grad
            given = in_ref[at, lanes].astype(F32)
            spread = jnp.zeros_like(grad)
            for k in range(taps):
                later = grad_ref[pl.ds((tok + taps - 1 - k) * seqs, 2 * seqs), lanes]
                spread = spread + tap[k] * later
                use = given * later
                sums[k] = sums[k] + use[:seqs] + use[seqs:]
            sums[taps] = sums[taps] + grad[:seqs] + grad[seqs:]
            out_at = pl.multiple_of(lead + block * rows + tok * seqs, 2 * seqs)
            spread_ref[pl.ds(out_at, 2 * seqs), lanes] = spread.astype(BF16)
        for k in range(taps + 1):
            sums_ref[k, :, lanes] = sums[k]
        return 0

    lax.fori_loop(0, width // LANES, tile_step, 0, unroll=4)

    @pl.when(block == 0)
    def _():
        first_ref[...] = grad_ref[:halo]
        given = before_ref[...].astype(F32)
        parts = [jnp.zeros((lead - halo, width), F32)]
        for tok in range(taps - 1):
            spread = jnp.zeros((seqs, width), F32)
            own = given[lead - halo + tok * seqs : lead - halo + (tok + 1) * seqs]
            for k in range(tok + 1):
                later = grad_ref[(tok - k) * seqs : (tok - k + 1) * seqs]
                spread = spread + taps_ref[k : k + 1] * later
                sums_ref[k] = sums_ref[k] + own * later
            parts.append(spread)
        spread_ref[:lead] = jnp.concatenate(parts, axis=0).astype(BF16)


def conv_back(proj_grad, weight, part, conv_out, conv_in, before, conv_taps, chunk):
    rows, width = part.shape
    taps = conv_taps.shape[0]
    columns = proj_grad.shape[0]
    seqs, lead = 8, before.shape[0]
    halo = (taps - 1) * seqs
    grid = rows // (chunk * seqs)
    at = lambda i: grid - 1 - i
    row_spec = pl.BlockSpec((chunk * seqs, width), lambda i: (at(i), 0))
    fixed = lambda *shape: pl.BlockSpec(shape, lambda i: (0,) * len(shape))
    return pl.pallas_call(
        functools.partial(conv_kernel, chunk, taps),
        grid=(grid,),
        in_specs=[pl.BlockSpec((columns, chunk * seqs), lambda i: (0, at(i))), fixed(columns, width), row_spec, row_spec, row_spec,
                  fixed(lead, width), fixed(taps, width)],
        out_specs=[fixed(rows + lead, width), fixed(halo, width), fixed(taps + 1, seqs, width)],
        out_shape=[jax.ShapeDtypeStruct((rows + lead, width), BF16), jax.ShapeDtypeStruct((halo, width), F32),
                   jax.ShapeDtypeStruct((taps + 1, seqs, width), F32)],
        scratch_shapes=[pltpu.VMEM((chunk * seqs + lead, width), F32), pltpu.VMEM((chunk * seqs, width), F32)],
        compiler_params=pltpu.CompilerParams(vmem_limit_bytes=VM),
        cost_estimate=pl.CostEstimate(flops=rows * width, bytes_accessed=rows * width, transcendentals=0),
        name="conv_backward",
    )(proj_grad, weight, part, conv_out, conv_in, before, conv_taps)


def merge_kernel(plan, messages, bits_ref, *refs):
    refs = list(refs)
    inputs = [[refs.pop(0) for _ in range(len(sizes) + 1 + (extra > 0))] for _, _, sizes, extra, *_ in plan]
    outputs = [[refs.pop(0) for _ in range(len(sizes) + (extra > 0))] for _, _, sizes, extra, *_ in plan]
    sent = [refs.pop(0) for _ in range(messages)]
    for index, (levels, dim, sizes, extra, got_at, message, sent_at) in enumerate(plan):
        bit = bits_ref[index]
        kept, got, whole = inputs[index][: len(sizes)], inputs[index][len(sizes)], inputs[index][-1]
        kept_out, whole_out, sent_out = outputs[index][: len(sizes)], outputs[index][-1], sent[message]
        after_dim = 1 << (levels - 1 - dim)
        for size, source, target in zip(sizes, kept, kept_out):
            for rest in range(1 << (levels - 1)):
                high, low = divmod(rest, after_dim)
                for side in range(2):
                    own = bit if side == 0 else 1 - bit
                    at = pl.multiple_of(((high * 2 + own) * after_dim + low) * size, 16)
                    total = source[pl.ds(at, size), :].astype(F32) + got[pl.ds(got_at + at, size), :].astype(F32)
                    if side == 0:
                        target[rest * size : (rest + 1) * size, :] = total.astype(BF16)
                    else:
                        sent_out[sent_at + rest * size : sent_at + (rest + 1) * size, :] = total.astype(BF16)
            got_at += size << levels
            sent_at += size << (levels - 1)
        if extra:
            other = got[got_at : got_at + extra, :].astype(F32) + got[got_at + extra : got_at + 2 * extra, :].astype(F32)
            total = whole[...] + other
            upper = total.astype(BF16)
            lower = (total - upper.astype(F32)).astype(BF16)
            sent_out[sent_at : sent_at + extra, :] = upper
            sent_out[sent_at + extra : sent_at + 2 * extra, :] = lower
            whole_out[...] = upper.astype(F32) + lower.astype(F32)


def product_kernel(count, core_ref, *refs):
    del core_ref
    kept_ref, sent_ref = refs[-2:]
    total = None
    for a_ref, b_ref in zip(refs[:count], refs[count : 2 * count]):
        part = lax.dot_general(a_ref[...], b_ref[...], (((1,), (1,)), ((), ())), preferred_element_type=F32)
        total = part if total is None else total + part
    side = pl.program_id(1)

    @pl.when(side == 0)
    def _():
        kept_ref[0] = total.astype(BF16)

    @pl.when(side == 1)
    def _():
        sent_ref[0] = total.astype(BF16)


def product_sides(core, share, *pairs):
    rows, columns = pairs[0][0].shape[0], pairs[0][1].shape[0]
    chips = columns // share // 2
    mine = lambda far, side, core_ref: (far * 2 + jnp.where(side == 0, core_ref[0], 1 - core_ref[0]), 0)
    out_spec = pl.BlockSpec((1, rows, share), lambda far, side, core_ref: (far, 0, 0))
    return pl.pallas_call(
        functools.partial(product_kernel, len(pairs)),
        grid_spec=pltpu.PrefetchScalarGridSpec(
            num_scalar_prefetch=1,
            grid=(chips, 2),
            in_specs=[pl.BlockSpec(a.shape, lambda far, side, core_ref: (0, 0)) for a, _ in pairs]
            + [pl.BlockSpec((share, b.shape[1]), mine) for _, b in pairs],
            out_specs=[out_spec, out_spec],
        ),
        out_shape=[jax.ShapeDtypeStruct((chips, rows, share), BF16)] * 2,
        compiler_params=pltpu.CompilerParams(vmem_limit_bytes=VM),
        cost_estimate=pl.CostEstimate(flops=1024, bytes_accessed=1024, transcendentals=0),
        name="product_sides",
    )(core.reshape(1).astype(jnp.int32), *[a for a, _ in pairs], *[b for _, b in pairs])


EPSILON = 1e-05
CONTRACT_LAST = (((1,), (1,)), ((), ()))
CONTRACT_FIRST = (((0,), (0,)), ((), ()))


def dot(a, b, dims=(((1,), (0,)), ((), ())), out=F32):
    return lax.dot_general(a, b, dims, preferred_element_type=out)


def after(value, *done):
    return lax.optimization_barrier((value, done))[0]


def swapped(value, axis, bit):
    count = lax.axis_size(axis)
    return lax.ppermute(value, axis, [(i, i ^ (1 << bit)) for i in range(count)])


def moved(value, axis, distance):
    count = lax.axis_size(axis)
    return lax.ppermute(value, axis, [(i, i + distance) for i in range(count) if 0 <= i + distance < count])


def bits_of(axis):
    return lax.axis_size(axis).bit_length() - 1


def own_bit(axis, bit):
    return (lax.axis_index(axis) >> bit) & 1


def gathered(value, axis, meanwhile=()):
    count = lax.axis_size(axis)
    parts = {0: value}
    for bit in reversed(range(bits_of(axis))):
        fresh = {mask | (1 << bit): swapped(part, axis, bit) for mask, part in parts.items()}
        if len(parts) == 1:
            fresh, meanwhile = lax.optimization_barrier((fresh, meanwhile))
        parts |= fresh
    for bit in range(bits_of(axis)):
        high = own_bit(axis, bit) == 1
        parts = {m: jnp.where(high, parts[m ^ (1 << bit)], parts[m]) for m in range(count)}
    return jnp.concatenate([parts[m] for m in range(count)], axis=-1), meanwhile


def summed(value, axis, narrow_from):
    for bit in range(bits_of(axis)):
        sent = value.astype(BF16) if bit >= narrow_from else value
        value = value + swapped(sent, axis, bit).astype(F32)
    return value


def summed_near(value, axis, narrow_from):
    if bits_of(axis) > 1 and narrow_from > 1:
        count = lax.axis_size(axis)
        near = [lax.ppermute(value, axis, [(i, i ^ mask) for i in range(count)]) for mask in (1, 2, 3)]
        value = (value + near[0]) + (near[1] + near[2])
        for bit in range(2, bits_of(axis)):
            value = value + swapped(value, axis, bit)
        return value
    return summed(value, axis, narrow_from)


def pick(value, dim, index):
    return lax.dynamic_index_in_dim(value, index, dim, keepdims=False)


class Scattered:
    def __init__(self, blocks, axis, order=None, halves=None):
        bits = bits_of(axis)
        self.axis, self.left, self.order = axis, list(range(bits)), list(order or range(bits))
        self.got, self.kept, self.sent = None, None, None
        if halves:
            self.kept, self.sent = halves
        else:
            self.value = blocks.reshape((2,) * bits + blocks.shape[1:])

    def split(self):
        if self.sent is not None:
            return
        bit = self.order[0]
        dim = len(self.left) - 1 - self.left.index(bit)
        mine = own_bit(self.axis, bit)
        self.kept, self.sent = pick(self.value, dim, mine), pick(self.value, dim, 1 - mine)

    def send(self):
        self.got = swapped(self.sent, self.axis, self.order[0])

    def add(self):
        bit = self.order.pop(0)
        self.left.remove(bit)
        value = self.kept.astype(F32) + self.got.astype(F32)
        self.value = value.astype(BF16) if self.left else value
        self.got, self.kept, self.sent = None, None, None


def start_all(sums, *values):
    sums = [s for s in sums if s.order]
    for s in sums:
        s.split()
    sent, values = lax.optimization_barrier(([s.sent for s in sums], values))
    for s, message in zip(sums, sent):
        s.sent = message
        s.send()
    return values


def end_all(sums, *values):
    sums = [s for s in sums if s.got is not None]
    got, values = lax.optimization_barrier(([s.got for s in sums], values))
    for s, message in zip(sums, got):
        s.got = message
        s.add()
    return values


def padded_rows(value, dim, multiple):
    width = -value.shape[dim] % multiple
    return jnp.pad(value, [(0, width if i == dim else 0) for i in range(value.ndim)])


def two_parts(value):
    upper = value.astype(BF16)
    return upper, (value - upper.astype(F32)).astype(BF16)


class Chain:
    def __init__(self, pieces, axis, order, whole=None, halves=None):
        bits = bits_of(axis)
        self.axis, self.order, self.left, self.whole, self.at = axis, list(order), list(range(bits)), [], 0
        if halves:
            self.sizes = [halves[1].shape[0] >> (bits - 1)]
            self.kept, self.sent = [halves[0]], halves[1]
            return
        self.sizes = [piece.shape[1] for piece in pieces]
        dim = bits - 1 - self.order[0]
        mine = own_bit(axis, self.order[0])
        halves = [piece.reshape((2,) * bits + piece.shape[1:]) for piece in pieces]
        flat = lambda value: value.reshape(-1, value.shape[-1])
        self.kept = [flat(pick(value, dim, mine)) for value in halves]
        message = [flat(pick(value, dim, 1 - mine)) for value in halves]
        if whole is not None:
            upper, lower = two_parts(whole)
            self.whole = [upper.astype(F32) + lower.astype(F32)]
            message += [upper, lower]
        self.sent = jnp.concatenate(message, axis=0) if len(message) > 1 else message[0]

    def finish(self):
        rows, values = self.at, []
        for size, kept in zip(self.sizes, self.kept):
            values.append(kept.astype(F32) + self.got[rows : rows + size].astype(F32))
            rows += size
        if self.whole:
            count = self.whole[0].shape[0]
            upper, lower = (self.got[rows + i * count : rows + (i + 1) * count].astype(F32) for i in range(2))
            values.append(self.whole[0] + (upper + lower))
        return values


def send_chains(groups, messages, *values):
    messages, values = lax.optimization_barrier((messages, values))
    for group, message in zip(groups, messages):
        got = swapped(message, group[0].axis, group[0].order[0])
        for c in group:
            c.got = got
            c.left.remove(c.order.pop(0))
    return values


def end_chains(groups, *values):
    got, values = lax.optimization_barrier(([group[0].got for group in groups], values))
    for group, message in zip(groups, got):
        for c in group:
            c.got = message
    return values


def last_of(chain):
    while chain.order:
        send_chains([[chain]], merge([[chain]]))
    return chain.finish()


def merge(groups):
    plan, operands, outputs, messages = [], [], [], []
    for number, group in enumerate(groups):
        rows = 0
        for c in group:
            levels, extra = len(c.left), c.whole[0].shape[0] if c.whole else 0
            columns = c.got.shape[1]
            plan.append((levels, levels - 1 - c.left.index(c.order[0]), tuple(c.sizes), extra, c.at, number, rows))
            operands += [*c.kept, c.got, *c.whole]
            outputs += [((size << (levels - 1), columns), BF16) for size in c.sizes] + [((extra, columns), F32)] * (extra > 0)
            c.at = rows
            rows += sum(size << (levels - 1) for size in c.sizes) + 2 * extra
        messages.append(((rows, columns), BF16))
    chains = [c for group in groups for c in group]
    bits = jnp.stack([own_bit(c.axis, c.order[0]) for c in chains]).astype(jnp.int32)
    outs = list(
        pl.pallas_call(
            functools.partial(merge_kernel, plan, len(messages)),
            in_specs=[pl.BlockSpec(memory_space=pltpu.SMEM)] + [pl.BlockSpec(memory_space=pltpu.VMEM)] * len(operands),
            out_specs=[pl.BlockSpec(memory_space=pltpu.VMEM)] * (len(outputs) + len(messages)),
            out_shape=[jax.ShapeDtypeStruct(*shape) for shape in outputs + messages],
            compiler_params=pltpu.CompilerParams(vmem_limit_bytes=VM),
            cost_estimate=pl.CostEstimate(flops=1024, bytes_accessed=1024, transcendentals=0),
            name="merge_messages",
        )(bits, *operands)
    )
    for c in chains:
        c.kept = [outs.pop(0) for _ in c.sizes]
        c.whole = [outs.pop(0) for _ in c.whole]
    return outs


def columns_by(value, axis, bit):
    count = lax.axis_size(axis)
    width = value.shape[1] // (count >> bit)
    parts = [value[:, i * width : (i + 1) * width] for i in range(count >> bit)]
    high = own_bit(axis, bit) == 1
    low, up = parts[0::2], parts[1::2]
    return [
        jnp.concatenate([jnp.where(high, b, a) for a, b in zip(one, two)], axis=1) for one, two in ((low, up), (up, low))
    ]


def finished_on_the_way(s):
    if s.got is not None:
        s.add()
    while s.order:
        s.split()
        s.send()
        s.add()
    return s.value


def entering(local, total, rate, axis, direction, fillers):
    states = rate.shape[0]
    enter, enter_sum = jnp.zeros_like(local), jnp.zeros_like(total)
    through, through_sum = local, total
    distance = 1
    filled, fillers = [], list(fillers)
    while distance < lax.axis_size(axis):
        upper = through_sum.astype(BF16)
        lower = (through_sum - upper.astype(F32)).astype(BF16)
        packet = jnp.concatenate([through.astype(BF16), upper[None], lower[None]], axis=0)
        got = moved(packet, axis, distance * direction)
        if fillers:
            out = fillers.pop(0)(packet, filled)
            got, out = lax.optimization_barrier((got, out))
            filled.append(out)
        got = got.astype(F32)
        state, step_sum = got[:states], got[states] + got[states + 1]
        enter, enter_sum = enter + jnp.exp2(rate * enter_sum) * state, enter_sum + step_sum
        through, through_sum = through + jnp.exp2(rate * through_sum) * state, through_sum + step_sum
        distance *= 2
    for filler in fillers:
        filled.append(filler(enter, filled))
    return enter, filled


def silu_slope(pre_value):
    sigmoid_value = jax.nn.sigmoid(pre_value)
    return sigmoid_value * (1.0 + pre_value * (1.0 - sigmoid_value))


def shards(
    residual_in,
    norm_gain,
    in_weight,
    conv_weight,
    conv_bias,
    proj_weight,
    step_weight,
    step_bias,
    decay_log,
    skip_gain,
    out_weight,
    out_grad,
):
    seqs, toks, share = residual_in.shape
    model = norm_gain.shape[0]
    taps, inner = conv_weight.shape
    states = decay_log.shape[0]
    rank = step_weight.shape[0]
    rows = seqs * toks
    chunk = math.gcd(toks, 16)
    chunks = toks // chunk
    seq_count = lax.axis_size("seq")
    chan_bits = bits_of("chan")
    own_in = residual_in.swapaxes(0, 1).reshape(rows, share)
    own_out_grad = out_grad.swapaxes(0, 1).reshape(rows, share)
    full_in, (conv_weights, gate_weights) = gathered(own_in, "chan", (in_weight[:, 0], in_weight[:, 1]))
    wide_in = full_in.astype(F32)
    inv_rms = lax.rsqrt(jnp.mean(wide_in * wide_in, axis=-1, keepdims=True) + EPSILON)
    gain_full = norm_gain.astype(F32)
    normed = (wide_in * inv_rms * gain_full).astype(BF16)
    conv_in = dot(normed, conv_weights, out=BF16)
    halo = (taps - 1) * seqs
    lead = halo + -halo % 16
    normed_halo = moved(normed[rows - lead :], "seq", 1)
    previous = dot(normed_halo, conv_weights, out=BF16)
    padded = jnp.concatenate([previous[lead - halo :], conv_in], axis=0).astype(F32)
    conv_taps = conv_weight.astype(F32)
    conv_out = conv_bias.astype(F32) + sum(
        conv_taps[k] * padded[k * seqs : k * seqs + rows] for k in range(taps)
    )
    mixed = jax.nn.silu(conv_out).astype(BF16)
    proj_part = dot(proj_weight, mixed, CONTRACT_LAST)
    for bit in range(chan_bits):
        received = swapped(proj_part.astype(BF16) if bit else proj_part, "chan", bit)
        if bit == chan_bits - 1:
            extended_normed = jnp.concatenate([normed_halo, after(normed, proj_part)], axis=0)
            gate_pre = dot(after(normed, extended_normed), gate_weights)
            received, gate_pre = lax.optimization_barrier((received, gate_pre))
        proj_part = proj_part + received.astype(F32)
    projected = proj_part
    step_low = projected[:rank].astype(BF16)
    step_pre = dot(step_low, step_weight, CONTRACT_FIRST) + step_bias.astype(F32)
    step = jax.nn.softplus(step_pre)
    decay_rate = -jnp.exp(decay_log)
    rate = jnp.broadcast_to((decay_rate * LOG2E)[:, None], (states, seqs, inner))
    skip = jnp.broadcast_to(skip_gain, (seqs, inner))
    local_end, wide_rows, narrow_rows = local_ends(step, mixed, projected[rank:], rate, chunk)
    step_total = jnp.sum(step.reshape(toks, seqs, inner), axis=0)
    grad_whole, _ = gathered(after(own_out_grad, gate_pre), "chan", local_end)

    def output_side(sent, _):
        gated_grad = dot(after(grad_whole, sent), out_weight)
        return gated_grad, gated_grad * jax.nn.silu(gate_pre)

    def starts_side(sent, filled):
        return local_starts(step, after(filled[0][1], sent), wide_rows, rate, chunk)

    seq_bits = list(range(bits_of("seq")))
    other_bits = [1, 0] + seq_bits[2:] if len(seq_bits) > 1 else seq_bits
    def columns_side(sent, _):
        return columns_by(after(grad_whole, sent), "seq", 0), columns_by(after(normed, sent), "seq", other_bits[0])

    enter_h, filled = entering(local_end, step_total, rate, "seq", 1, [output_side, starts_side, columns_side])
    (gated_grad, y_grad), local_start, sides = filled[:3]
    shapes = [
        (rate.shape, F32),
        ((toks, inner // LANES, states * seqs, LANES), BF16),
        ((chunks, states, seqs, inner), BF16),
        ((rows, inner), BF16),
        ((rows, inner), BF16),
    ]
    arrays = (step, mixed, gate_pre, gated_grad, wide_rows, narrow_rows, rate)
    middle = chunks // 2

    def first_side(sent, _):
        return forward(arrays, skip, after(enter_h, sent), (), shapes, chunk, 0, middle)

    def second_side(sent, filled):
        state, *done = after(filled[1], sent)
        return forward(arrays, skip, state, done, shapes, chunk, middle, chunks)

    enter_g, filled = entering(
        local_start, step_total, rate, "seq", -1, [lambda sent, _: enter_h, first_side, second_side]
    )
    _, history, starts, gated_out, gate_grad = filled[2]
    by_part = lambda value: value.reshape(seq_count, -1, value.shape[-1])
    first_product = lambda columns, value: dot(columns, value, CONTRACT_FIRST, out=BF16)
    out_sent, gate_sent = (
        first_product(columns[1], value) for columns, value in zip(sides, (gated_out, gate_grad))
    )
    out_kept, gate_kept = (
        first_product(columns[0], after(value, out_sent, gate_sent)) for columns, value in zip(sides, (gated_out, gate_grad))
    )
    out_chain = Chain(None, "seq", seq_bits, halves=(out_kept, out_sent))
    gate_chain = Chain(None, "seq", other_bits, halves=(gate_kept, gate_sent))
    apart, joint = [[out_chain], [gate_chain]], [[out_chain, gate_chain]]
    (enter_g,) = send_chains(apart, [out_sent, gate_sent], enter_g)
    enter_g = after(enter_g, out_kept, gate_kept)
    chips = (2,) * (chan_bits - 1)

    def features(*pairs):
        sides = product_sides(own_bit("chan", 0), share, *pairs)
        return tuple(side.reshape(chips + side.shape[1:]) for side in sides)

    scan_sums, pre_grad, mixed_part, proj_sum = backward(
        step, mixed, y_grad, wide_rows, narrow_rows, rate, skip, step_weight, history, starts, enter_g, chunk
    )
    pre_grad, proj_sum = end_chains(apart, pre_grad, proj_sum)
    for bit in range(chan_bits):
        received = swapped(proj_sum.astype(BF16) if bit else proj_sum, "chan", bit)
        if bit == 0:
            (received,) = send_chains(apart, merge(apart), received)
        if bit == chan_bits - 1:
            branch_sum = Scattered(None, "chan", halves=features((after(gated_out, proj_sum), out_weight)))
            received, branch_sum.kept, branch_sum.sent = lax.optimization_barrier(
                (received, branch_sum.kept, branch_sum.sent)
            )
        proj_sum = proj_sum + received.astype(F32)
    proj_grad = proj_sum.astype(BF16)
    own_spread, first_grad, conv_sums = conv_back(
        proj_grad, proj_weight, mixed_part, conv_out, conv_in, previous, conv_taps, math.gcd(toks, 32)
    )
    incoming = moved(first_grad, "seq", -1)
    (own_spread,) = end_chains(apart, own_spread)
    half = inner // 2
    first_last, second_last = (
        by_part(dot(extended_normed, own_spread[:, at : at + half], CONTRACT_FIRST, out=BF16)) for at in (0, half)
    )
    first, second = Chain([first_last], "seq", seq_bits), Chain([second_last], "seq", other_bits)
    out_chain.got, first.sent, second.sent = lax.optimization_barrier((out_chain.got, first.sent, second.sent))
    weight_message = merge(apart)
    in_window = [[first], [second], [out_chain]]
    (own_spread,) = start_all([branch_sum], own_spread)
    own_spread, incoming = send_chains(in_window[:2], [first.sent, second.sent], own_spread, incoming)
    (own_spread,) = send_chains(in_window[2:], weight_message[:1], own_spread)
    zeros = jnp.zeros((halo, inner), F32)
    from_after = jnp.concatenate([zeros, incoming, zeros], axis=0)
    late = sum(
        conv_taps[k] * from_after[(2 * taps - 2 - k) * seqs - halo : (2 * taps - 2 - k) * seqs] for k in range(taps)
    )
    conv_in_grad = jnp.concatenate(
        [own_spread[lead : lead + rows - halo], (own_spread[lead + rows - halo :].astype(F32) + late).astype(BF16)], axis=0
    )
    late_proj, late_pre, late_sums = after((proj_grad, pre_grad, conv_sums), own_spread)
    proj_weight_part = dot(late_proj, mixed, out=BF16)
    step_weight_part = dot(step_low, late_pre, out=BF16)
    sums = jnp.concatenate([scan_sums, jnp.sum(late_sums, axis=1)], axis=0)
    sum_rows = sums.shape[0]
    sums = padded_rows(jnp.concatenate([sums[:, :half], sums[:, half:]], axis=0), 0, 16)
    small_blocks = jnp.concatenate([by_part(proj_weight_part), by_part(step_weight_part)], axis=1)
    small_blocks = padded_rows(jnp.concatenate([small_blocks[..., :half], small_blocks[..., half:]], axis=1), 1, 16)
    third = Chain([small_blocks], "seq", seq_bits, sums)
    row_dots = jnp.sum(
        conv_in_grad.astype(F32) * conv_in.astype(F32) + gate_grad.astype(F32) * gate_pre, axis=1
    )
    last_pair = (gate_grad, after(gate_weights, third.sent, row_dots))
    normed_sum = Scattered(None, "chan", halves=features((conv_in_grad, conv_weights), last_pair))
    normed_sum.sent, normed_sum.kept, third.sent = end_chains(
        in_window, normed_sum.sent, normed_sum.kept, third.sent
    )
    row_dots, third.sent = end_all([branch_sum], row_dots, third.sent)
    groups = [[first], [second]]
    messages = merge(groups)
    (row_dots,) = start_all([normed_sum, branch_sum], row_dots)
    in_window = [*groups, [third], [gate_chain]]
    (row_dots,) = send_chains(in_window, [*messages, third.sent, weight_message[1]], row_dots)
    row_dots = row_dots + swapped(row_dots, "chan", 0)
    (row_dots,) = end_all([normed_sum], row_dots)
    (row_dots,) = start_all([normed_sum], row_dots)
    (row_dots,) = end_all([branch_sum], row_dots)
    (row_dots,) = end_chains(in_window, row_dots)
    groups = [[first], [second], [third]]
    (row_dots,) = send_chains(groups, merge(groups), row_dots)
    for bit in range(1, chan_bits):
        row_dots = row_dots + swapped(row_dots, "chan", bit)
    (row_dots,) = end_all([normed_sum], row_dots)
    normed_grad = finished_on_the_way(normed_sum)
    row_dots = row_dots[:, None]
    wide_own = own_in.astype(F32)
    own_gain = lax.dynamic_slice_in_dim(gain_full, lax.axis_index("chan") * share, share, 0)
    in_rows = (
        own_out_grad.astype(F32)
        + inv_rms * own_gain * normed_grad
        - wide_own * (inv_rms * inv_rms / model) * row_dots
    ).astype(BF16)
    in_grad = in_rows.reshape(toks, seqs, share).swapaxes(0, 1)
    gain_grad = jnp.sum(normed_grad * wide_own * inv_rms, axis=0)
    in_grad, gain_grad = end_chains(groups, in_grad, gain_grad)
    if third.order:
        (gain_grad,) = send_chains([[third]], merge([[third]]), gain_grad)
    gain_grad = summed_near(gain_grad, "seq", bits_of("seq"))
    (first_last,), (second_last,), (small, sums) = last_of(first), last_of(second), last_of(third)
    (out_weight_grad,), (gate_weight_grad,) = last_of(out_chain), last_of(gate_chain)
    last = jnp.concatenate([first_last, second_last], axis=1)
    sums = jnp.concatenate([sums[:sum_rows], sums[sum_rows : 2 * sum_rows]], axis=1)
    proj_share, step_share = proj_weight.shape[0] // seq_count, rank // seq_count
    each = proj_share + step_share
    small_of = lambda start, count: jnp.concatenate([small[start : start + count], small[each + start : each + start + count]], axis=1)
    block_rows = (own_in.astype(F32) + finished_on_the_way(branch_sum)).astype(BF16)
    block_out = block_rows.reshape(toks, seqs, share).swapaxes(0, 1)
    return (
        block_out,
        in_grad,
        gain_grad,
        jnp.stack([last, gate_weight_grad], axis=1),
        sums[states + 2 : states + 2 + taps],
        sums[states + 2 + taps],
        small_of(0, proj_share),
        small_of(proj_share, step_share),
        sums[states],
        sums[:states],
        sums[states + 1],
        out_weight_grad,
    )


def solution(mesh):
    in_specs = (
        P(None, "seq", "chan"),
        P(),
        P(None, None, "chan"),
        P(None, "chan"),
        P("chan"),
        P(None, "chan"),
        P(None, "chan"),
        P("chan"),
        P(None, "chan"),
        P("chan"),
        P(None, "chan"),
        P(None, "seq", "chan"),
    )
    out_specs = (
        P(None, "seq", "chan"),
        P(None, "seq", "chan"),
        P("chan"),
        P("seq", None, "chan"),
        P(None, "chan"),
        P("chan"),
        P("seq", "chan"),
        P("seq", "chan"),
        P("chan"),
        P(None, "chan"),
        P("chan"),
        P("seq", "chan"),
    )
    return jax.shard_map(shards, mesh=mesh, in_specs=in_specs, out_specs=out_specs, check_vma=False)
```

```python
import functools, math
import jax, jax.numpy as jnp
from jax import lax
from jax.sharding import PartitionSpec as P
from jax.experimental import pallas as pl
from jax.experimental.pallas import tpu as pltpu

LANES = 128
LOG2E = 1.4426950408889634
VM = 56 * 1024 * 1024
F32, BF16 = jnp.float32, jnp.bfloat16


def spread(rows_ref, select_ref, spread_ref, narrow_ref, chunk, count, seqs):
    left, parts = rows_ref[...], []
    for _ in range(3):
        parts.append(left.astype(BF16))
        left = left - parts[-1].astype(F32)
    stacked = jnp.concatenate(parts, axis=0)
    for col in range(0, count, 2):
        wide = lax.dot_general(
            stacked, select_ref[:, col * LANES : (col + 2) * LANES], (((0,), (0,)), ((), ())), preferred_element_type=F32
        )
        for tok in range(chunk):
            both = [wide[tok * seqs : (tok + 1) * seqs, i * LANES : (i + 1) * LANES] for i in range(2)]
            for i in range(2):
                spread_ref[tok, col + i] = both[i]
            narrow_ref[tok, pl.ds(col * seqs, 2 * seqs), :] = jnp.concatenate(both, axis=0).astype(BF16)


def ends_kernel(chunk, step_ref, mixed_ref, rows_ref, rate_ref, h_ref, spread_ref, narrow_ref, select_ref):
    states, seqs, width = rate_ref.shape

    @pl.when(pl.program_id(0) == 0)
    def _():
        h_ref[...] = jnp.zeros_like(h_ref)
        row = lax.broadcasted_iota(jnp.int32, select_ref.shape, 0)
        col = lax.broadcasted_iota(jnp.int32, select_ref.shape, 1)
        select_ref[...] = (row % (2 * states) == col // LANES).astype(BF16)

    spread(rows_ref, select_ref, spread_ref, narrow_ref, chunk, 2 * states, seqs)

    def tile_step(j, _):
        lanes = pl.ds(pl.multiple_of(j * LANES, LANES), LANES)
        h = [h_ref[n, :, lanes] for n in range(states)]
        for tok in range(0, chunk, 2):
            m = mixed_ref[pl.ds(tok * seqs, 2 * seqs), lanes].astype(F32)
            for k in range(2):
                s = step_ref[pl.ds((tok + k) * seqs, seqs), lanes]
                x = s * m[k * seqs : (k + 1) * seqs]
                for n in range(states):
                    h[n] = jnp.exp2(s * rate_ref[n, :, lanes]) * h[n] + spread_ref[tok + k, n] * x
        for n in range(states):
            h_ref[n, :, lanes] = h[n]
        return 0

    lax.fori_loop(0, width // LANES, tile_step, 0, unroll=width // LANES)


def starts_kernel(chunk, step_ref, yg_ref, spread_ref, rate_ref, q_ref):
    states, seqs, width = rate_ref.shape

    @pl.when(pl.program_id(0) == 0)
    def _():
        q_ref[...] = jnp.zeros_like(q_ref)

    def tile_step(j, _):
        lanes = pl.ds(pl.multiple_of(j * LANES, LANES), LANES)
        q = [q_ref[n, :, lanes] for n in range(states)]
        for tok in reversed(range(chunk)):
            rows = pl.ds(tok * seqs, seqs)
            s, y = step_ref[rows, lanes], yg_ref[rows, lanes]
            for n in range(states):
                q[n] = jnp.exp2(s * rate_ref[n, :, lanes]) * (q[n] + spread_ref[tok, n] * y)
        for n in range(states):
            q_ref[n, :, lanes] = q[n]
        return 0

    lax.fori_loop(0, width // LANES, tile_step, 0, unroll=width // LANES)


def spread_spec(chunk, count, seqs, part, at):
    return pl.BlockSpec((chunk, count, seqs, LANES), lambda i: (at(i), part, 0, 0))


def narrow_spec(chunk, count, seqs, part, at):
    return pl.BlockSpec((chunk, count * seqs, LANES), lambda i: (at(i), part, 0))


def halves_sum(parts):
    while len(parts) > 1:
        parts = [a + b for a, b in zip(parts[::2], parts[1::2])]
    total = parts[0].astype(F32)
    seqs = total.shape[0] // 2
    return total[:seqs] + total[seqs:]


def local_ends(step, mixed, rows_t, rate, chunk):
    rows, width = step.shape
    states, seqs, _ = rate.shape
    elements = rows * width * states
    grid = rows // (chunk * seqs)
    row_spec = pl.BlockSpec((chunk * seqs, width), lambda i: (i, 0))
    whole = pl.BlockSpec((states, seqs, width), lambda i: (0, 0, 0))
    return pl.pallas_call(
        functools.partial(ends_kernel, chunk),
        grid=(grid,),
        in_specs=[row_spec, row_spec, pl.BlockSpec((2 * states, chunk * seqs), lambda i: (0, i)), whole],
        out_specs=[whole, spread_spec(chunk, 2 * states, seqs, 0, lambda i: i), narrow_spec(chunk, 2 * states, seqs, 0, lambda i: i)],
        out_shape=[jax.ShapeDtypeStruct(rate.shape, F32), jax.ShapeDtypeStruct((rows // seqs, 2 * states, seqs, LANES), F32),
                   jax.ShapeDtypeStruct((rows // seqs, 2 * states * seqs, LANES), BF16)],
        scratch_shapes=[pltpu.VMEM((6 * states, 2 * states * LANES), BF16)],
        compiler_params=pltpu.CompilerParams(vmem_limit_bytes=VM),
        cost_estimate=pl.CostEstimate(flops=elements, bytes_accessed=elements, transcendentals=0),
        name="local_ends",
    )(step, mixed, rows_t, rate)


def local_starts(step, yg, wide_rows, rate, chunk):
    rows, width = step.shape
    states, seqs, _ = rate.shape
    elements = rows * width * states
    grid = rows // (chunk * seqs)
    at = lambda i: grid - 1 - i
    row_spec = pl.BlockSpec((chunk * seqs, width), lambda i: (at(i), 0))
    whole = pl.BlockSpec((states, seqs, width), lambda i: (0, 0, 0))
    return pl.pallas_call(
        functools.partial(starts_kernel, chunk),
        grid=(grid,),
        in_specs=[row_spec, row_spec, spread_spec(chunk, states, seqs, 1, at), whole],
        out_specs=whole,
        out_shape=jax.ShapeDtypeStruct(rate.shape, F32),
        compiler_params=pltpu.CompilerParams(vmem_limit_bytes=VM),
        cost_estimate=pl.CostEstimate(flops=elements, bytes_accessed=elements, transcendentals=0),
        name="local_starts",
    )(step, yg, wide_rows, rate)


def fwd_kernel(chunk, step_ref, mixed_ref, gate_ref, gg_ref, spread_ref, narrow_ref, rate_ref, skip_ref,
               hin_ref, *refs):
    state_ref, hist_ref, start_ref, gated_ref, ggrad_ref = refs[-5:]
    states, seqs, width = rate_ref.shape

    @pl.when(pl.program_id(0) == 0)
    def _():
        state_ref[...] = hin_ref[...]

    start_ref[0] = state_ref[...].astype(BF16)

    def tile_step(j, _):
        lanes = pl.ds(pl.multiple_of(j * LANES, LANES), LANES)
        h = [state_ref[n, :, lanes] for n in range(states)]
        skip = skip_ref[:, lanes]
        for tok in range(0, chunk, 2):
            pair_rows = pl.ds(tok * seqs, 2 * seqs)
            pair = mixed_ref[pair_rows, lanes].astype(F32)
            gated, ggrad = [], []
            for k in range(2):
                rows = pl.ds((tok + k) * seqs, seqs)
                s = step_ref[rows, lanes]
                m = pair[k * seqs : (k + 1) * seqs]
                x = s * m
                terms = []
                for n in range(0, states, 2):
                    for i in (n, n + 1):
                        h[i] = jnp.exp2(s * rate_ref[i, :, lanes]) * h[i] + spread_ref[tok + k, i] * x
                    both = jnp.concatenate([h[n], h[n + 1]], axis=0).astype(BF16)
                    hist_ref[tok + k, j, pl.ds(n * seqs, 2 * seqs), :] = both
                    terms.append(both * narrow_ref[tok + k, pl.ds(n * seqs, 2 * seqs), :])
                y = skip * m + halves_sum(terms)
                v = gate_ref[rows, lanes]
                sig = 1.0 / (1.0 + jnp.exp2(v * (-LOG2E)))
                gated.append(y * (v * sig))
                ggrad.append(gg_ref[rows, lanes] * y * (sig * (1.0 + v * (1.0 - sig))))
            gated_ref[pair_rows, lanes] = jnp.concatenate(gated, axis=0).astype(BF16)
            ggrad_ref[pair_rows, lanes] = jnp.concatenate(ggrad, axis=0).astype(BF16)
        for n in range(states):
            state_ref[n, :, lanes] = h[n]
        return 0

    lax.fori_loop(0, width // LANES, tile_step, 0, unroll=width // LANES)


def forward(arrays, skip, carried, filled, shapes, chunk, first, last):
    step, mixed, gate, gg, wide_rows, narrow_rows, rate = arrays
    rows, width = step.shape
    states, seqs, _ = rate.shape
    at = lambda i: first + i
    row_spec = pl.BlockSpec((chunk * seqs, width), lambda i: (at(i), 0))
    whole = pl.BlockSpec((states, seqs, width), lambda i: (0, 0, 0))
    anywhere = pl.BlockSpec(memory_space=pl.ANY)
    elements = (last - first) * chunk * seqs * width * states
    return pl.pallas_call(
        functools.partial(fwd_kernel, chunk),
        grid=(last - first,),
        in_specs=[row_spec, row_spec, row_spec, row_spec, spread_spec(chunk, states, seqs, 0, at), narrow_spec(chunk, states, seqs, 1, at), whole,
                  pl.BlockSpec((seqs, width), lambda i: (0, 0)), whole] + [anywhere] * len(filled),
        out_specs=[whole, pl.BlockSpec((chunk, width // LANES, states * seqs, LANES), lambda i: (at(i), 0, 0, 0)),
                   pl.BlockSpec((1, states, seqs, width), lambda i: (at(i), 0, 0, 0)), row_spec, row_spec],
        out_shape=[jax.ShapeDtypeStruct(*shape) for shape in shapes],
        input_output_aliases={8 + i: i for i in range(len(filled) + 1)},
        compiler_params=pltpu.CompilerParams(vmem_limit_bytes=VM),
        cost_estimate=pl.CostEstimate(flops=elements, bytes_accessed=elements, transcendentals=0),
        name="scan_forward",
    )(step, mixed, gate, gg, wide_rows, narrow_rows, rate, skip, carried, *filled)


def bwd_kernel(chunk, step_ref, mixed_ref, yg_ref, spread_ref, narrow_ref, rate_ref, skip_ref, low_ref, hist_ref, start_ref, gin_ref,
               sums_ref, pre_ref, part_ref, proj_ref, decay_ref, bias_ref, skipg_ref, state_ref, b_ref, c_ref):
    states, seqs, width = rate_ref.shape
    span = states * seqs

    @pl.when(pl.program_id(0) == 0)
    def _():
        state_ref[...] = gin_ref[...]
        decay_ref[...] = jnp.zeros_like(decay_ref)
        bias_ref[...] = jnp.zeros_like(bias_ref)
        skipg_ref[...] = jnp.zeros_like(skipg_ref)

    b_ref[...] = jnp.zeros_like(b_ref)
    c_ref[...] = jnp.zeros_like(c_ref)
    contract = (((1,), (1,)), ((), ()))

    def tile_step(j, _):
        lanes = pl.ds(pl.multiple_of(j * LANES, LANES), LANES)
        q = [state_ref[n, :, lanes] for n in range(states)]
        acc = [decay_ref[n, :, lanes] for n in range(states)]
        skip = skip_ref[:, lanes]
        bias = bias_ref[:, lanes]
        skipg = skipg_ref[:, lanes]
        for tok in range(chunk - 2, -1, -2):
            pair_rows = pl.ds(tok * seqs, 2 * seqs)
            pair = mixed_ref[pair_rows, lanes].astype(F32)
            pre, xs, packed, weights = [None, None], [None, None], [None, None], [None, None]
            for k in (1, 0):
                now = tok + k
                rows = pl.ds(now * seqs, seqs)
                s = step_ref[rows, lanes]
                y = yg_ref[rows, lanes]
                m = pair[k * seqs : (k + 1) * seqs]
                gs, along_terms, size_terms = [], [], []
                for n in range(0, states, 2):
                    if now > 0:
                        before = hist_ref[now - 1, j, pl.ds(n * seqs, 2 * seqs), :]
                    else:
                        before = jnp.concatenate([start_ref[0, n + i, :, lanes] for i in range(2)], axis=0)
                    both, moves = [], []
                    for i in (n, n + 1):
                        z = s * rate_ref[i, :, lanes]
                        g = spread_ref[now, i] * y + q[i]
                        q[i] = jnp.exp2(z) * g
                        both.append(g)
                        moves.append(q[i] * z)
                    gs.append(jnp.concatenate(both, axis=0).astype(BF16))
                    along_terms.append(gs[-1] * narrow_ref[now, pl.ds(n * seqs, 2 * seqs), :])
                    size_terms.append(jnp.concatenate(moves, axis=0).astype(BF16) * before)
                packed[k] = jnp.concatenate(gs, axis=0)
                weights[k] = size_terms
                along, size = halves_sum(along_terms), halves_sum(size_terms)
                part_ref[rows, lanes] = s * along + skip * y
                skipg = skipg + y * m
                xs[k] = s * m
                series = 1.0 - s * (1.0 / 2) * (1.0 - s * (1.0 / 3) * (1.0 - s * (1.0 / 4) * (1.0 - s * (1.0 / 5))))
                ratio = jnp.where(s < 0.1, series, (1.0 - jnp.exp2(s * (-LOG2E))) / jnp.maximum(s, 0.1))
                pre[k] = ratio * (size * (1.0 / LOG2E) + xs[k] * along)
            for n in range(0, states, 2):
                total = (weights[0][n // 2] + weights[1][n // 2]).astype(F32)
                acc[n] = acc[n] + total[:seqs]
                acc[n + 1] = acc[n + 1] + total[seqs:]
            rounded = jnp.concatenate(pre, axis=0).astype(BF16)
            pre_ref[pair_rows, lanes] = rounded
            wide = rounded.astype(F32)
            bias = bias + wide[:seqs] + wide[seqs:]
            x = jnp.concatenate(xs, axis=0).astype(BF16)
            pair_hist = jnp.concatenate([hist_ref[tok, j], hist_ref[tok + 1, j]], axis=0)
            b_ref[tok // 2] += lax.dot_general(x, jnp.concatenate(packed, axis=0), contract, preferred_element_type=F32)
            c_ref[tok // 2] += lax.dot_general(
                yg_ref[pair_rows, lanes].astype(BF16), pair_hist, contract, preferred_element_type=F32
            )
        for n in range(states):
            state_ref[n, :, lanes] = q[n]
            decay_ref[n, :, lanes] = acc[n]
        bias_ref[:, lanes] = bias
        skipg_ref[:, lanes] = skipg
        return 0

    lax.fori_loop(0, width // LANES, tile_step, 0, unroll=width // LANES)
    wide = 2 * span
    row = lax.broadcasted_iota(jnp.int32, (2 * seqs, wide), 0)
    col = lax.broadcasted_iota(jnp.int32, (2 * seqs, wide), 1)
    match = (row // seqs == col // span) & (row % seqs == col % seqs)
    b_rows = [jnp.where(match, b_ref[i], 0.0) for i in range(chunk // 2)]
    c_rows = [jnp.where(match, c_ref[i], 0.0) for i in range(chunk // 2)]
    src = lax.broadcasted_iota(jnp.int32, (2 * states, wide), 1) // seqs % states
    dst = lax.broadcasted_iota(jnp.int32, (2 * states, wide), 0)
    fold_b = (src == dst).astype(BF16)
    fold_c = (src + states == dst).astype(BF16)
    rank = low_ref.shape[0]
    proj_ref[:rank] = lax.dot_general(low_ref[...], pre_ref[...], contract, preferred_element_type=F32)
    proj_ref[rank:] = lax.dot_general(
        fold_b, jnp.concatenate(b_rows, axis=0).astype(BF16), contract, preferred_element_type=F32
    ) + lax.dot_general(fold_c, jnp.concatenate(c_rows, axis=0).astype(BF16), contract, preferred_element_type=F32)

    @pl.when(pl.program_id(0) == pl.num_programs(0) - 1)
    def _():
        sums_ref[:states] = jnp.sum(decay_ref[...], axis=1) * (1.0 / LOG2E)
        sums_ref[states : states + 1] = jnp.sum(bias_ref[...], axis=0, keepdims=True)
        sums_ref[states + 1 : states + 2] = jnp.sum(skipg_ref[...], axis=0, keepdims=True)


def backward(step, mixed, yg, wide_rows, narrow_rows, rate, skip, low_weight, hist, start, gin, chunk):
    rows, width = step.shape
    states, seqs, _ = rate.shape
    grid = rows // (chunk * seqs)
    elements = rows * width * states
    at = lambda i: grid - 1 - i
    row_spec = pl.BlockSpec((chunk * seqs, width), lambda i: (at(i), 0))
    rank = low_weight.shape[0]
    whole = pl.BlockSpec((states, seqs, width), lambda i: (0, 0, 0))
    one = pl.BlockSpec((seqs, width), lambda i: (0, 0))
    return pl.pallas_call(
        functools.partial(bwd_kernel, chunk),
        grid=(grid,),
        in_specs=[row_spec, row_spec, row_spec, spread_spec(chunk, states, seqs, 1, at),
                  narrow_spec(chunk, states, seqs, 0, at), whole, one,
                  pl.BlockSpec((rank, width), lambda i: (0, 0)),
                  pl.BlockSpec((chunk, width // LANES, states * seqs, LANES), lambda i: (at(i), 0, 0, 0)),
                  pl.BlockSpec((1, states, seqs, width), lambda i: (at(i), 0, 0, 0)), whole],
        out_specs=[pl.BlockSpec((states + 2, width), lambda i: (0, 0)), row_spec, row_spec,
                   pl.BlockSpec((rank + 2 * states, chunk * seqs), lambda i: (0, at(i)))],
        out_shape=[jax.ShapeDtypeStruct((states + 2, width), F32), jax.ShapeDtypeStruct((rows, width), BF16),
                   jax.ShapeDtypeStruct((rows, width), F32), jax.ShapeDtypeStruct((rank + 2 * states, rows), F32)],
        scratch_shapes=[pltpu.VMEM(rate.shape, F32), pltpu.VMEM((seqs, width), F32), pltpu.VMEM((seqs, width), F32),
                        pltpu.VMEM(rate.shape, F32)] + [pltpu.VMEM((chunk // 2, 2 * seqs, 2 * states * seqs), F32)] * 2,
        compiler_params=pltpu.CompilerParams(vmem_limit_bytes=VM),
        cost_estimate=pl.CostEstimate(flops=elements, bytes_accessed=elements, transcendentals=0),
        name="scan_backward",
    )(step, mixed, yg, wide_rows, narrow_rows, rate, skip, low_weight, hist, start, gin)


def conv_kernel(chunk, taps, proj_ref, weight_ref, part_ref, conv_ref, in_ref, before_ref, taps_ref,
                spread_ref, first_ref, sums_ref, grad_ref, back_ref):
    rows, width = part_ref.shape
    seqs = rows // chunk
    halo = (taps - 1) * seqs
    lead = before_ref.shape[0]
    step = pl.program_id(0)
    block = pl.num_programs(0) - 1 - step

    @pl.when(step == 0)
    def _():
        grad_ref[rows:] = jnp.zeros_like(grad_ref[rows:])
        sums_ref[...] = jnp.zeros_like(sums_ref)

    @pl.when(step > 0)
    def _():
        grad_ref[rows : rows + halo] = grad_ref[:halo]

    back_ref[...] = lax.dot_general(
        proj_ref[...], weight_ref[...], (((0,), (0,)), ((), ())), preferred_element_type=F32
    )

    def tile_step(j, _):
        lanes = pl.ds(pl.multiple_of(j * LANES, LANES), LANES)
        tap = [taps_ref[k : k + 1, lanes] for k in range(taps)]
        sums = [sums_ref[k, :, lanes] for k in range(taps + 1)]
        for tok in reversed(range(0, chunk, 2)):
            at = pl.ds(tok * seqs, 2 * seqs)
            v = conv_ref[at, lanes]
            sig = 1.0 / (1.0 + jnp.exp2(v * (-LOG2E)))
            grad = (part_ref[at, lanes] + back_ref[at, lanes]) * (sig * (1.0 + v * (1.0 - sig)))
            grad_ref[at, lanes] = grad
            given = in_ref[at, lanes].astype(F32)
            spread = jnp.zeros_like(grad)
            for k in range(taps):
                later = grad_ref[pl.ds((tok + taps - 1 - k) * seqs, 2 * seqs), lanes]
                spread = spread + tap[k] * later
                use = given * later
                sums[k] = sums[k] + use[:seqs] + use[seqs:]
            sums[taps] = sums[taps] + grad[:seqs] + grad[seqs:]
            out_at = pl.multiple_of(lead + block * rows + tok * seqs, 2 * seqs)
            spread_ref[pl.ds(out_at, 2 * seqs), lanes] = spread.astype(BF16)
        for k in range(taps + 1):
            sums_ref[k, :, lanes] = sums[k]
        return 0

    lax.fori_loop(0, width // LANES, tile_step, 0, unroll=width // LANES)

    @pl.when(block == 0)
    def _():
        first_ref[...] = grad_ref[:halo]
        given = before_ref[...].astype(F32)
        parts = [jnp.zeros((lead - halo, width), F32)]
        for tok in range(taps - 1):
            spread = jnp.zeros((seqs, width), F32)
            own = given[lead - halo + tok * seqs : lead - halo + (tok + 1) * seqs]
            for k in range(tok + 1):
                later = grad_ref[(tok - k) * seqs : (tok - k + 1) * seqs]
                spread = spread + taps_ref[k : k + 1] * later
                sums_ref[k] = sums_ref[k] + own * later
            parts.append(spread)
        spread_ref[:lead] = jnp.concatenate(parts, axis=0).astype(BF16)


def conv_back(proj_grad, weight, part, conv_out, conv_in, before, conv_taps, chunk):
    rows, width = part.shape
    taps = conv_taps.shape[0]
    columns = proj_grad.shape[0]
    seqs, lead = 8, before.shape[0]
    halo = (taps - 1) * seqs
    grid = rows // (chunk * seqs)
    at = lambda i: grid - 1 - i
    row_spec = pl.BlockSpec((chunk * seqs, width), lambda i: (at(i), 0))
    fixed = lambda *shape: pl.BlockSpec(shape, lambda i: (0,) * len(shape))
    return pl.pallas_call(
        functools.partial(conv_kernel, chunk, taps),
        grid=(grid,),
        in_specs=[pl.BlockSpec((columns, chunk * seqs), lambda i: (0, at(i))), fixed(columns, width), row_spec, row_spec, row_spec,
                  fixed(lead, width), fixed(taps, width)],
        out_specs=[fixed(rows + lead, width), fixed(halo, width), fixed(taps + 1, seqs, width)],
        out_shape=[jax.ShapeDtypeStruct((rows + lead, width), BF16), jax.ShapeDtypeStruct((halo, width), F32),
                   jax.ShapeDtypeStruct((taps + 1, seqs, width), F32)],
        scratch_shapes=[pltpu.VMEM((chunk * seqs + lead, width), F32), pltpu.VMEM((chunk * seqs, width), F32)],
        compiler_params=pltpu.CompilerParams(vmem_limit_bytes=VM),
        cost_estimate=pl.CostEstimate(flops=rows * width, bytes_accessed=rows * width, transcendentals=0),
        name="conv_backward",
    )(proj_grad, weight, part, conv_out, conv_in, before, conv_taps)


def merge_kernel(plan, messages, bits_ref, *refs):
    refs = list(refs)
    inputs = [[refs.pop(0) for _ in range(len(sizes) + 1 + (extra > 0))] for _, _, sizes, extra, *_ in plan]
    outputs = [[refs.pop(0) for _ in range(len(sizes) + (extra > 0))] for _, _, sizes, extra, *_ in plan]
    sent = [refs.pop(0) for _ in range(messages)]
    for index, (levels, dim, sizes, extra, got_at, message, sent_at) in enumerate(plan):
        bit = bits_ref[index]
        kept, got, whole = inputs[index][: len(sizes)], inputs[index][len(sizes)], inputs[index][-1]
        kept_out, whole_out, sent_out = outputs[index][: len(sizes)], outputs[index][-1], sent[message]
        after_dim = 1 << (levels - 1 - dim)
        for size, source, target in zip(sizes, kept, kept_out):
            for rest in range(1 << (levels - 1)):
                high, low = divmod(rest, after_dim)
                for side in range(2):
                    own = bit if side == 0 else 1 - bit
                    at = pl.multiple_of(((high * 2 + own) * after_dim + low) * size, 16)
                    total = source[pl.ds(at, size), :].astype(F32) + got[pl.ds(got_at + at, size), :].astype(F32)
                    if side == 0:
                        target[rest * size : (rest + 1) * size, :] = total.astype(BF16)
                    else:
                        sent_out[sent_at + rest * size : sent_at + (rest + 1) * size, :] = total.astype(BF16)
            got_at += size << levels
            sent_at += size << (levels - 1)
        if extra:
            other = got[got_at : got_at + extra, :].astype(F32) + got[got_at + extra : got_at + 2 * extra, :].astype(F32)
            total = whole[...] + other
            upper = total.astype(BF16)
            lower = (total - upper.astype(F32)).astype(BF16)
            sent_out[sent_at : sent_at + extra, :] = upper
            sent_out[sent_at + extra : sent_at + 2 * extra, :] = lower
            whole_out[...] = upper.astype(F32) + lower.astype(F32)


def product_kernel(count, core_ref, *refs):
    del core_ref
    kept_ref, sent_ref = refs[-2:]
    total = None
    for a_ref, b_ref in zip(refs[:count], refs[count : 2 * count]):
        part = lax.dot_general(a_ref[...], b_ref[...], (((1,), (1,)), ((), ())), preferred_element_type=F32)
        total = part if total is None else total + part
    side = pl.program_id(1)

    @pl.when(side == 0)
    def _():
        kept_ref[0] = total.astype(BF16)

    @pl.when(side == 1)
    def _():
        sent_ref[0] = total.astype(BF16)


def product_sides(core, share, *pairs):
    rows, columns = pairs[0][0].shape[0], pairs[0][1].shape[0]
    chips = columns // share // 2
    mine = lambda far, side, core_ref: (far * 2 + jnp.where(side == 0, core_ref[0], 1 - core_ref[0]), 0)
    out_spec = pl.BlockSpec((1, rows, share), lambda far, side, core_ref: (far, 0, 0))
    return pl.pallas_call(
        functools.partial(product_kernel, len(pairs)),
        grid_spec=pltpu.PrefetchScalarGridSpec(
            num_scalar_prefetch=1,
            grid=(chips, 2),
            in_specs=[pl.BlockSpec(a.shape, lambda far, side, core_ref: (0, 0)) for a, _ in pairs]
            + [pl.BlockSpec((share, b.shape[1]), mine) for _, b in pairs],
            out_specs=[out_spec, out_spec],
        ),
        out_shape=[jax.ShapeDtypeStruct((chips, rows, share), BF16)] * 2,
        compiler_params=pltpu.CompilerParams(vmem_limit_bytes=VM),
        cost_estimate=pl.CostEstimate(flops=1024, bytes_accessed=1024, transcendentals=0),
        name="product_sides",
    )(core.reshape(1).astype(jnp.int32), *[a for a, _ in pairs], *[b for _, b in pairs])


EPSILON = 1e-05
CONTRACT_LAST = (((1,), (1,)), ((), ()))
CONTRACT_FIRST = (((0,), (0,)), ((), ()))


def dot(a, b, dims=(((1,), (0,)), ((), ())), out=F32):
    return lax.dot_general(a, b, dims, preferred_element_type=out)


def after(value, *done):
    return lax.optimization_barrier((value, done))[0]


def swapped(value, axis, bit):
    count = lax.axis_size(axis)
    return lax.ppermute(value, axis, [(i, i ^ (1 << bit)) for i in range(count)])


def moved(value, axis, distance):
    count = lax.axis_size(axis)
    return lax.ppermute(value, axis, [(i, i + distance) for i in range(count) if 0 <= i + distance < count])


def bits_of(axis):
    return lax.axis_size(axis).bit_length() - 1


def own_bit(axis, bit):
    return (lax.axis_index(axis) >> bit) & 1


def gathered(value, axis, meanwhile=()):
    count = lax.axis_size(axis)
    parts = {0: value}
    for bit in reversed(range(bits_of(axis))):
        fresh = {mask | (1 << bit): swapped(part, axis, bit) for mask, part in parts.items()}
        if len(parts) == 1:
            fresh, meanwhile = lax.optimization_barrier((fresh, meanwhile))
        parts |= fresh
    for bit in range(bits_of(axis)):
        high = own_bit(axis, bit) == 1
        parts = {m: jnp.where(high, parts[m ^ (1 << bit)], parts[m]) for m in range(count)}
    return jnp.concatenate([parts[m] for m in range(count)], axis=-1), meanwhile


def summed(value, axis, narrow_from):
    for bit in range(bits_of(axis)):
        sent = value.astype(BF16) if bit >= narrow_from else value
        value = value + swapped(sent, axis, bit).astype(F32)
    return value


def summed_near(value, axis, narrow_from):
    if bits_of(axis) > 1 and narrow_from > 1:
        count = lax.axis_size(axis)
        near = [lax.ppermute(value, axis, [(i, i ^ mask) for i in range(count)]) for mask in (1, 2, 3)]
        value = (value + near[0]) + (near[1] + near[2])
        for bit in range(2, bits_of(axis)):
            value = value + swapped(value, axis, bit)
        return value
    return summed(value, axis, narrow_from)


def pick(value, dim, index):
    return lax.dynamic_index_in_dim(value, index, dim, keepdims=False)


class Scattered:
    def __init__(self, blocks, axis, order=None, halves=None):
        bits = bits_of(axis)
        self.axis, self.left, self.order = axis, list(range(bits)), list(order or range(bits))
        self.got, self.kept, self.sent = None, None, None
        if halves:
            self.kept, self.sent = halves
        else:
            self.value = blocks.reshape((2,) * bits + blocks.shape[1:])

    def split(self):
        if self.sent is not None:
            return
        bit = self.order[0]
        dim = len(self.left) - 1 - self.left.index(bit)
        mine = own_bit(self.axis, bit)
        self.kept, self.sent = pick(self.value, dim, mine), pick(self.value, dim, 1 - mine)

    def send(self):
        self.got = swapped(self.sent, self.axis, self.order[0])

    def add(self):
        bit = self.order.pop(0)
        self.left.remove(bit)
        value = self.kept.astype(F32) + self.got.astype(F32)
        self.value = value.astype(BF16) if self.left else value
        self.got, self.kept, self.sent = None, None, None


def start_all(sums, *values):
    sums = [s for s in sums if s.order]
    for s in sums:
        s.split()
    sent, values = lax.optimization_barrier(([s.sent for s in sums], values))
    for s, message in zip(sums, sent):
        s.sent = message
        s.send()
    return values


def end_all(sums, *values):
    sums = [s for s in sums if s.got is not None]
    got, values = lax.optimization_barrier(([s.got for s in sums], values))
    for s, message in zip(sums, got):
        s.got = message
        s.add()
    return values


def padded_rows(value, dim, multiple):
    width = -value.shape[dim] % multiple
    return jnp.pad(value, [(0, width if i == dim else 0) for i in range(value.ndim)])


def two_parts(value):
    upper = value.astype(BF16)
    return upper, (value - upper.astype(F32)).astype(BF16)


class Chain:
    def __init__(self, pieces, axis, order, whole=None, halves=None):
        bits = bits_of(axis)
        self.axis, self.order, self.left, self.whole, self.at = axis, list(order), list(range(bits)), [], 0
        if halves:
            self.sizes = [halves[1].shape[0] >> (bits - 1)]
            self.kept, self.sent = [halves[0]], halves[1]
            return
        self.sizes = [piece.shape[1] for piece in pieces]
        dim = bits - 1 - self.order[0]
        mine = own_bit(axis, self.order[0])
        halves = [piece.reshape((2,) * bits + piece.shape[1:]) for piece in pieces]
        flat = lambda value: value.reshape(-1, value.shape[-1])
        self.kept = [flat(pick(value, dim, mine)) for value in halves]
        message = [flat(pick(value, dim, 1 - mine)) for value in halves]
        if whole is not None:
            upper, lower = two_parts(whole)
            self.whole = [upper.astype(F32) + lower.astype(F32)]
            message += [upper, lower]
        self.sent = jnp.concatenate(message, axis=0) if len(message) > 1 else message[0]

    def finish(self):
        rows, values = self.at, []
        for size, kept in zip(self.sizes, self.kept):
            values.append(kept.astype(F32) + self.got[rows : rows + size].astype(F32))
            rows += size
        if self.whole:
            count = self.whole[0].shape[0]
            upper, lower = (self.got[rows + i * count : rows + (i + 1) * count].astype(F32) for i in range(2))
            values.append(self.whole[0] + (upper + lower))
        return values


def send_chains(groups, messages, *values):
    messages, values = lax.optimization_barrier((messages, values))
    for group, message in zip(groups, messages):
        got = swapped(message, group[0].axis, group[0].order[0])
        for c in group:
            c.got = got
            c.left.remove(c.order.pop(0))
    return values


def end_chains(groups, *values):
    got, values = lax.optimization_barrier(([group[0].got for group in groups], values))
    for group, message in zip(groups, got):
        for c in group:
            c.got = message
    return values


def last_of(chain):
    while chain.order:
        send_chains([[chain]], merge([[chain]]))
    return chain.finish()


def merge(groups):
    plan, operands, outputs, messages = [], [], [], []
    for number, group in enumerate(groups):
        rows = 0
        for c in group:
            levels, extra = len(c.left), c.whole[0].shape[0] if c.whole else 0
            columns = c.got.shape[1]
            plan.append((levels, levels - 1 - c.left.index(c.order[0]), tuple(c.sizes), extra, c.at, number, rows))
            operands += [*c.kept, c.got, *c.whole]
            outputs += [((size << (levels - 1), columns), BF16) for size in c.sizes] + [((extra, columns), F32)] * (extra > 0)
            c.at = rows
            rows += sum(size << (levels - 1) for size in c.sizes) + 2 * extra
        messages.append(((rows, columns), BF16))
    chains = [c for group in groups for c in group]
    bits = jnp.stack([own_bit(c.axis, c.order[0]) for c in chains]).astype(jnp.int32)
    outs = list(
        pl.pallas_call(
            functools.partial(merge_kernel, plan, len(messages)),
            in_specs=[pl.BlockSpec(memory_space=pltpu.SMEM)] + [pl.BlockSpec(memory_space=pltpu.VMEM)] * len(operands),
            out_specs=[pl.BlockSpec(memory_space=pltpu.VMEM)] * (len(outputs) + len(messages)),
            out_shape=[jax.ShapeDtypeStruct(*shape) for shape in outputs + messages],
            compiler_params=pltpu.CompilerParams(vmem_limit_bytes=VM),
            cost_estimate=pl.CostEstimate(flops=1024, bytes_accessed=1024, transcendentals=0),
            name="merge_messages",
        )(bits, *operands)
    )
    for c in chains:
        c.kept = [outs.pop(0) for _ in c.sizes]
        c.whole = [outs.pop(0) for _ in c.whole]
    return outs


def columns_by(value, axis, bit):
    count = lax.axis_size(axis)
    width = value.shape[1] // (count >> bit)
    parts = [value[:, i * width : (i + 1) * width] for i in range(count >> bit)]
    high = own_bit(axis, bit) == 1
    low, up = parts[0::2], parts[1::2]
    return [
        jnp.concatenate([jnp.where(high, b, a) for a, b in zip(one, two)], axis=1) for one, two in ((low, up), (up, low))
    ]


def finished_on_the_way(s):
    if s.got is not None:
        s.add()
    while s.order:
        s.split()
        s.send()
        s.add()
    return s.value


def entering(local, total, rate, axis, direction, fillers):
    states = rate.shape[0]
    enter, enter_sum = jnp.zeros_like(local), jnp.zeros_like(total)
    through, through_sum = local, total
    distance = 1
    filled, fillers = [], list(fillers)
    while distance < lax.axis_size(axis):
        upper = through_sum.astype(BF16)
        lower = (through_sum - upper.astype(F32)).astype(BF16)
        packet = jnp.concatenate([through.astype(BF16), upper[None], lower[None]], axis=0)
        got = moved(packet, axis, distance * direction)
        if fillers:
            out = fillers.pop(0)(packet, filled)
            got, out = lax.optimization_barrier((got, out))
            filled.append(out)
        got = got.astype(F32)
        state, step_sum = got[:states], got[states] + got[states + 1]
        enter, enter_sum = enter + jnp.exp2(rate * enter_sum) * state, enter_sum + step_sum
        through, through_sum = through + jnp.exp2(rate * through_sum) * state, through_sum + step_sum
        distance *= 2
    for filler in fillers:
        filled.append(filler(enter, filled))
    return enter, filled


def silu_slope(pre_value):
    sigmoid_value = jax.nn.sigmoid(pre_value)
    return sigmoid_value * (1.0 + pre_value * (1.0 - sigmoid_value))


def shards(
    residual_in,
    norm_gain,
    in_weight,
    conv_weight,
    conv_bias,
    proj_weight,
    step_weight,
    step_bias,
    decay_log,
    skip_gain,
    out_weight,
    out_grad,
):
    seqs, toks, share = residual_in.shape
    model = norm_gain.shape[0]
    taps, inner = conv_weight.shape
    states = decay_log.shape[0]
    rank = step_weight.shape[0]
    rows = seqs * toks
    chunk = math.gcd(toks, 16)
    chunks = toks // chunk
    seq_count = lax.axis_size("seq")
    chan_bits = bits_of("chan")
    own_in = residual_in.swapaxes(0, 1).reshape(rows, share)
    own_out_grad = out_grad.swapaxes(0, 1).reshape(rows, share)
    full_in, (conv_weights, gate_weights) = gathered(own_in, "chan", (in_weight[:, 0], in_weight[:, 1]))
    wide_in = full_in.astype(F32)
    inv_rms = lax.rsqrt(jnp.mean(wide_in * wide_in, axis=-1, keepdims=True) + EPSILON)
    gain_full = norm_gain.astype(F32)
    normed = (wide_in * inv_rms * gain_full).astype(BF16)
    conv_in = dot(normed, conv_weights, out=BF16)
    halo = (taps - 1) * seqs
    lead = halo + -halo % 16
    normed_halo = moved(normed[rows - lead :], "seq", 1)
    previous = dot(normed_halo, conv_weights, out=BF16)
    padded = jnp.concatenate([previous[lead - halo :], conv_in], axis=0).astype(F32)
    conv_taps = conv_weight.astype(F32)
    conv_out = conv_bias.astype(F32) + sum(
        conv_taps[k] * padded[k * seqs : k * seqs + rows] for k in range(taps)
    )
    mixed = jax.nn.silu(conv_out).astype(BF16)
    proj_part = dot(proj_weight, mixed, CONTRACT_LAST)
    for bit in range(chan_bits):
        received = swapped(proj_part.astype(BF16) if bit else proj_part, "chan", bit)
        if bit == chan_bits - 1:
            extended_normed = jnp.concatenate([normed_halo, after(normed, proj_part)], axis=0)
            gate_pre = dot(after(normed, extended_normed), gate_weights)
            received, gate_pre = lax.optimization_barrier((received, gate_pre))
        proj_part = proj_part + received.astype(F32)
    projected = proj_part
    step_low = projected[:rank].astype(BF16)
    step_pre = dot(step_low, step_weight, CONTRACT_FIRST) + step_bias.astype(F32)
    step = jax.nn.softplus(step_pre)
    decay_rate = -jnp.exp(decay_log)
    rate = jnp.broadcast_to((decay_rate * LOG2E)[:, None], (states, seqs, inner))
    skip = jnp.broadcast_to(skip_gain, (seqs, inner))
    local_end, wide_rows, narrow_rows = local_ends(step, mixed, projected[rank:], rate, chunk)
    step_total = jnp.sum(step.reshape(toks, seqs, inner), axis=0)
    grad_whole, _ = gathered(after(own_out_grad, gate_pre), "chan", local_end)

    def output_side(sent, _):
        gated_grad = dot(after(grad_whole, sent), out_weight)
        return gated_grad, gated_grad * jax.nn.silu(gate_pre)

    def starts_side(sent, filled):
        return local_starts(step, after(filled[0][1], sent), wide_rows, rate, chunk)

    seq_bits = list(range(bits_of("seq")))
    other_bits = [1, 0] + seq_bits[2:] if len(seq_bits) > 1 else seq_bits
    def columns_side(sent, _):
        return columns_by(after(grad_whole, sent), "seq", 0), columns_by(after(normed, sent), "seq", other_bits[0])

    enter_h, filled = entering(local_end, step_total, rate, "seq", 1, [output_side, starts_side, columns_side])
    (gated_grad, y_grad), local_start, sides = filled[:3]
    shapes = [
        (rate.shape, F32),
        ((toks, inner // LANES, states * seqs, LANES), BF16),
        ((chunks, states, seqs, inner), BF16),
        ((rows, inner), BF16),
        ((rows, inner), BF16),
    ]
    arrays = (step, mixed, gate_pre, gated_grad, wide_rows, narrow_rows, rate)
    middle = chunks // 2

    def first_side(sent, _):
        return forward(arrays, skip, after(enter_h, sent), (), shapes, chunk, 0, middle)

    def second_side(sent, filled):
        state, *done = after(filled[1], sent)
        return forward(arrays, skip, state, done, shapes, chunk, middle, chunks)

    enter_g, filled = entering(
        local_start, step_total, rate, "seq", -1, [lambda sent, _: enter_h, first_side, second_side]
    )
    _, history, starts, gated_out, gate_grad = filled[2]
    by_part = lambda value: value.reshape(seq_count, -1, value.shape[-1])
    first_product = lambda columns, value: dot(columns, value, CONTRACT_FIRST, out=BF16)
    out_sent, gate_sent = (
        first_product(columns[1], value) for columns, value in zip(sides, (gated_out, gate_grad))
    )
    out_kept, gate_kept = (
        first_product(columns[0], after(value, out_sent, gate_sent)) for columns, value in zip(sides, (gated_out, gate_grad))
    )
    out_chain = Chain(None, "seq", seq_bits, halves=(out_kept, out_sent))
    gate_chain = Chain(None, "seq", other_bits, halves=(gate_kept, gate_sent))
    apart, joint = [[out_chain], [gate_chain]], [[out_chain, gate_chain]]
    (enter_g,) = send_chains(apart, [out_sent, gate_sent], enter_g)
    enter_g = after(enter_g, out_kept, gate_kept)
    chips = (2,) * (chan_bits - 1)

    def features(*pairs):
        sides = product_sides(own_bit("chan", 0), share, *pairs)
        return tuple(side.reshape(chips + side.shape[1:]) for side in sides)

    scan_sums, pre_grad, mixed_part, proj_sum = backward(
        step, mixed, y_grad, wide_rows, narrow_rows, rate, skip, step_weight, history, starts, enter_g, chunk
    )
    pre_grad, proj_sum = end_chains(apart, pre_grad, proj_sum)
    for bit in range(chan_bits):
        received = swapped(proj_sum.astype(BF16) if bit else proj_sum, "chan", bit)
        if bit == 0:
            (received,) = send_chains(apart, merge(apart), received)
        if bit == chan_bits - 1:
            branch_sum = Scattered(None, "chan", halves=features((after(gated_out, proj_sum), out_weight)))
            received, branch_sum.kept, branch_sum.sent = lax.optimization_barrier(
                (received, branch_sum.kept, branch_sum.sent)
            )
        proj_sum = proj_sum + received.astype(F32)
    proj_grad = proj_sum.astype(BF16)
    own_spread, first_grad, conv_sums = conv_back(
        proj_grad, proj_weight, mixed_part, conv_out, conv_in, previous, conv_taps, math.gcd(toks, 32)
    )
    incoming = moved(first_grad, "seq", -1)
    (own_spread,) = end_chains(apart, own_spread)
    half = inner // 2
    first_last, second_last = (
        by_part(dot(extended_normed, own_spread[:, at : at + half], CONTRACT_FIRST, out=BF16)) for at in (0, half)
    )
    first, second = Chain([first_last], "seq", seq_bits), Chain([second_last], "seq", other_bits)
    out_chain.got, first.sent, second.sent = lax.optimization_barrier((out_chain.got, first.sent, second.sent))
    weight_message = merge(apart)
    in_window = [[first], [second], [out_chain]]
    (own_spread,) = start_all([branch_sum], own_spread)
    own_spread, incoming = send_chains(in_window[:2], [first.sent, second.sent], own_spread, incoming)
    (own_spread,) = send_chains(in_window[2:], weight_message[:1], own_spread)
    zeros = jnp.zeros((halo, inner), F32)
    from_after = jnp.concatenate([zeros, incoming, zeros], axis=0)
    late = sum(
        conv_taps[k] * from_after[(2 * taps - 2 - k) * seqs - halo : (2 * taps - 2 - k) * seqs] for k in range(taps)
    )
    conv_in_grad = jnp.concatenate(
        [own_spread[lead : lead + rows - halo], (own_spread[lead + rows - halo :].astype(F32) + late).astype(BF16)], axis=0
    )
    late_proj, late_pre, late_sums = after((proj_grad, pre_grad, conv_sums), own_spread)
    proj_weight_part = dot(late_proj, mixed, out=BF16)
    step_weight_part = dot(step_low, late_pre, out=BF16)
    sums = jnp.concatenate([scan_sums, jnp.sum(late_sums, axis=1)], axis=0)
    sum_rows = sums.shape[0]
    sums = padded_rows(jnp.concatenate([sums[:, :half], sums[:, half:]], axis=0), 0, 16)
    small_blocks = jnp.concatenate([by_part(proj_weight_part), by_part(step_weight_part)], axis=1)
    small_blocks = padded_rows(jnp.concatenate([small_blocks[..., :half], small_blocks[..., half:]], axis=1), 1, 16)
    third = Chain([small_blocks], "seq", seq_bits, sums)
    row_dots = jnp.sum(
        conv_in_grad.astype(F32) * conv_in.astype(F32) + gate_grad.astype(F32) * gate_pre, axis=1
    )
    last_pair = (gate_grad, after(gate_weights, third.sent, row_dots))
    normed_sum = Scattered(None, "chan", halves=features((conv_in_grad, conv_weights), last_pair))
    normed_sum.sent, normed_sum.kept, third.sent = end_chains(
        in_window, normed_sum.sent, normed_sum.kept, third.sent
    )
    row_dots, third.sent = end_all([branch_sum], row_dots, third.sent)
    groups = [[first], [second]]
    messages = merge(groups)
    (row_dots,) = start_all([normed_sum, branch_sum], row_dots)
    in_window = [*groups, [third], [gate_chain]]
    (row_dots,) = send_chains(in_window, [*messages, third.sent, weight_message[1]], row_dots)
    row_dots = row_dots + swapped(row_dots, "chan", 0)
    (row_dots,) = end_all([normed_sum], row_dots)
    (row_dots,) = start_all([normed_sum], row_dots)
    (row_dots,) = end_all([branch_sum], row_dots)
    (row_dots,) = end_chains(in_window, row_dots)
    groups = [[first], [second], [third]]
    (row_dots,) = send_chains(groups, merge(groups), row_dots)
    for bit in range(1, chan_bits):
        row_dots = row_dots + swapped(row_dots, "chan", bit)
    (row_dots,) = end_all([normed_sum], row_dots)
    normed_grad = finished_on_the_way(normed_sum)
    row_dots = row_dots[:, None]
    wide_own = own_in.astype(F32)
    own_gain = lax.dynamic_slice_in_dim(gain_full, lax.axis_index("chan") * share, share, 0)
    in_rows = (
        own_out_grad.astype(F32)
        + inv_rms * own_gain * normed_grad
        - wide_own * (inv_rms * inv_rms / model) * row_dots
    ).astype(BF16)
    in_grad = in_rows.reshape(toks, seqs, share).swapaxes(0, 1)
    gain_grad = jnp.sum(normed_grad * wide_own * inv_rms, axis=0)
    in_grad, gain_grad = end_chains(groups, in_grad, gain_grad)
    if third.order:
        (gain_grad,) = send_chains([[third]], merge([[third]]), gain_grad)
    gain_grad = summed_near(gain_grad, "seq", bits_of("seq"))
    (first_last,), (second_last,), (small, sums) = last_of(first), last_of(second), last_of(third)
    (out_weight_grad,), (gate_weight_grad,) = last_of(out_chain), last_of(gate_chain)
    last = jnp.concatenate([first_last, second_last], axis=1)
    sums = jnp.concatenate([sums[:sum_rows], sums[sum_rows : 2 * sum_rows]], axis=1)
    proj_share, step_share = proj_weight.shape[0] // seq_count, rank // seq_count
    each = proj_share + step_share
    small_of = lambda start, count: jnp.concatenate([small[start : start + count], small[each + start : each + start + count]], axis=1)
    block_rows = (own_in.astype(F32) + finished_on_the_way(branch_sum)).astype(BF16)
    block_out = block_rows.reshape(toks, seqs, share).swapaxes(0, 1)
    return (
        block_out,
        in_grad,
        gain_grad,
        jnp.stack([last, gate_weight_grad], axis=1),
        sums[states + 2 : states + 2 + taps],
        sums[states + 2 + taps],
        small_of(0, proj_share),
        small_of(proj_share, step_share),
        sums[states],
        sums[:states],
        sums[states + 1],
        out_weight_grad,
    )


def solution(mesh):
    in_specs = (
        P(None, "seq", "chan"),
        P(),
        P(None, None, "chan"),
        P(None, "chan"),
        P("chan"),
        P(None, "chan"),
        P(None, "chan"),
        P("chan"),
        P(None, "chan"),
        P("chan"),
        P(None, "chan"),
        P(None, "seq", "chan"),
    )
    out_specs = (
        P(None, "seq", "chan"),
        P(None, "seq", "chan"),
        P("chan"),
        P("seq", None, "chan"),
        P(None, "chan"),
        P("chan"),
        P("seq", "chan"),
        P("seq", "chan"),
        P("chan"),
        P(None, "chan"),
        P("chan"),
        P("seq", "chan"),
    )
    return jax.shard_map(shards, mesh=mesh, in_specs=in_specs, out_specs=out_specs, check_vma=False)
```
